256 devices in a mesh: wall: 32 (over y, z), span: 2 (over x_hi), stream: 4 (over x_lo, core).
Axes of the slice: x: 4 (x_hi: 2, x_lo: 2; x = x_hi * 2 + x_lo), y: 4, z: 8, core: 2. Of those that a mesh axis runs over, the one named last changes fastest.
Arguments:
- right_side: float32 [1024, 128, 512], P('wall', 'span', 'stream'), may hold values from -6 to 6
- viscosity: float32 [1024, 128, 512], P('wall', 'span', 'stream'), may hold values from 0.05 to 1
- wall_metric: float32 [1024], P('wall'), may hold values from 0.5 to 4
- line_inverse: bfloat16 [1024, 1024], replicated
Outputs:
- solution: float32 [1024, 128, 512], P('wall', 'span', 'stream')
- residual: float32 [1024, 128, 512], P('wall', 'span', 'stream')
The draws below stay inside these ranges and needn't reach their ends.
All inputs are finite; a program needn't handle non-finite values.
Results may differ from the reference program's by a relative error of at most 0.0057.
Values may be sent and summed in bfloat16 or wider, within the bound.
No kernel may reach another device: no remote copies, remote signals or barrier semaphores. Data moves between devices by JAX's collectives and lax.ppermute only.
A program may use at most 128 MiB of HBM per device.

```python
import math
import jax
import jax.numpy as jnp

NW = 1024
STEPS = 3
NS = 128
NX = 512


def draw_line_inverse(key, part):
    key = jax.random.fold_in(key, 7)
    reach_key = jax.random.fold_in(key, 11)
    noise_key = jax.random.fold_in(key, 13)
    rows = jnp.arange(NW)[:, None]
    cols = jnp.arange(NW)[None, :]
    distance = jnp.abs(rows - cols).astype(jnp.float32)
    reach = NW * jnp.exp2(-jax.random.uniform(reach_key, (), jnp.float32))
    noise = jax.random.normal(noise_key, (NW, NW), jnp.float32)
    kernel = 2.0 * jnp.exp(-distance / reach) * (1.0 + 0.8 * noise) / NW
    diagonal = jnp.where(rows == cols, 1.0, 0.0).astype(jnp.float32)
    return (kernel + diagonal).astype(jnp.bfloat16)


def level_of(key, shape, cuts, least, top_value):
    def one(dim, parts):
        draws = jax.random.uniform(jax.random.fold_in(jax.random.fold_in(key, 6), dim), (parts,), jnp.float32, least / len(cuts), top_value / len(cuts))
        return jnp.repeat(jnp.exp(draws), shape[dim] // parts).reshape((-1,) + (1,) * (len(shape) - dim - 1))

    loudness = one(*cuts[0])
    for cut in cuts[1:]:
        loudness = loudness * one(*cut)
    return loudness


def gaussian(rng, dims, deviation, most, shards=(), held_as=jnp.bfloat16):
    values = deviation * jax.random.normal(rng, dims, jnp.float32)
    if shards:
        values = values * level_of(rng, dims, shards, -0.22, 0.18)
    return jnp.clip(values, -most, most).astype(held_as)


def setup_inputs(seed: int = 0) -> dict:
    key_list = jax.random.split(jax.random.key(seed), 5)
    return {
        "right_side": gaussian(key_list[0], (NW, NS, NX), 1.0, 6.0, ((0, 32), (1, 2), (2, 4)), jnp.float32),
        "viscosity": jnp.clip(jnp.exp(math.log(1.0) - 2.9957323 * jax.random.uniform(key_list[1], (NW, NS, NX), jnp.float32) ** level_of(key_list[1], (NW, NS, NX), ((0, 32), (1, 2), (2, 4)), -0.2, 0.2)), 0.05, 1.0),
        "wall_metric": jnp.clip(jnp.exp(math.log(4.0) - 2.0794415 * jax.random.uniform(key_list[2], (NW,), jnp.float32) ** level_of(key_list[2], (NW,), ((0, 32),), -0.2, 0.2)), 0.5, 4.0),
        "line_inverse": draw_line_inverse(jax.random.fold_in(key_list[4], 71), 0),
    }


def chebyshev_weights(steps):
    lowest = 0.25
    highest = 2.5
    center = 0.5 * (highest + lowest)
    half = 0.5 * (highest - lowest)
    ratio = center / half
    weights = [(0.0, 1.0 / center)]
    rho_old = 1.0 / ratio
    for step in range(1, steps):
        rho_new = 1.0 / (2.0 * ratio - rho_old)
        weights.append((rho_new * rho_old, 2.0 * rho_new / half))
        rho_old = rho_new
    return weights


def operate(field, kappa, viscosity):
    zero_pad = ((1, 1), (0, 0), (0, 0))
    kappa_pad = jnp.pad(kappa, zero_pad)
    field_pad = jnp.pad(field, zero_pad)
    result = field + 0.5 * (kappa + kappa_pad[:-2]) * (field - field_pad[:-2])
    result = result + 0.5 * (kappa + kappa_pad[2:]) * (field - field_pad[2:])
    for axis_dim in (1, 2):
        for offset in (1, -1):
            near_visc = jnp.roll(viscosity, offset, axis=axis_dim)
            near_field = jnp.roll(field, offset, axis=axis_dim)
            result = result + 0.5 * (viscosity + near_visc) * (field - near_field)
    return result


def line_apply(line_inverse, resid):
    rounded = resid.astype(jnp.bfloat16)
    flat = jnp.dot(line_inverse, rounded.reshape(rounded.shape[0], -1), preferred_element_type=jnp.float32)
    return flat.reshape(resid.shape)


def reference(right_side, viscosity, wall_metric, line_inverse):
    kappa = viscosity * wall_metric[:, None, None]
    solution = jnp.zeros_like(right_side)
    direction = jnp.zeros_like(right_side)
    resid = right_side
    for step, pair in enumerate(chebyshev_weights(STEPS)):
        if step > 0:
            resid = right_side - operate(solution, kappa, viscosity)
        correction = line_apply(line_inverse, resid)
        direction = pair[0] * direction + pair[1] * correction
        solution = solution + direction
    residual = right_side - operate(solution, kappa, viscosity)
    return solution, residual
```

```python
import functools

import jax
import jax.numpy as jnp
from jax import lax
from jax.experimental import pallas as pl
from jax.experimental.pallas import tpu as pltpu
from jax.sharding import PartitionSpec as P

STEPS = 3
NW, WY, WZ = 1024, 4, 8
ROWS, SPAN, LANES = 32, 64, 128
BS, BX = 16, 16
CELLS = BS * BX
TAIL = 8
MID = 0.5
F32, BF16 = jnp.float32, jnp.bfloat16
VMEM = pl.BlockSpec(memory_space=pltpu.VMEM)
PARAMS = pltpu.CompilerParams(vmem_limit_bytes=40 * 1024 * 1024)


def chebyshev_weights(steps):
    lowest = 0.25
    highest = 2.5
    center = 0.5 * (highest + lowest)
    half = 0.5 * (highest - lowest)
    ratio = center / half
    weights = [(0.0, 1.0 / center)]
    rho_old = 1.0 / ratio
    for step in range(1, steps):
        rho_new = 1.0 / (2.0 * ratio - rho_old)
        weights.append((rho_new * rho_old, 2.0 * rho_new / half))
        rho_old = rho_new
    return weights


WEIGHTS = chebyshev_weights(STEPS)


def shape(dims, dtype):
    return jax.ShapeDtypeStruct(dims, dtype)


def call(kernel, outs, scratch=(), **cost):
    return pl.pallas_call(
        kernel,
        out_shape=outs,
        scratch_shapes=list(scratch),
        compiler_params=PARAMS,
        cost_estimate=pl.CostEstimate(
            flops=cost.get("flops", 10**7), bytes_accessed=cost.get("size", 4 * 10**6), transcendentals=0
        ),
    )


def lane_blocks(rows):
    block = lax.broadcasted_iota(jnp.int32, rows[0].shape, 1) // BX
    rows = list(rows)
    for bit in range(3):
        step = 1 << bit
        upper = (block // step) % 2 == 1
        for i in range(8):
            if i & step:
                continue
            a, b = rows[i], rows[i + step]
            rows[i] = jnp.where(upper, pltpu.roll(b, BX * step, 1), a)
            rows[i + step] = jnp.where(upper, b, pltpu.roll(a, LANES - BX * step, 1))
    return rows


def strided(s):
    return pl.ds(s, ROWS, stride=SPAN)


def pack(b_ref, v_ref, m_ref, send, ew0, ew1, es, exl, exr):
    m = m_ref[...]
    rest = m
    parts = []
    for _ in range(3):
        part = rest.astype(BF16)
        rest = rest - part.astype(F32)
        parts.append(part.astype(F32))
    tail = jnp.concatenate(parts + [jnp.zeros((TAIL - 3, ROWS), F32)], axis=0)
    tail = jnp.concatenate([tail, jnp.zeros((TAIL, LANES - ROWS), F32)], axis=1).astype(BF16)
    for k in range(WY * WZ):
        send[k, 4 * ROWS :, :] = tail
    for t in range(WY):
        for g in range(2):
            for ref, off, mid in ((b_ref, 0, 0.0), (v_ref, 2, MID)):
                parts = lane_blocks([ref[strided(16 * t + 8 * g + i), :] - mid for i in range(8)])
                rows = slice(ROWS * (off + g), ROWS * (off + g + 1))
                for z in range(WZ):
                    send[WZ * t + z, rows, :] = parts[z].astype(BF16)
                if off:
                    exl[2 * t + g] = parts[0].astype(BF16)
                    exr[2 * t + g] = parts[7].astype(BF16)
    ew0[...] = v_ref[0:SPAN, :] * m[:, :1]
    ew1[...] = v_ref[(ROWS - 1) * SPAN :, :] * m[:, ROWS - 1 :]
    es[0] = (v_ref[strided(0), :] - MID).astype(BF16)
    es[1] = (v_ref[strided(SPAN - 1), :] - MID).astype(BF16)


def to_lines(recv, bt, vt, metric, *edges):
    for i in range(8):
        row = jnp.zeros((TAIL, LANES), F32)
        for j in range(4):
            row += pltpu.roll(recv[4 * i + j, 4 * ROWS :, :].astype(F32), ROWS * j, 1)
        metric[:, i * LANES : (i + 1) * LANES] = jnp.sum(row, axis=0, keepdims=True)
    for j in range(4):
        for i in range(8):
            tile = recv[4 * i : 4 * i + 4, ROWS * j : ROWS * (j + 1), :].astype(F32).reshape(LANES, LANES).T
            out = bt if j < 2 else vt
            out[(j % 2) * LANES : (j % 2 + 1) * LANES, i * LANES : (i + 1) * LANES] = tile.astype(BF16)
    for k, ref in enumerate((bt, vt)):
        grid = ref[...].astype(F32).reshape(BS, BX, NW)
        rows = slice(BX * k, BX * (k + 1))
        edges[0][rows] = grid[0].astype(BF16)
        edges[1][rows] = grid[BS - 1].astype(BF16)
        edges[2][rows] = grid[:, 0, :].astype(BF16)
        edges[3][rows] = grid[:, BX - 1, :].astype(BF16)


def apply_lines(rows, line):
    return lax.dot_general(rows, line, (((1,), (1,)), ((), ())), preferred_element_type=F32)


def first_lines(bt, line, x1):
    x1[...] = WEIGHTS[0][1] * apply_lines(bt[...], line[...])


def fill(ext, middle, su, sd, xl, xr):
    ext[1 : BS + 1, 8 : 8 + BX, :] = middle
    ext[0, 8 : 8 + BX, :] = su
    ext[BS + 1, 8 : 8 + BX, :] = sd
    for s in range(BS):
        ext[s + 1, 7:8, :] = xl[s : s + 1]
        ext[s + 1, 8 + BX : 9 + BX, :] = xr[s : s + 1]


def line_resid(s, bt, xe, ve, metric, out):
    lane = lax.broadcasted_iota(jnp.int32, (BX, LANES), 1)
    count = NW // LANES

    def load(ref, j):
        lanes = slice(j * LANES, (j + 1) * LANES)
        return ref[s + 1, 8 : 8 + BX, lanes]

    xs = [load(xe, j) for j in range(count)]
    ks = [load(ve, j) * metric[:, j * LANES : (j + 1) * LANES] for j in range(count)]
    zero = jnp.zeros((BX, LANES), F32)
    xroll = [pltpu.roll(v, LANES - 1, 1) for v in xs] + [zero]
    kroll = [pltpu.roll(v, LANES - 1, 1) for v in ks] + [zero]
    last = lane == LANES - 1
    first = lane == 0
    carry = None
    for j in range(count):
        lanes = slice(j * LANES, (j + 1) * LANES)
        xc, kc = xs[j], ks[j]
        xn = jnp.where(last, xroll[j + 1], xroll[j])
        kn = jnp.where(last, kroll[j + 1], kroll[j])
        above = (kc + kn) * (xc - xn)
        moved = pltpu.roll(above, 1, 1)
        entry = kc * xc if j == 0 else carry
        total = above - jnp.where(first, entry if j else -entry, moved)
        carry = moved
        vc = ve[s + 1, 8 : 8 + BX, lanes]
        for si, x0 in ((s, 8), (s + 2, 8), (s + 1, 7), (s + 1, 9)):
            total += (vc + ve[si, x0 : x0 + BX, lanes]) * (xc - xe[si, x0 : x0 + BX, lanes])
        resid = bt[pl.ds(pl.multiple_of(s * BX, BX), BX), lanes].astype(F32) - (xc + 0.5 * total)
        out[pl.ds(pl.multiple_of(s * BX, BX), BX), lanes] = resid.astype(BF16)


def second_step(
    x1, bt, vt, su, sd, xl, xr, line, metric, x2, d2, e0, e1, e2, e3, xe, ve, rt, ends
):
    for k, ref in enumerate((su, sd, xl, xr)):
        ends[k * BX : (k + 1) * BX] = ref[0:BX]
    ends1 = WEIGHTS[0][1] * apply_lines(ends[...], line[...])
    fill(xe, x1[...].reshape(BS, BX, NW), *(ends1[k * BX : (k + 1) * BX] for k in range(4)))
    fill(
        ve,
        vt[...].astype(F32).reshape(BS, BX, NW) + MID,
        *(ref[BX : 2 * BX].astype(F32) + MID for ref in (su, sd, xl, xr)),
    )

    def one(s, _):
        line_resid(s, bt, xe, ve, metric, rt)
        return 0

    lax.fori_loop(0, BS, one, 0)
    keep, scale = WEIGHTS[1]
    d2[...] = keep * x1[...] + scale * apply_lines(rt[...], line[...])
    x2[...] = x1[...] + d2[...]
    grid = x2[...].reshape(BS, BX, NW)
    e0[...] = grid[0]
    e1[...] = grid[BS - 1]
    e2[...] = grid[:, 0, :]
    e3[...] = grid[:, BX - 1, :]


def third_step(x2, d2, bt, vt, su, sd, xl, xr, vsu, vsd, vxl, vxr, line, metric, send, xe, ve, rt, x3):
    fill(xe, x2[...].reshape(BS, BX, NW), su[...], sd[...], xl[...], xr[...])
    fill(
        ve,
        vt[...].astype(F32).reshape(BS, BX, NW) + MID,
        *(ref[BX : 2 * BX].astype(F32) + MID for ref in (vsu, vsd, vxl, vxr)),
    )

    def one(s, _):
        line_resid(s, bt, xe, ve, metric, rt)
        return 0

    lax.fori_loop(0, BS, one, 0)
    keep, scale = WEIGHTS[2]
    x3[...] = x2[...] + keep * d2[...] + scale * apply_lines(rt[...], line[...])
    for j in range(2):
        for i in range(8):
            tile = x3[j * LANES : (j + 1) * LANES, i * LANES : (i + 1) * LANES].T
            send[i * LANES : (i + 1) * LANES, j * LANES : (j + 1) * LANES] = tile.astype(BF16)


def unpack(recv, x3, xs, ew0, ew1, es, exl, exr):
    for t in range(WY):
        for g in range(2):
            lanes = slice(LANES * g, LANES * (g + 1))
            parts = [recv[WZ * t + z, :, lanes] for z in range(WZ)]
            exl[2 * t + g] = parts[0]
            exr[2 * t + g] = parts[7]
            parts = lane_blocks([p.astype(F32) for p in parts])
            for i in range(8):
                s = 16 * t + 8 * g + i
                x3[strided(s), :] = parts[i]
                xs[s] = parts[i]
    ew0[...] = x3[0:SPAN, :]
    ew1[...] = x3[(ROWS - 1) * SPAN :, :]
    es[0] = xs[0].astype(BF16)
    es[1] = xs[SPAN - 1].astype(BF16)


def last_resid(
    xs, v_ref, b_ref, m_ref, xdn, xup, xsp, xlf, xrt, kdn, kup, vsp, vlf, vrt, out, xe, ve
):
    xe[1 : SPAN + 1] = xs[...]
    xe[0] = xsp[1].astype(F32)
    xe[SPAN + 1] = xsp[0].astype(F32)
    for s in range(SPAN):
        ve[s + 1] = v_ref[strided(s), :]
    ve[0] = vsp[1].astype(F32) + MID
    ve[SPAN + 1] = vsp[0].astype(F32) + MID
    row = lax.broadcasted_iota(jnp.int32, (ROWS, LANES), 0)
    lane = lax.broadcasted_iota(jnp.int32, (ROWS, LANES), 1)
    square = lax.broadcasted_iota(jnp.int32, (ROWS, ROWS), 0)
    square = square == lax.broadcasted_iota(jnp.int32, (ROWS, ROWS), 1)
    m = jnp.sum(jnp.where(square, m_ref[...], 0.0), axis=1, keepdims=True)

    def eight(q, _):
        rows = pl.ds(pl.multiple_of(8 * q, 8), 8)
        beyond = [ref[rows, :] for ref in (xdn, xup, kdn, kup)]
        for i in range(8):
            s = 8 * q + i
            xc, vc = xe[s + 1], ve[s + 1]
            total = (vc + ve[s]) * (xc - xe[s]) + (vc + ve[s + 2]) * (xc - xe[s + 2])
            xb, xa, kb, ka = (block[i : i + 1] for block in beyond)
            xn = jnp.where(row == 0, xb, pltpu.roll(xc, 1, 0))
            kc = m * vc
            kn = jnp.where(row == 0, kb, pltpu.roll(kc, 1, 0))
            total += (kc + kn) * (xc - xn)
            xn = jnp.where(row == ROWS - 1, xa, pltpu.roll(xc, ROWS - 1, 0))
            kn = jnp.where(row == ROWS - 1, ka, pltpu.roll(kc, ROWS - 1, 0))
            total += (kc + kn) * (xc - xn)
            left = (LANES - (BX * i + BX - 1)) % LANES
            xn = jnp.where(lane == 0, pltpu.roll(xlf[q].astype(F32), left, 1), pltpu.roll(xc, 1, 1))
            vn = jnp.where(
                lane == 0, pltpu.roll(vlf[q].astype(F32) + MID, left, 1), pltpu.roll(vc, 1, 1)
            )
            total += (vc + vn) * (xc - xn)
            right = LANES - 1 - BX * i
            xn = jnp.where(
                lane == LANES - 1,
                pltpu.roll(xrt[q].astype(F32), right, 1),
                pltpu.roll(xc, LANES - 1, 1),
            )
            vn = jnp.where(
                lane == LANES - 1,
                pltpu.roll(vrt[q].astype(F32) + MID, right, 1),
                pltpu.roll(vc, LANES - 1, 1),
            )
            total += (vc + vn) * (xc - xn)
            out[strided(s), :] = b_ref[strided(s), :] - (xc + 0.5 * total)
        return 0

    lax.fori_loop(0, SPAN // 8, eight, 0)


def block_edges(ew0, ew1, es, exl, exr):
    walls = lax.axis_size("wall")
    streams = lax.axis_size("stream")
    rising = [(i, i + 1) for i in range(walls - 1)]
    falling = [(i + 1, i) for i in range(walls - 1)]
    right = [(i, (i + 1) % streams) for i in range(streams)]
    left = [((i + 1) % streams, i) for i in range(streams)]
    return (
        lax.ppermute(ew1, "wall", rising),
        lax.ppermute(ew0, "wall", falling),
        lax.ppermute(es, "span", [(0, 1), (1, 0)]),
        lax.ppermute(exr, "stream", right),
        lax.ppermute(exl, "stream", left),
    )


def line_shift(value, ds, dx):
    spans, streams = lax.axis_size("span"), lax.axis_size("stream")
    pairs = []
    for y in range(WY):
        for z in range(WZ):
            for sp in range(spans):
                for st in range(streams):
                    sb = (sp * WY + y + ds) % (spans * WY)
                    xb = (st * WZ + z + dx) % (streams * WZ)
                    here = ((y * WZ + z) * spans + sp) * streams + st
                    there = ((sb % WY) * WZ + xb % WZ) * spans + sb // WY
                    pairs.append((here, there * streams + xb // WZ))
    return lax.ppermute(value, ("wall", "span", "stream"), pairs)


def line_edges(*edges):
    return (
        line_shift(edges[1], 1, 0),
        line_shift(edges[0], -1, 0),
        line_shift(edges[3], 0, 1),
        line_shift(edges[2], 0, -1),
    )


def body(right_side, viscosity, wall_metric, line_inverse):
    b = right_side.reshape(ROWS * SPAN, LANES)
    v = viscosity.reshape(ROWS * SPAN, LANES)
    m = wall_metric.reshape(1, ROWS)
    chunk = shape((2 * WY, ROWS, LANES), BF16)
    wide = shape((SPAN, LANES), F32)
    deep = shape((2, ROWS, LANES), BF16)
    block_outs = (wide, wide, deep, chunk, chunk)
    send, *edges = call(pack, (shape((WY * WZ, 4 * ROWS + TAIL, LANES), BF16), *block_outs))(b, v, m)
    v_edges = block_edges(*edges)
    recv = lax.all_to_all(send, "wall", 0, 0, tiled=True)
    lines = shape((CELLS, NW), BF16)
    bt, vt, metric, *edges = call(
        to_lines, (lines, lines, shape((1, NW), F32)) + (shape((2 * BX, NW), BF16),) * 4
    )(recv)
    near = line_edges(*edges)
    x1 = call(first_lines, shape((CELLS, NW), F32))(bt, line_inverse)
    ext = pltpu.VMEM((BS + 2, 2 * BX, NW), F32)
    field = shape((CELLS, NW), F32)
    rounded = pltpu.VMEM((CELLS, NW), BF16)
    x2, d2, *edges = call(
        second_step,
        (field, field) + (shape((BX, NW), F32),) * 4,
        (ext, ext, rounded, pltpu.VMEM((4 * BX, NW), BF16)),
    )(x1, bt, vt, *near, line_inverse, metric)
    x_near = line_edges(*edges)
    send = call(
        third_step,
        shape((NW, CELLS), BF16),
        (ext, ext, rounded, pltpu.VMEM((CELLS, NW), F32)),
    )(x2, d2, bt, vt, *x_near, *near, line_inverse, metric)
    recv = lax.all_to_all(send.reshape(WY * WZ, ROWS, CELLS), "wall", 0, 0, tiled=True)
    x3, xs, *edges = call(
        unpack,
        (shape((ROWS * SPAN, LANES), F32), shape((SPAN, ROWS, LANES), F32), *block_outs),
    )(recv)
    x_edges = block_edges(*edges)
    tall = pltpu.VMEM((SPAN + 2, ROWS, LANES), F32)
    residual = call(last_resid, shape((ROWS * SPAN, LANES), F32), (tall, tall))(
        xs, v, b, m, *x_edges, *v_edges
    )
    dims = right_side.shape
    return x3.reshape(dims), residual.reshape(dims)


def solution(mesh):
    in_specs = (P("wall", "span", "stream"), P("wall", "span", "stream"), P("wall"), P())
    out_specs = (P("wall", "span", "stream"), P("wall", "span", "stream"))
    return jax.shard_map(body, mesh=mesh, in_specs=in_specs, out_specs=out_specs, check_vma=False)
```

```python
import functools

import jax
import jax.numpy as jnp
from jax import lax
from jax.experimental import pallas as pl
from jax.experimental.pallas import tpu as pltpu
from jax.sharding import PartitionSpec as P

STEPS = 3
NW, WY, WZ = 1024, 4, 8
ROWS, SPAN, LANES = 32, 64, 128
BS, BX = 16, 16
CELLS = BS * BX
TAIL = 8
MID = 0.5
F32, BF16 = jnp.float32, jnp.bfloat16
PARAMS = pltpu.CompilerParams(vmem_limit_bytes=40 * 1024 * 1024)


def chebyshev_weights(steps):
    lowest = 0.25
    highest = 2.5
    center = 0.5 * (highest + lowest)
    half = 0.5 * (highest - lowest)
    ratio = center / half
    weights = [(0.0, 1.0 / center)]
    rho_old = 1.0 / ratio
    for step in range(1, steps):
        rho_new = 1.0 / (2.0 * ratio - rho_old)
        weights.append((rho_new * rho_old, 2.0 * rho_new / half))
        rho_old = rho_new
    return weights


WEIGHTS = chebyshev_weights(STEPS)


def shape(dims, dtype):
    return jax.ShapeDtypeStruct(dims, dtype)


def call(kernel, outs, scratch=(), **specs):
    return pl.pallas_call(
        kernel,
        out_shape=outs,
        scratch_shapes=list(scratch),
        compiler_params=PARAMS,
        cost_estimate=pl.CostEstimate(flops=10**7, bytes_accessed=4 * 10**6, transcendentals=0),
        **specs,
    )


def lane_blocks(rows):
    block = lax.broadcasted_iota(jnp.int32, rows[0].shape, 1) // BX
    rows = list(rows)
    for bit in range(3):
        step = 1 << bit
        upper = (block // step) % 2 == 1
        for i in range(8):
            if i & step:
                continue
            a, b = rows[i], rows[i + step]
            rows[i] = jnp.where(upper, pltpu.roll(b, BX * step, 1), a)
            rows[i + step] = jnp.where(upper, b, pltpu.roll(a, LANES - BX * step, 1))
    return rows


def strided(s):
    return pl.ds(s, ROWS, stride=SPAN)


def edge_lanes(sides, offset):
    at = lax.broadcasted_iota(jnp.int32, (8 * LANES, LANES), 0)
    to = lax.broadcasted_iota(jnp.int32, (8 * LANES, LANES), 1)
    out = []
    for lanes, pick in sides:
        chosen = (at % BX == pick) & (to == at // BX + offset)
        one = jnp.where(chosen, 1.0, 0.0).astype(BF16)
        out.append(jnp.dot(lanes, one, preferred_element_type=F32).astype(BF16))
    return out


def pack(b_hbm, v_hbm, m_ref, send, es, dl, dr, b_buf, v_buf, cl, cr, sems):
    copies = []
    for t in range(WY):
        cells = (slice(None), slice(BS * t, BS * (t + 1)), slice(None))
        for k, (src, dst) in enumerate(((b_hbm, b_buf), (v_hbm, v_buf))):
            copies.append(pltpu.make_async_copy(src.at[cells], dst.at[cells], sems.at[k, t]))
            copies[-1].start()
    m = m_ref[...]
    rest = m
    parts = []
    for _ in range(3):
        part = rest.astype(BF16)
        rest = rest - part.astype(F32)
        parts.append(part.astype(F32))
    tail = jnp.concatenate(parts + [jnp.zeros((TAIL - 3, ROWS), F32)], axis=0)
    tail = jnp.concatenate([tail, jnp.zeros((TAIL, LANES - ROWS), F32)], axis=1).astype(BF16)
    for k in range(WY * WZ):
        send[k, 4 * ROWS :, :] = tail
    flat = [buf.reshape(ROWS * SPAN, LANES) for buf in (b_buf, v_buf)]
    for t in range(WY):
        for k, mid in enumerate((0.0, MID)):
            copies[2 * t + k].wait()
            for g in range(2):
                parts = lane_blocks([flat[k][strided(16 * t + 8 * g + i), :] - mid for i in range(8)])
                rows = slice(ROWS * (2 * k + g), ROWS * (2 * k + g + 1))
                for z in range(WZ):
                    send[WZ * t + z, rows, :] = parts[z].astype(BF16)
                if k:
                    lanes = slice(LANES * (2 * t + g), LANES * (2 * t + g + 1))
                    cl[:, lanes] = parts[0].astype(BF16)
                    cr[:, lanes] = parts[7].astype(BF16)
    es[0] = (flat[1][strided(0), :] - MID).astype(BF16)
    es[1] = (flat[1][strided(SPAN - 1), :] - MID).astype(BF16)
    dl[...], dr[...] = edge_lanes(((cl[...], 0), (cr[...], BX - 1)), SPAN)


def to_lines(recv, bt, vt, metric, ends, *edges):
    count = WY * WZ
    nothing = jnp.zeros((1, LANES), F32)
    for k in range(count):
        rows = []
        for other, at in ((k - 1, ROWS - 1), (k + 1, 0)):
            if not 0 <= other < count:
                rows += [nothing] * 2
                continue
            m = jnp.sum(recv[other, 4 * ROWS :, :].astype(F32), axis=0, keepdims=True)
            for g in range(2):
                v = recv[other, ROWS * (2 + g) : ROWS * (3 + g), :].astype(F32) + MID
                rows.append(v[at : at + 1] * m[:, at : at + 1])
        ends[k] = jnp.concatenate(rows, axis=0)
    for i in range(8):
        row = jnp.zeros((TAIL, LANES), F32)
        for j in range(4):
            row += pltpu.roll(recv[4 * i + j, 4 * ROWS :, :].astype(F32), ROWS * j, 1)
        metric[:, i * LANES : (i + 1) * LANES] = jnp.sum(row, axis=0, keepdims=True)
    for j in range(4):
        for i in range(8):
            tile = recv[4 * i : 4 * i + 4, ROWS * j : ROWS * (j + 1), :].astype(F32).reshape(LANES, LANES).T
            out = bt if j < 2 else vt
            out[(j % 2) * LANES : (j % 2 + 1) * LANES, i * LANES : (i + 1) * LANES] = tile.astype(BF16)
    for k, ref in enumerate((bt, vt)):
        grid = ref[...].astype(F32).reshape(BS, BX, NW)
        rows = slice(BX * k, BX * (k + 1))
        edges[0][rows] = grid[0].astype(BF16)
        edges[1][rows] = grid[BS - 1].astype(BF16)
        edges[2][rows] = grid[:, 0, :].astype(BF16)
        edges[3][rows] = grid[:, BX - 1, :].astype(BF16)


def apply_lines(rows, line):
    return lax.dot_general(rows, line, (((1,), (1,)), ((), ())), preferred_element_type=F32)


def first_lines(bt, line, x1):
    x1[...] = WEIGHTS[0][1] * apply_lines(bt[...], line[...])


def fill(ext, middle, su, sd, xl, xr):
    ext[1 : BS + 1, 8 : 8 + BX, :] = middle
    ext[0, 8 : 8 + BX, :] = su
    ext[BS + 1, 8 : 8 + BX, :] = sd
    for s in range(BS):
        ext[s + 1, 7:8, :] = xl[s : s + 1]
        ext[s + 1, 8 + BX : 9 + BX, :] = xr[s : s + 1]


def line_resid(s, bt, xe, ve, metric, out):
    lane = lax.broadcasted_iota(jnp.int32, (BX, LANES), 1)
    count = NW // LANES

    def load(ref, j):
        lanes = slice(j * LANES, (j + 1) * LANES)
        return ref[s + 1, 8 : 8 + BX, lanes]

    xs = [load(xe, j) for j in range(count)]
    ks = [load(ve, j) * metric[:, j * LANES : (j + 1) * LANES] for j in range(count)]
    zero = jnp.zeros((BX, LANES), F32)
    xroll = [pltpu.roll(v, LANES - 1, 1) for v in xs] + [zero]
    kroll = [pltpu.roll(v, LANES - 1, 1) for v in ks] + [zero]
    last = lane == LANES - 1
    first = lane == 0
    carry = None
    for j in range(count):
        lanes = slice(j * LANES, (j + 1) * LANES)
        xc, kc = xs[j], ks[j]
        xn = jnp.where(last, xroll[j + 1], xroll[j])
        kn = jnp.where(last, kroll[j + 1], kroll[j])
        above = (kc + kn) * (xc - xn)
        moved = pltpu.roll(above, 1, 1)
        entry = kc * xc if j == 0 else carry
        total = above - jnp.where(first, entry if j else -entry, moved)
        carry = moved
        vc = ve[s + 1, 8 : 8 + BX, lanes]
        for si, x0 in ((s, 8), (s + 2, 8), (s + 1, 7), (s + 1, 9)):
            total += (vc + ve[si, x0 : x0 + BX, lanes]) * (xc - xe[si, x0 : x0 + BX, lanes])
        resid = bt[pl.ds(pl.multiple_of(s * BX, BX), BX), lanes].astype(F32) - (xc + 0.5 * total)
        out[pl.ds(pl.multiple_of(s * BX, BX), BX), lanes] = resid.astype(BF16)


def second_step(
    x1, bt, vt, su, sd, xl, xr, line, metric, x2, d2, e0, e1, e2, e3, xe, ve, rt, ends
):
    for k, ref in enumerate((su, sd, xl, xr)):
        ends[k * BX : (k + 1) * BX] = ref[0:BX]
    ends1 = WEIGHTS[0][1] * apply_lines(ends[...], line[...])
    fill(xe, x1[...].reshape(BS, BX, NW), *(ends1[k * BX : (k + 1) * BX] for k in range(4)))
    fill(
        ve,
        vt[...].astype(F32).reshape(BS, BX, NW) + MID,
        *(ref[BX : 2 * BX].astype(F32) + MID for ref in (su, sd, xl, xr)),
    )

    def one(s, _):
        line_resid(s, bt, xe, ve, metric, rt)
        return 0

    lax.fori_loop(0, BS, one, 0)
    keep, scale = WEIGHTS[1]
    d2[...] = keep * x1[...] + scale * apply_lines(rt[...], line[...])
    x2[...] = x1[...] + d2[...]
    grid = x2[...].reshape(BS, BX, NW)
    e0[...] = grid[0].astype(BF16)
    e1[...] = grid[BS - 1].astype(BF16)
    e2[...] = grid[:, 0, :].astype(BF16)
    e3[...] = grid[:, BX - 1, :].astype(BF16)


def third_step(
    x2, d2, bt, vt, su, sd, xl, xr, vsu, vsd, vxl, vxr, line, metric, ends, send, xe, ve, rt, x3
):
    fill(xe, x2[...].reshape(BS, BX, NW), *(ref[...].astype(F32) for ref in (su, sd, xl, xr)))
    fill(
        ve,
        vt[...].astype(F32).reshape(BS, BX, NW) + MID,
        *(ref[BX : 2 * BX].astype(F32) + MID for ref in (vsu, vsd, vxl, vxr)),
    )

    def one(s, _):
        line_resid(s, bt, xe, ve, metric, rt)
        return 0

    lax.fori_loop(0, BS, one, 0)
    keep, scale = WEIGHTS[2]
    x3[...] = x2[...] + keep * d2[...] + scale * apply_lines(rt[...], line[...])
    count = WY * WZ
    nothing = jnp.zeros((1, LANES), F32)
    firsts, lasts = {}, {}
    for j in range(2):
        for i in range(8):
            tile = x3[j * LANES : (j + 1) * LANES, i * LANES : (i + 1) * LANES].T
            for k in range(4):
                part = tile[ROWS * k : ROWS * (k + 1)]
                send[4 * i + k, ROWS * j : ROWS * (j + 1), :] = part.astype(BF16)
                firsts[4 * i + k, j] = part[:1]
                lasts[4 * i + k, j] = part[ROWS - 1 :]
    for k in range(count):
        rows = [lasts.get((k - 1, j), nothing) for j in range(2)]
        rows += [firsts.get((k + 1, j), nothing) for j in range(2)]
        send[k, 2 * ROWS :, :] = jnp.concatenate(rows + [ends[k]], axis=0).astype(BF16)


def unpack(recv, ves, vdl, vdr, xs, beyond, es, dl, dr, cl, cr):
    for t in range(WY):
        for g in range(2):
            rows = slice(ROWS * g, ROWS * (g + 1))
            parts = [recv[WZ * t + z, rows, :] for z in range(WZ)]
            lanes = slice(LANES * (2 * t + g), LANES * (2 * t + g + 1))
            cl[:, lanes] = parts[0]
            cr[:, lanes] = parts[7]
            parts = lane_blocks([p.astype(F32) for p in parts])
            for i in range(8):
                xs[16 * t + 8 * g + i] = parts[i]
        parts = lane_blocks([recv[WZ * t + z, 2 * ROWS :, :].astype(F32) for z in range(WZ)])
        for i in range(8):
            beyond[t, i] = parts[i]
    es[0] = xs[0].astype(BF16)
    es[1] = xs[SPAN - 1].astype(BF16)
    es[2] = ves[0]
    es[3] = ves[1]
    left, right = edge_lanes(((cl[...], 0), (cr[...], BX - 1)), 0)
    dl[...] = left + vdl[...]
    dr[...] = right + vdr[...]


def last_resid(
    xs, v_ref, b_ref, m_ref, beyond, spans, lefts, rights, x3, out, xe, ve, x_buf, r_buf, sems
):
    xe[1 : SPAN + 1] = xs[...]
    xe[0] = spans[1].astype(F32)
    xe[SPAN + 1] = spans[0].astype(F32)
    for s in range(SPAN):
        ve[s + 1] = v_ref[strided(s), :]
    ve[0] = spans[3].astype(F32) + MID
    ve[SPAN + 1] = spans[2].astype(F32) + MID
    row = lax.broadcasted_iota(jnp.int32, (ROWS, LANES), 0)
    lane = lax.broadcasted_iota(jnp.int32, (ROWS, LANES), 1)
    square = lax.broadcasted_iota(jnp.int32, (ROWS, ROWS), 0)
    square = square == lax.broadcasted_iota(jnp.int32, (ROWS, ROWS), 1)
    m = jnp.sum(jnp.where(square, m_ref[...], 0.0), axis=1, keepdims=True)
    near_left = lefts[...].astype(F32)
    near_right = rights[...].astype(F32)
    x_flat = x_buf.reshape(ROWS * SPAN, LANES)
    r_flat = r_buf.reshape(ROWS * SPAN, LANES)
    copies = []
    for t in range(WY):
        for g in range(2):
            for i in range(8):
                s = 16 * t + 8 * g + i
                xc, vc = xe[s + 1], ve[s + 1]
                x_flat[strided(s), :] = xc
                total = (vc + ve[s]) * (xc - xe[s]) + (vc + ve[s + 2]) * (xc - xe[s + 2])
                edge = beyond[t, i]
                xb, xa, kb, ka = (edge[2 * k + g : 2 * k + g + 1] for k in range(4))
                kc = m * vc
                xn = jnp.where(row == 0, xb, pltpu.roll(xc, 1, 0))
                kn = jnp.where(row == 0, kb, pltpu.roll(kc, 1, 0))
                total += (kc + kn) * (xc - xn)
                xn = jnp.where(row == ROWS - 1, xa, pltpu.roll(xc, ROWS - 1, 0))
                kn = jnp.where(row == ROWS - 1, ka, pltpu.roll(kc, ROWS - 1, 0))
                total += (kc + kn) * (xc - xn)
                xn = jnp.where(lane == 0, near_left[:, s : s + 1], pltpu.roll(xc, 1, 1))
                vn = near_left[:, SPAN + s : SPAN + s + 1] + MID
                vn = jnp.where(lane == 0, vn, pltpu.roll(vc, 1, 1))
                total += (vc + vn) * (xc - xn)
                xn = jnp.where(lane == LANES - 1, near_right[:, s : s + 1], pltpu.roll(xc, LANES - 1, 1))
                vn = near_right[:, SPAN + s : SPAN + s + 1] + MID
                vn = jnp.where(lane == LANES - 1, vn, pltpu.roll(vc, LANES - 1, 1))
                total += (vc + vn) * (xc - xn)
                r_flat[strided(s), :] = b_ref[strided(s), :] - (xc + 0.5 * total)
        cells = (slice(None), slice(BS * t, BS * (t + 1)), slice(None))
        for k, (src, dst) in enumerate(((x_buf, x3), (r_buf, out))):
            copies.append(pltpu.make_async_copy(src.at[cells], dst.at[cells], sems.at[k, t]))
            copies[-1].start()
    for copy in copies:
        copy.wait()


def block_edges(es, dl, dr):
    streams = lax.axis_size("stream")
    right = [(i, (i + 1) % streams) for i in range(streams)]
    left = [((i + 1) % streams, i) for i in range(streams)]
    return (
        lax.ppermute(es, "span", [(0, 1), (1, 0)]),
        lax.ppermute(dr, "stream", right),
        lax.ppermute(dl, "stream", left),
    )


def line_shift(value, ds, dx):
    spans, streams = lax.axis_size("span"), lax.axis_size("stream")
    pairs = []
    for y in range(WY):
        for z in range(WZ):
            for sp in range(spans):
                for st in range(streams):
                    sb = (sp * WY + y + ds) % (spans * WY)
                    xb = (st * WZ + z + dx) % (streams * WZ)
                    here = ((y * WZ + z) * spans + sp) * streams + st
                    there = ((sb % WY) * WZ + xb % WZ) * spans + sb // WY
                    pairs.append((here, there * streams + xb // WZ))
    return lax.ppermute(value, ("wall", "span", "stream"), pairs)


def line_edges(*edges):
    return (
        line_shift(edges[1], 1, 0),
        line_shift(edges[0], -1, 0),
        line_shift(edges[3], 0, 1),
        line_shift(edges[2], 0, -1),
    )


def body(right_side, viscosity, wall_metric, line_inverse):
    b = right_side.reshape(ROWS * SPAN, LANES)
    v = viscosity.reshape(ROWS * SPAN, LANES)
    m = wall_metric.reshape(1, ROWS)
    block = pltpu.VMEM((ROWS, SPAN, LANES), F32)
    sems = pltpu.SemaphoreType.DMA((2, WY))
    side = pltpu.VMEM((ROWS, 8 * LANES), BF16)
    dense = shape((ROWS, LANES), BF16)
    hbm, vmem = pl.BlockSpec(memory_space=pltpu.HBM), pl.BlockSpec(memory_space=pltpu.VMEM)
    send, *v_edges = call(
        pack,
        (
            shape((WY * WZ, 4 * ROWS + TAIL, LANES), BF16),
            shape((2, ROWS, LANES), BF16),
            dense,
            dense,
        ),
        (block, block, side, side, sems),
        in_specs=(hbm, hbm, vmem),
    )(right_side, viscosity, m)
    recv = lax.all_to_all(send, "wall", 0, 0, tiled=True)
    lines = shape((CELLS, NW), BF16)
    bt, vt, metric, ends, *edges = call(
        to_lines,
        (lines, lines, shape((1, NW), F32), shape((WY * WZ, 4, LANES), F32))
        + (shape((2 * BX, NW), BF16),) * 4,
    )(recv)
    near = line_edges(*edges)
    x1 = call(first_lines, shape((CELLS, NW), F32))(bt, line_inverse)
    ext = pltpu.VMEM((BS + 2, 2 * BX, NW), F32)
    field = shape((CELLS, NW), F32)
    rounded = pltpu.VMEM((CELLS, NW), BF16)
    x2, d2, *edges = call(
        second_step,
        (field, field) + (shape((BX, NW), BF16),) * 4,
        (ext, ext, rounded, pltpu.VMEM((4 * BX, NW), BF16)),
    )(x1, bt, vt, *near, line_inverse, metric)
    x_near = line_edges(*edges)
    send = call(
        third_step,
        shape((WY * WZ, 2 * ROWS + TAIL, LANES), BF16),
        (ext, ext, rounded, pltpu.VMEM((CELLS, NW), F32)),
    )(x2, d2, bt, vt, *x_near, *near, line_inverse, metric, ends)
    recv = lax.all_to_all(send, "wall", 0, 0, tiled=True)
    xs, beyond, *edges = call(
        unpack,
        (
            shape((SPAN, ROWS, LANES), F32),
            shape((WY, 8, TAIL, LANES), F32),
            shape((4, ROWS, LANES), BF16),
            dense,
            dense,
        ),
        (side, side),
    )(recv, *v_edges)
    x_edges = block_edges(*edges)
    tall = pltpu.VMEM((SPAN + 2, ROWS, LANES), F32)
    whole = shape(right_side.shape, F32)
    return call(
        last_resid,
        (whole, whole),
        (tall, tall, block, block, sems),
        out_specs=(hbm, hbm),
    )(xs, v, b, m, beyond, *x_edges)


def solution(mesh):
    in_specs = (P("wall", "span", "stream"), P("wall", "span", "stream"), P("wall"), P())
    out_specs = (P("wall", "span", "stream"), P("wall", "span", "stream"))
    return jax.shard_map(body, mesh=mesh, in_specs=in_specs, out_specs=out_specs, check_vma=False)
```

```python
import functools

import jax
import jax.numpy as jnp
from jax import lax
from jax.experimental import pallas as pl
from jax.experimental.pallas import tpu as pltpu
from jax.sharding import PartitionSpec as P

STEPS = 3
NW, WY, WZ = 1024, 4, 8
ROWS, SPAN, LANES = 32, 64, 128
BS, BX = 16, 16
CELLS = BS * BX
CHUNKS = NW // 128
LP, FIRST, BUSY, ROW_COUNT = BX + 2, 24, 288, 336
RUN = 48
CP = SPAN + 3
BLOCK_ROWS = 2280
TAIL = 8
MID = 0.5
F32, BF16 = jnp.float32, jnp.bfloat16
MIB = 1024 * 1024


def chebyshev_weights(steps):
    lowest = 0.25
    highest = 2.5
    center = 0.5 * (highest + lowest)
    half = 0.5 * (highest - lowest)
    ratio = center / half
    weights = [(0.0, 1.0 / center)]
    rho_old = 1.0 / ratio
    for step in range(1, steps):
        rho_new = 1.0 / (2.0 * ratio - rho_old)
        weights.append((rho_new * rho_old, 2.0 * rho_new / half))
        rho_old = rho_new
    return weights


WEIGHTS = chebyshev_weights(STEPS)


def shape(dims, dtype):
    return jax.ShapeDtypeStruct(dims, dtype)


def call(kernel, outs, scratch=(), limit=40 * MIB, **specs):
    return pl.pallas_call(
        kernel,
        out_shape=outs,
        scratch_shapes=list(scratch),
        compiler_params=pltpu.CompilerParams(vmem_limit_bytes=limit),
        cost_estimate=pl.CostEstimate(flops=10**7, bytes_accessed=4 * 10**6, transcendentals=0),
        **specs,
    )


def skew(arrays):
    block = lax.broadcasted_iota(jnp.int32, arrays[0].shape, 1) // BX
    arrays = list(arrays)
    for bit in range(3):
        step = 1 << bit
        upper = (block // step) % 2 == 1
        arrays = [jnp.where(upper, arrays[(j + step) % 8], arrays[j]) for j in range(8)]
    return [arrays[-z % 8] for z in range(8)]


def to_blocks(rows):
    return skew([pltpu.roll(row, BX * i, 1) if i else row for i, row in enumerate(rows)])


def from_blocks(blocks):
    return [pltpu.roll(row, LANES - BX * i, 1) if i else row for i, row in enumerate(skew(blocks))]


def turned(p):
    z, odd = lax.axis_index("wall") % WZ, lax.axis_index("stream") % 2
    return (p - (z + odd * (WZ - 1 - 2 * z)) + WZ) % WZ


def owner(t, z):
    span, odd = lax.axis_index("span"), lax.axis_index("stream") % 2
    return WZ * (t + span * (WY - 1 - 2 * t)) + z + odd * (WZ - 1 - 2 * z)


def strided(s):
    return pl.ds(s, ROWS, stride=SPAN + 1)


def edge_lanes(blocks, pick, turn, offset):
    at = lax.broadcasted_iota(jnp.int32, (LANES, LANES), 0)
    to = lax.broadcasted_iota(jnp.int32, (LANES, LANES), 1)
    one = jnp.where((at % BX == pick) & (to == (at // BX + turn) % 8), 1.0, 0.0).astype(BF16)
    eights = jnp.dot(blocks.reshape(8 * ROWS, LANES), one, preferred_element_type=F32)
    out = jnp.zeros((ROWS, LANES), F32)
    for q in range(8):
        out += pltpu.roll(eights[ROWS * q : ROWS * (q + 1)], (8 * q + offset) % LANES, 1)
    return out.astype(BF16)


def pack(
    b_hbm, v_hbm, m_hbm, send_hbm, es_hbm, dl_hbm, dr_hbm, b_buf, v_buf, m_buf, send, es, dl, dr, cl, cr,
    sems, done, small,
):
    def copy(k, w):
        src, dst = ((v_hbm, v_buf), (b_hbm, b_buf))[k]
        return pltpu.make_async_copy(src.at[w], dst.at[pl.ds((SPAN + 1) * w, SPAN)], sems.at[k, w])

    def result(y):
        peers = pl.ds(WZ * y, WZ)
        return pltpu.make_async_copy(send.at[peers], send_hbm.at[peers], done.at[y])

    for k in range(2):
        for w in range(ROWS):
            copy(k, w).start()
    metric = pltpu.make_async_copy(m_hbm, m_buf, small.at[3])
    metric.start()
    edges = [
        pltpu.make_async_copy(src, dst, small.at[n])
        for n, (src, dst) in enumerate(((es, es_hbm), (dl, dl_hbm), (dr, dr_hbm)))
    ]
    metric.wait()
    rest = m_buf[...]
    parts = []
    for _ in range(3):
        part = rest.astype(BF16)
        rest = rest - part.astype(F32)
        parts.append(part.astype(F32))
    tail = jnp.concatenate(parts + [jnp.zeros((TAIL - 3, ROWS), F32)], axis=0)
    tail = jnp.concatenate([tail, jnp.zeros((TAIL, LANES - ROWS), F32)], axis=1).astype(BF16)
    for k in range(WY * WZ):
        send[k, 4 * ROWS :, :] = tail

    def move(t, k, buf, mid):
        for g in range(2):
            parts = [buf[strided(16 * t + 8 * g + i), :] - mid for i in range(8)]
            parts = to_blocks([part.astype(BF16) for part in parts])
            rows = slice(ROWS * (2 * k + g), ROWS * (2 * k + g + 1))
            for z in range(WZ):
                send[owner(t, z), rows, :] = parts[z]
            if k:
                cl[2 * t + g] = parts[0]
                cr[2 * t + g] = parts[7]
        return 0

    for w in range(ROWS):
        copy(0, w).wait()
    lax.fori_loop(0, WY, lambda t, _: move(t, 1, v_buf, MID), 0)
    es[0] = (v_buf[strided(0), :] - MID).astype(BF16)
    es[1] = (v_buf[strided(SPAN - 1), :] - MID).astype(BF16)
    dl[...] = edge_lanes(cl[...], 0, 0, SPAN)
    dr[...] = edge_lanes(cr[...], BX - 1, 1, SPAN)
    for edge in edges:
        edge.start()
    for w in range(ROWS):
        copy(1, w).wait()

    def last(t, _):
        move(t, 0, b_buf, 0.0)
        result(owner(t, 0) // WZ).start()
        return 0

    lax.fori_loop(0, WY, last, 0)
    for t in range(WY):
        result(t).wait()
    for edge in edges:
        edge.wait()


def to_lines(recv, bf, hf, b0, metric, ends, *edges):
    count = WY * WZ
    nothing = jnp.zeros((1, LANES), F32)
    for k in range(count):
        rows = []
        for g in range(2):
            for other, at in ((k - 1, ROWS - 1), (k + 1, 0)):
                if not 0 <= other < count:
                    rows.append(nothing)
                    continue
                m = jnp.sum(recv[other, 4 * ROWS :, :].astype(F32), axis=0, keepdims=True)
                v = recv[other, ROWS * (2 + g) : ROWS * (3 + g), :].astype(F32) + MID
                rows.append(v[at : at + 1] * m[:, at : at + 1])
        ends[k] = jnp.concatenate(rows, axis=0)
    for i in range(8):
        row = jnp.zeros((TAIL, LANES), F32)
        for j in range(4):
            row += pltpu.roll(recv[4 * i + j, 4 * ROWS :, :].astype(F32), ROWS * j, 1)
        metric[:, i * LANES : (i + 1) * LANES] = jnp.sum(row, axis=0, keepdims=True)
    for k, ref in enumerate((bf, hf)):
        for i in range(CHUNKS):
            for g in range(2):
                tile = recv[4 * i : 4 * i + 4, ROWS * (2 * k + g) : ROWS * (2 * k + g + 1), :]
                tile = tile.astype(F32).reshape(LANES, LANES).T
                if k:
                    tile = 0.5 * tile + 0.5 * MID
                for p in range(8):
                    ref[line_rows(i, 8 * g + turned(p)), :] = tile[BX * p : BX * (p + 1)]
    for i in range(CHUNKS):
        lanes = slice(i * LANES, (i + 1) * LANES)
        b0[:, lanes] = bf[pl.ds(ROW_COUNT * i + FIRST, BUSY), :].astype(BF16)
        for n, rows in enumerate(edge_rows(i)):
            edges[n][:BX, lanes] = bf[rows, :].astype(BF16)
            edges[n][BX:, lanes] = (2.0 * hf[rows, :] - MID).astype(BF16)


def line_rows(i, s):
    return pl.ds(ROW_COUNT * i + FIRST + LP * s, BX)


def edge_rows(i):
    base = ROW_COUNT * i + FIRST
    return (
        line_rows(i, 0),
        line_rows(i, BS - 1),
        pl.ds(base, BS, stride=LP),
        pl.ds(base + BX - 1, BS, stride=LP),
    )


def near_rows(i):
    base = ROW_COUNT * i + FIRST
    return (
        line_rows(i, -1),
        line_rows(i, BS),
        pl.ds(base - 1, BS, stride=LP),
        pl.ds(base + BX, BS, stride=LP),
    )


def busy(i):
    return pl.ds(ROW_COUNT * i + FIRST, BUSY)


def apply_lines(rows, line):
    return lax.dot_general(rows, line, (((1,), (1,)), ((), ())), preferred_element_type=F32)


def first_lines(b0, hf, metric, line, x1, fw):
    y = WEIGHTS[0][1] * apply_lines(b0[...], line[...])
    for i in range(CHUNKS):
        x1[busy(i), :] = y[:, i * LANES : (i + 1) * LANES]
    last = lax.broadcasted_iota(jnp.int32, (RUN, LANES), 1) == LANES - 1

    def one(c, _):
        after = jnp.zeros((RUN, LANES), F32)
        for i in reversed(range(CHUNKS)):
            rows = pl.ds(ROW_COUNT * i + FIRST + RUN * c, RUN)
            half = hf[rows, :] * metric[:, i * LANES : (i + 1) * LANES]
            moved = pltpu.roll(half, LANES - 1, 1)
            fw[rows, :] = half + jnp.where(last, after, moved)
            after = moved
        return 0

    lax.fori_loop(0, BUSY // RUN, one, 0)


def line_resid(bf, xe, he, fw, metric, out):
    lane = lax.broadcasted_iota(jnp.int32, (RUN, LANES), 1)
    last, first = lane == LANES - 1, lane == 0

    def one(c, _):
        def load(ref, i, shift=0):
            return ref[pl.ds(ROW_COUNT * i + FIRST + shift + RUN * c, RUN), :]

        xc = load(xe, 0)
        moved_x = pltpu.roll(xc, LANES - 1, 1)
        entry = load(he, 0) * metric[:, :LANES] * -xc
        for i in range(CHUNKS):
            if i + 1 < CHUNKS:
                after = load(xe, i + 1)
                moved_after = pltpu.roll(after, LANES - 1, 1)
            else:
                after = moved_after = jnp.zeros((RUN, LANES), F32)
            above = load(fw, i) * (xc - jnp.where(last, moved_after, moved_x))
            below = pltpu.roll(above, 1, 1)
            hc = load(he, i)
            total = above - jnp.where(first, entry, below)
            for shift in (-LP, -1, 1, LP):
                total += (hc + load(he, i, shift)) * (xc - load(xe, i, shift))
            rows = pl.ds(pl.multiple_of(RUN * c, BX), RUN)
            out[rows, i * LANES : (i + 1) * LANES] = (load(bf, i) - (xc + total)).astype(BF16)
            xc, moved_x, entry = after, moved_after, below
        return 0

    lax.fori_loop(0, BUSY // RUN, one, 0)


def second_step(x1, bf, hf, fw, su, sd, xl, xr, line, metric, x2, d2, he, e0, e1, e2, e3, xe, rt, ends):
    for k, ref in enumerate((su, sd, xl, xr)):
        ends[k * BX : (k + 1) * BX] = ref[0:BX]
    ends1 = WEIGHTS[0][1] * apply_lines(ends[...], line[...])
    for i in range(CHUNKS):
        lanes = slice(i * LANES, (i + 1) * LANES)
        xe[busy(i), :] = x1[busy(i), :]
        he[busy(i), :] = hf[busy(i), :]
        for k, (rows, ref) in enumerate(zip(near_rows(i), (su, sd, xl, xr))):
            xe[rows, :] = ends1[k * BX : (k + 1) * BX, lanes]
            he[rows, :] = 0.5 * ref[BX : 2 * BX, lanes].astype(F32) + 0.5 * MID
    line_resid(bf, xe, he, fw, metric, rt)
    keep, scale = WEIGHTS[1]
    y = scale * apply_lines(rt[...], line[...])
    for i in range(CHUNKS):
        lanes = slice(i * LANES, (i + 1) * LANES)
        x = x1[busy(i), :]
        d = keep * x + y[:, lanes]
        d2[busy(i), :] = d
        x2[busy(i), :] = x + d
        for rows, ref in zip(edge_rows(i), (e0, e1, e2, e3)):
            ref[:, lanes] = x2[rows, :].astype(BF16)


def third_step(x2, d2, bf, he, fw, su, sd, xl, xr, line, metric, ends, send, xe, rt):
    for i in range(CHUNKS):
        lanes = slice(i * LANES, (i + 1) * LANES)
        xe[busy(i), :] = x2[busy(i), :]
        for rows, ref in zip(near_rows(i), (su, sd, xl, xr)):
            xe[rows, :] = ref[:, lanes].astype(F32)
    line_resid(bf, xe, he, fw, metric, rt)
    keep, scale = WEIGHTS[2]
    y = scale * apply_lines(rt[...], line[...])
    count = WY * WZ
    nothing = jnp.zeros((1, LANES), F32)
    firsts, lasts = {}, {}
    for i in range(CHUNKS):
        xe[busy(i), :] = x2[busy(i), :] + keep * d2[busy(i), :] + y[:, i * LANES : (i + 1) * LANES]
        for j in range(2):
            tile = jnp.concatenate([xe[line_rows(i, 8 * j + turned(p)), :] for p in range(8)], axis=0).T
            for k in range(4):
                part = tile[ROWS * k : ROWS * (k + 1)]
                send[4 * i + k, ROWS * j : ROWS * (j + 1), :] = part.astype(BF16)
                firsts[4 * i + k, j] = part[:1]
                lasts[4 * i + k, j] = part[ROWS - 1 :]
    for k in range(count):
        rows = []
        for j in range(2):
            rows += [lasts.get((k - 1, j), nothing), firsts.get((k + 1, j), nothing)]
            rows.append(ends[k, 2 * j : 2 * j + 2, :])
        send[k, 2 * ROWS :, :] = jnp.concatenate(rows, axis=0).astype(BF16)


def block_row(w, s=0):
    return CP * (w + 1) + 1 + s


def unpack(recv, ves, vdl, vdr, xf, kappas, es, dl, dr, cl, cr):
    def one(t, _):
        for g in range(2):
            rows = slice(ROWS * g, ROWS * (g + 1))
            parts = [recv[owner(t, z), rows, :] for z in range(WZ)]
            cl[2 * t + g] = parts[0]
            cr[2 * t + g] = parts[7]
            parts = from_blocks(parts)
            for i in range(8):
                s = 16 * t + 8 * g + i
                xf[pl.ds(block_row(0) + s, ROWS, stride=CP), :] = parts[i].astype(F32)
        parts = from_blocks([recv[owner(t, z), 2 * ROWS :, :].astype(F32) for z in range(WZ)])
        for g in range(2):
            for i in range(8):
                s = 16 * t + 8 * g + i
                for k, (ref, row) in enumerate(
                    ((xf, block_row(-1)), (xf, block_row(ROWS)), (kappas, 0), (kappas, SPAN))
                ):
                    ref[pl.ds(row + s, 1), :] = parts[i][4 * g + k : 4 * g + k + 1]
        return 0

    lax.fori_loop(0, WY, one, 0)
    es[0] = xf[pl.ds(block_row(0), ROWS, stride=CP), :].astype(BF16)
    es[1] = xf[pl.ds(block_row(0, SPAN - 1), ROWS, stride=CP), :].astype(BF16)
    es[2] = ves[0]
    es[3] = ves[1]
    dl[...] = edge_lanes(cl[...], 0, 0, 0) + vdl[...]
    dr[...] = edge_lanes(cr[...], BX - 1, 1, 0) + vdr[...]


def stage(xf, v_ref, kappas, m_ref, x3, hf, gx, gk, x_buf, sems):
    def result(n):
        rows = pl.ds(4 * n, 4)
        return pltpu.make_async_copy(x_buf.at[rows], x3.at[rows], sems.at[n])

    def four(n, below):
        for k in range(4):
            w = 4 * n + k
            x_buf[w] = xf[pl.ds(block_row(w), SPAN), :]
        result(n).start()
        for k in range(4):
            w = 4 * n + k
            half = 0.5 * v_ref[w]
            hf[pl.ds(block_row(w), SPAN), :] = half
            cells = pl.ds(pl.multiple_of(SPAN * w, SPAN), SPAN)
            gx[cells, :] = half + pltpu.roll(half, LANES - 1, 1)
            half = m_ref[w] * half
            gk[cells, :] = below + half
            below = half
        return below

    below = lax.fori_loop(0, ROWS // 4, four, 0.5 * kappas[:SPAN, :])
    gk[SPAN * ROWS :, :] = below + 0.5 * kappas[SPAN:, :]
    for n in range(ROWS // 4):
        result(n).wait()


def last_resid(xf, hf, gx, gk, b_ref, spans, lefts, rights, dl, dr, out, xe, he, r_buf, sems):
    xe[...] = xf[...]
    he[...] = hf[...]
    for s, k in ((-1, 1), (SPAN, 0)):
        rows = pl.ds(block_row(0, s), ROWS, stride=CP)
        xe[rows, :] = spans[k].astype(F32)
        he[rows, :] = 0.5 * spans[2 + k].astype(F32) + 0.5 * MID
    at = lax.broadcasted_iota(jnp.int32, (2 * ROWS, LANES), 0)
    to = lax.broadcasted_iota(jnp.int32, (2 * ROWS, LANES), 1)
    place = jnp.where(to == 2 * (at % ROWS) + at // ROWS, 1.0, 0.0).astype(BF16)

    def placed(right, left):
        both = jnp.concatenate([right[...], left[...]], axis=0)
        return lax.dot_general(both, place, (((0,), (0,)), ((), ())), preferred_element_type=F32)

    own, near = placed(dr, dl), placed(rights, lefts)
    sides = (0.5 * (own[SPAN:] + near[SPAN:]) + MID) * (own[:SPAN] - near[:SPAN])
    lane = lax.broadcasted_iota(jnp.int32, (ROWS, LANES), 1)
    halves = (0, ROWS)

    def load(ref, w, s):
        return ref[pl.ds(block_row(w, s), ROWS), :]

    def results(q):
        rows = pl.ds(4 * q, 4)
        return pltpu.make_async_copy(r_buf.at[rows], out.at[rows], sems.at[q])

    def four(q, carry):
        carry = list(carry)
        for n in range(4):
            w = 4 * q + n
            for h, s in enumerate(halves):
                xc, hc = load(xe, w, s), load(he, w, s)
                above = gk[pl.ds(SPAN * (w + 1) + s, ROWS), :] * (xc - load(xe, w + 1, s))
                total = above - carry[h]
                carry[h] = above
                for d in (-1, 1):
                    total += (hc + load(he, w, s + d)) * (xc - load(xe, w, s + d))
                side = pltpu.roll(sides[s : s + ROWS], LANES - 1 - 2 * w, 1)
                right = gx[pl.ds(SPAN * w + s, ROWS), :] * (xc - pltpu.roll(xc, LANES - 1, 1))
                total += jnp.where(lane == LANES - 1, side, right)
                total += jnp.where(lane == 0, side, -pltpu.roll(right, 1, 1))
                r_buf[w, s : s + ROWS, :] = b_ref[w, s : s + ROWS, :] - (xc + total)
        results(q).start()
        return tuple(carry)

    start = [gk[s : s + ROWS, :] * (load(xe, -1, s) - load(xe, 0, s)) for s in halves]
    lax.fori_loop(0, ROWS // 4, four, tuple(start))
    for q in range(ROWS // 4):
        results(q).wait()


def block_edges(es, dl, dr):
    streams = lax.axis_size("stream")
    right = [(i, (i + 1) % streams) for i in range(streams)]
    left = [((i + 1) % streams, i) for i in range(streams)]
    return (
        lax.ppermute(es, "span", [(0, 1), (1, 0)]),
        lax.ppermute(dr, "stream", right),
        lax.ppermute(dl, "stream", left),
    )


def line_shift(value, ds, dx):
    spans, streams = lax.axis_size("span"), lax.axis_size("stream")

    def device(sb, xb):
        sp, y = divmod(sb % (spans * WY), WY)
        st, z = divmod(xb % (streams * WZ), WZ)
        y, z = (WY - 1 - y if sp % 2 else y), (WZ - 1 - z if st % 2 else z)
        return ((y * WZ + z) * spans + sp) * streams + st

    pairs = [
        (device(sb, xb), device(sb + ds, xb + dx))
        for sb in range(spans * WY)
        for xb in range(streams * WZ)
    ]
    return lax.ppermute(value, ("wall", "span", "stream"), pairs)


def line_edges(*edges):
    return (
        line_shift(edges[1], 1, 0),
        line_shift(edges[0], -1, 0),
        line_shift(edges[3], 0, 1),
        line_shift(edges[2], 0, -1),
    )


def body(right_side, viscosity, wall_metric, line_inverse):
    block = pltpu.VMEM((ROWS, SPAN, LANES), F32)
    side = pltpu.VMEM((8, ROWS, LANES), BF16)
    dense = shape((ROWS, LANES), BF16)
    hbm, vmem = pl.BlockSpec(memory_space=pltpu.HBM), pl.BlockSpec(memory_space=pltpu.VMEM)
    sent = (WY * WZ, 4 * ROWS + TAIL, LANES)
    loose = pltpu.VMEM(((SPAN + 1) * ROWS, LANES), F32)
    dma = pltpu.SemaphoreType.DMA
    send, *v_edges = call(
        pack,
        (shape(sent, BF16), shape((2, ROWS, LANES), BF16), dense, dense),
        (
            loose,
            loose,
            pltpu.VMEM((1, ROWS), F32),
            pltpu.VMEM(sent, BF16),
            pltpu.VMEM((2, ROWS, LANES), BF16),
            pltpu.VMEM((ROWS, LANES), BF16),
            pltpu.VMEM((ROWS, LANES), BF16),
            side,
            side,
            dma((2, ROWS)),
            dma((WY,)),
            dma((4,)),
        ),
        62 * MIB + MIB // 2,
        in_specs=(hbm,) * 3,
        out_specs=(hbm,) * 4,
    )(right_side, viscosity, wall_metric.reshape(1, ROWS))
    recv = lax.all_to_all(send, "wall", 0, 0, tiled=True)
    field = shape((CHUNKS * ROW_COUNT, LANES), F32)
    bf, hf, b0, metric, ends, *edges = call(
        to_lines,
        (field, field, shape((BUSY, NW), BF16), shape((1, NW), F32))
        + (shape((WY * WZ, 4, LANES), F32),)
        + (shape((2 * BX, NW), BF16),) * 4,
    )(recv)
    near = line_edges(*edges)
    x1, fw = call(first_lines, (field, field))(b0, hf, metric, line_inverse)
    ext = pltpu.VMEM((CHUNKS * ROW_COUNT, LANES), F32)
    rounded = pltpu.VMEM((BUSY, NW), BF16)
    x2, d2, he, *edges = call(
        second_step,
        (field, field, field) + (shape((BX, NW), BF16),) * 4,
        (ext, rounded, pltpu.VMEM((4 * BX, NW), BF16)),
    )(x1, bf, hf, fw, *near, line_inverse, metric)
    x_near = line_edges(*edges)
    send = call(
        third_step, shape((WY * WZ, 2 * ROWS + TAIL, LANES), BF16), (ext, rounded)
    )(x2, d2, bf, he, fw, *x_near, line_inverse, metric, ends)
    recv = lax.all_to_all(send, "wall", 0, 0, tiled=True)
    cells = shape((BLOCK_ROWS, LANES), F32)
    xf, kappas, *edges = call(
        unpack,
        (cells, shape((2 * SPAN, LANES), F32), shape((4, ROWS, LANES), BF16), dense, dense),
        (side, side),
    )(recv, *v_edges)
    x_edges = block_edges(*edges)
    whole = shape(right_side.shape, F32)
    smem = pl.BlockSpec(memory_space=pltpu.SMEM)
    x3, hf, gx, gk = call(
        stage,
        (
            whole,
            cells,
            shape((ROWS * SPAN, LANES), F32),
            shape(((ROWS + 1) * SPAN, LANES), F32),
        ),
        (block, dma((ROWS // 4,))),
        in_specs=(vmem, vmem, vmem, smem),
        out_specs=(hbm, vmem, vmem, vmem),
    )(xf, viscosity, kappas, wall_metric)
    loose = pltpu.VMEM((BLOCK_ROWS, LANES), F32)
    residual = call(
        last_resid,
        whole,
        (loose, loose, block, dma((ROWS // 4,))),
        out_specs=hbm,
    )(xf, hf, gx, gk, right_side, *x_edges, *edges[1:])
    return x3, residual


def solution(mesh):
    in_specs = (P("wall", "span", "stream"), P("wall", "span", "stream"), P("wall"), P())
    out_specs = (P("wall", "span", "stream"), P("wall", "span", "stream"))
    return jax.shard_map(body, mesh=mesh, in_specs=in_specs, out_specs=out_specs, check_vma=False)
```

```python
import functools

import jax
import jax.numpy as jnp
from jax import lax
from jax.experimental import pallas as pl
from jax.experimental.pallas import tpu as pltpu
from jax.sharding import PartitionSpec as P

STEPS = 3
NW, WY, WZ = 1024, 4, 8
ROWS, SPAN, LANES = 32, 64, 128
BS, BX = 16, 16
CELLS = BS * BX
CHUNKS = NW // 128
LP, FIRST, BUSY, ROW_COUNT = BX + 2, 24, 288, 336
RUN = 48
CP = SPAN + 3
BLOCK_ROWS = 2280
TAIL = 8
MID = 0.5
F32, BF16 = jnp.float32, jnp.bfloat16
MIB = 1024 * 1024


def chebyshev_weights(steps):
    lowest = 0.25
    highest = 2.5
    center = 0.5 * (highest + lowest)
    half = 0.5 * (highest - lowest)
    ratio = center / half
    weights = [(0.0, 1.0 / center)]
    rho_old = 1.0 / ratio
    for step in range(1, steps):
        rho_new = 1.0 / (2.0 * ratio - rho_old)
        weights.append((rho_new * rho_old, 2.0 * rho_new / half))
        rho_old = rho_new
    return weights


WEIGHTS = chebyshev_weights(STEPS)


def shape(dims, dtype):
    return jax.ShapeDtypeStruct(dims, dtype)


def call(kernel, outs, scratch=(), limit=40 * MIB, **specs):
    return pl.pallas_call(
        kernel,
        out_shape=outs,
        scratch_shapes=list(scratch),
        compiler_params=pltpu.CompilerParams(vmem_limit_bytes=limit),
        cost_estimate=pl.CostEstimate(flops=10**7, bytes_accessed=4 * 10**6, transcendentals=0),
        **specs,
    )


def skew(arrays):
    block = lax.broadcasted_iota(jnp.int32, arrays[0].shape, 1) // BX
    arrays = list(arrays)
    for bit in range(3):
        step = 1 << bit
        upper = (block // step) % 2 == 1
        arrays = [jnp.where(upper, arrays[(j + step) % 8], arrays[j]) for j in range(8)]
    return [arrays[-z % 8] for z in range(8)]


def to_blocks(rows):
    return skew([pltpu.roll(row, BX * i, 1) if i else row for i, row in enumerate(rows)])


def from_blocks(blocks):
    return [pltpu.roll(row, LANES - BX * i, 1) if i else row for i, row in enumerate(skew(blocks))]


def turned(p):
    z, odd = lax.axis_index("wall") % WZ, lax.axis_index("stream") % 2
    return (p - (z + odd * (WZ - 1 - 2 * z)) + WZ) % WZ


def owner(t, z):
    span, odd = lax.axis_index("span"), lax.axis_index("stream") % 2
    return WZ * (t + span * (WY - 1 - 2 * t)) + z + odd * (WZ - 1 - 2 * z)


def strided(s):
    return pl.ds(s, ROWS, stride=SPAN + 1)


def edge_lanes(blocks, pick, turn, offset):
    at = lax.broadcasted_iota(jnp.int32, (LANES, LANES), 0)
    to = lax.broadcasted_iota(jnp.int32, (LANES, LANES), 1)
    one = jnp.where((at % BX == pick) & (to == (at // BX + turn) % 8), 1.0, 0.0).astype(BF16)
    eights = jnp.dot(blocks.reshape(8 * ROWS, LANES), one, preferred_element_type=F32)
    out = jnp.zeros((ROWS, LANES), F32)
    for q in range(8):
        out += pltpu.roll(eights[ROWS * q : ROWS * (q + 1)], (8 * q + offset) % LANES, 1)
    return out.astype(BF16)


def pack(
    b_hbm, v_hbm, m_hbm, send_hbm, es_hbm, dl_hbm, dr_hbm, b_buf, v_buf, m_buf, send, es, dl, dr, cl, cr,
    sems, done, small,
):
    def copy(k, w):
        src, dst = ((v_hbm, v_buf), (b_hbm, b_buf))[k]
        return pltpu.make_async_copy(src.at[w], dst.at[pl.ds((SPAN + 1) * w, SPAN)], sems.at[k, w])

    def result(y):
        peers = pl.ds(WZ * y, WZ)
        return pltpu.make_async_copy(send.at[peers], send_hbm.at[peers], done.at[y])

    for k in range(2):
        for w in range(ROWS):
            copy(k, w).start()
    metric = pltpu.make_async_copy(m_hbm, m_buf, small.at[3])
    metric.start()
    edges = [
        pltpu.make_async_copy(src, dst, small.at[n])
        for n, (src, dst) in enumerate(((es, es_hbm), (dl, dl_hbm), (dr, dr_hbm)))
    ]
    metric.wait()
    rest = m_buf[...]
    parts = []
    for _ in range(3):
        part = rest.astype(BF16)
        rest = rest - part.astype(F32)
        parts.append(part.astype(F32))
    tail = jnp.concatenate(parts + [jnp.zeros((TAIL - 3, ROWS), F32)], axis=0)
    tail = jnp.concatenate([tail, jnp.zeros((TAIL, LANES - ROWS), F32)], axis=1).astype(BF16)
    for k in range(WY * WZ):
        send[k, 4 * ROWS :, :] = tail

    def move(t, k, buf, mid):
        for g in range(2):
            parts = [buf[strided(16 * t + 8 * g + i), :] - mid for i in range(8)]
            parts = to_blocks([part.astype(BF16) for part in parts])
            rows = slice(ROWS * (2 * k + g), ROWS * (2 * k + g + 1))
            for z in range(WZ):
                send[owner(t, z), rows, :] = parts[z]
            if k:
                cl[2 * t + g] = parts[0]
                cr[2 * t + g] = parts[7]
        return 0

    for w in range(ROWS):
        copy(0, w).wait()
    lax.fori_loop(0, WY, lambda t, _: move(t, 1, v_buf, MID), 0)
    es[0] = (v_buf[strided(0), :] - MID).astype(BF16)
    es[1] = (v_buf[strided(SPAN - 1), :] - MID).astype(BF16)
    dl[...] = edge_lanes(cl[...], 0, 0, SPAN)
    dr[...] = edge_lanes(cr[...], BX - 1, 1, SPAN)
    for edge in edges:
        edge.start()
    for w in range(ROWS):
        copy(1, w).wait()

    def last(t, _):
        move(t, 0, b_buf, 0.0)
        result(owner(t, 0) // WZ).start()
        return 0

    lax.fori_loop(0, WY, last, 0)
    for t in range(WY):
        result(t).wait()
    for edge in edges:
        edge.wait()


def to_lines(recv, bf, hf, b0, metric, ends, *edges):
    count = WY * WZ
    nothing = jnp.zeros((1, LANES), F32)
    for k in range(count):
        rows = []
        for g in range(2):
            for other, at in ((k - 1, ROWS - 1), (k + 1, 0)):
                if not 0 <= other < count:
                    rows.append(nothing)
                    continue
                m = jnp.sum(recv[other, 4 * ROWS :, :].astype(F32), axis=0, keepdims=True)
                v = recv[other, ROWS * (2 + g) : ROWS * (3 + g), :].astype(F32) + MID
                rows.append(v[at : at + 1] * m[:, at : at + 1])
        ends[k] = jnp.concatenate(rows, axis=0)
    for i in range(8):
        row = jnp.zeros((TAIL, LANES), F32)
        for j in range(4):
            row += pltpu.roll(recv[4 * i + j, 4 * ROWS :, :].astype(F32), ROWS * j, 1)
        metric[:, i * LANES : (i + 1) * LANES] = jnp.sum(row, axis=0, keepdims=True)
    for k, ref in enumerate((bf, hf)):
        for i in range(CHUNKS):
            for g in range(2):
                tile = recv[4 * i : 4 * i + 4, ROWS * (2 * k + g) : ROWS * (2 * k + g + 1), :]
                tile = tile.astype(F32).reshape(LANES, LANES).T
                if k:
                    tile = 0.5 * tile + 0.5 * MID
                for p in range(8):
                    ref[line_rows(i, 8 * g + turned(p)), :] = tile[BX * p : BX * (p + 1)]
    for i in range(CHUNKS):
        lanes = slice(i * LANES, (i + 1) * LANES)
        b0[:, lanes] = bf[pl.ds(ROW_COUNT * i + FIRST, BUSY), :].astype(BF16)
        for n, rows in enumerate(edge_rows(i)):
            edges[n][:BX, lanes] = bf[rows, :].astype(BF16)
            edges[n][BX:, lanes] = (2.0 * hf[rows, :] - MID).astype(BF16)
    mirror(hf)


def line_rows(i, s):
    return pl.ds(ROW_COUNT * i + FIRST + LP * s, BX)


def edge_rows(i):
    base = ROW_COUNT * i + FIRST
    return (
        line_rows(i, 0),
        line_rows(i, BS - 1),
        pl.ds(base, BS, stride=LP),
        pl.ds(base + BX - 1, BS, stride=LP),
    )


def near_rows(i):
    base = ROW_COUNT * i + FIRST
    return (
        line_rows(i, -1),
        line_rows(i, BS),
        pl.ds(base - 1, BS, stride=LP),
        pl.ds(base + BX, BS, stride=LP),
    )


def mirror(field):
    for i in range(CHUNKS):
        for near, edge in zip(near_rows(i), edge_rows(i)):
            field[near, :] = field[edge, :]


def busy(i):
    return pl.ds(ROW_COUNT * i + FIRST, BUSY)


def apply_lines(rows, line):
    return lax.dot_general(rows, line, (((1,), (1,)), ((), ())), preferred_element_type=F32)


def first_lines(b0, bf, hf, metric, line, x1, fw, resid):
    y = WEIGHTS[0][1] * apply_lines(b0[...], line[...])
    for i in range(CHUNKS):
        x1[busy(i), :] = y[:, i * LANES : (i + 1) * LANES]
    mirror(x1)
    last = lax.broadcasted_iota(jnp.int32, (RUN, LANES), 1) == LANES - 1

    def one(c, _):
        after = jnp.zeros((RUN, LANES), F32)
        for i in reversed(range(CHUNKS)):
            rows = pl.ds(ROW_COUNT * i + FIRST + RUN * c, RUN)
            half = hf[rows, :] * metric[:, i * LANES : (i + 1) * LANES]
            moved = pltpu.roll(half, LANES - 1, 1)
            fw[rows, :] = half + jnp.where(last, after, moved)
            after = moved
        return 0

    lax.fori_loop(0, BUSY // RUN, one, 0)
    line_resid(bf, x1, hf, fw, metric, resid)


def line_resid(bf, xe, he, fw, metric, out):
    lane = lax.broadcasted_iota(jnp.int32, (RUN, LANES), 1)
    last, first = lane == LANES - 1, lane == 0

    def one(c, _):
        def load(ref, i, shift=0):
            return ref[pl.ds(ROW_COUNT * i + FIRST + shift + RUN * c, RUN), :]

        xc = load(xe, 0)
        moved_x = pltpu.roll(xc, LANES - 1, 1)
        entry = load(he, 0) * metric[:, :LANES] * -xc
        for i in range(CHUNKS):
            if i + 1 < CHUNKS:
                after = load(xe, i + 1)
                moved_after = pltpu.roll(after, LANES - 1, 1)
            else:
                after = moved_after = jnp.zeros((RUN, LANES), F32)
            above = load(fw, i) * (xc - jnp.where(last, moved_after, moved_x))
            below = pltpu.roll(above, 1, 1)
            hc = load(he, i)
            total = above - jnp.where(first, entry, below)
            for shift in (-LP, -1, 1, LP):
                total += (hc + load(he, i, shift)) * (xc - load(xe, i, shift))
            out[pl.ds(ROW_COUNT * i + FIRST + RUN * c, RUN), :] = load(bf, i) - (xc + total)
            xc, moved_x, entry = after, moved_after, below
        return 0

    lax.fori_loop(0, BUSY // RUN, one, 0)


def finish_resid(resid, x, hf, near, x_near, out, rounded):
    for i in range(CHUNKS):
        lanes = slice(i * LANES, (i + 1) * LANES)
        out[busy(i), :] = resid[busy(i), :]
        for k, rows in enumerate(edge_rows(i)):
            weight = hf[rows, :] + 0.5 * near[k][BX:, lanes].astype(F32) + 0.5 * MID
            out[rows, :] = out[rows, :] - weight * (x[rows, :] - x_near(k, i))
        rounded[:, lanes] = out[busy(i), :].astype(BF16)


def second_step(resid, x1, hf, su, sd, xl, xr, line, x2, d2, e0, e1, e2, e3, full, rt, ends):
    near = (su, sd, xl, xr)
    for k, ref in enumerate(near):
        ends[k * BX : (k + 1) * BX] = ref[0:BX]
    ends1 = WEIGHTS[0][1] * apply_lines(ends[...], line[...])

    def x_near(k, i):
        return ends1[k * BX : (k + 1) * BX, i * LANES : (i + 1) * LANES]

    finish_resid(resid, x1, hf, near, x_near, full, rt)
    keep, scale = WEIGHTS[1]
    y = scale * apply_lines(rt[...], line[...])
    for i in range(CHUNKS):
        lanes = slice(i * LANES, (i + 1) * LANES)
        x = x1[busy(i), :]
        d = keep * x + y[:, lanes]
        d2[busy(i), :] = d
        x2[busy(i), :] = x + d
        for rows, ref in zip(edge_rows(i), (e0, e1, e2, e3)):
            ref[:, lanes] = x2[rows, :].astype(BF16)
    mirror(x2)


def third_step(
    resid, x2, d2, hf, su, sd, xl, xr, vsu, vsd, vxl, vxr, line, ends, send, xe, rt
):
    x_edges = (su, sd, xl, xr)

    def x_near(k, i):
        return x_edges[k][:, i * LANES : (i + 1) * LANES].astype(F32)

    finish_resid(resid, x2, hf, (vsu, vsd, vxl, vxr), x_near, xe, rt)
    keep, scale = WEIGHTS[2]
    y = scale * apply_lines(rt[...], line[...])
    count = WY * WZ
    nothing = jnp.zeros((1, LANES), F32)
    firsts, lasts = {}, {}
    for i in range(CHUNKS):
        xe[busy(i), :] = x2[busy(i), :] + keep * d2[busy(i), :] + y[:, i * LANES : (i + 1) * LANES]
        for j in range(2):
            tile = jnp.concatenate([xe[line_rows(i, 8 * j + turned(p)), :] for p in range(8)], axis=0).T
            for k in range(4):
                part = tile[ROWS * k : ROWS * (k + 1)]
                send[4 * i + k, ROWS * j : ROWS * (j + 1), :] = part.astype(BF16)
                firsts[4 * i + k, j] = part[:1]
                lasts[4 * i + k, j] = part[ROWS - 1 :]
    for k in range(count):
        rows = []
        for j in range(2):
            rows += [lasts.get((k - 1, j), nothing), firsts.get((k + 1, j), nothing)]
            rows.append(ends[k, 2 * j : 2 * j + 2, :])
        send[k, 2 * ROWS :, :] = jnp.concatenate(rows, axis=0).astype(BF16)


def block_row(w, s=0):
    return CP * (w + 1) + 1 + s


def block_span(s):
    return pl.ds(block_row(0, s), ROWS, stride=CP)


def unpack(recv, ves, vdl, vdr, xf, kappas, es, dl, dr, cl, cr):
    def one(t, _):
        for g in range(2):
            rows = slice(ROWS * g, ROWS * (g + 1))
            parts = [recv[owner(t, z), rows, :] for z in range(WZ)]
            cl[2 * t + g] = parts[0]
            cr[2 * t + g] = parts[7]
            parts = from_blocks(parts)
            for i in range(8):
                s = 16 * t + 8 * g + i
                xf[pl.ds(block_row(0) + s, ROWS, stride=CP), :] = parts[i].astype(F32)
        parts = from_blocks([recv[owner(t, z), 2 * ROWS :, :].astype(F32) for z in range(WZ)])
        for g in range(2):
            for i in range(8):
                s = 16 * t + 8 * g + i
                for k, (ref, row) in enumerate(
                    ((xf, block_row(-1)), (xf, block_row(ROWS)), (kappas, 0), (kappas, SPAN))
                ):
                    ref[pl.ds(row + s, 1), :] = parts[i][4 * g + k : 4 * g + k + 1]
        return 0

    lax.fori_loop(0, WY, one, 0)
    for k, (s, beside) in enumerate(((0, -1), (SPAN - 1, SPAN))):
        edge = xf[block_span(s), :]
        xf[block_span(beside), :] = edge
        es[k] = edge.astype(BF16)
    es[2] = ves[0]
    es[3] = ves[1]
    dl[...] = edge_lanes(cl[...], 0, 0, 0) + vdl[...]
    dr[...] = edge_lanes(cr[...], BX - 1, 1, 0) + vdr[...]


def weights(v_ref, m_ref, hf, gx, gk):
    def four(n, below):
        for k in range(4):
            w = 4 * n + k
            half = 0.5 * v_ref[w]
            hf[pl.ds(block_row(w), SPAN), :] = half
            cells = pl.ds(pl.multiple_of(SPAN * w, SPAN), SPAN)
            gx[cells, :] = half + pltpu.roll(half, LANES - 1, 1)
            half = m_ref[w] * half
            gk[cells, :] = below + half
            below = half
        return below

    gk[SPAN * ROWS :, :] = lax.fori_loop(0, ROWS // 4, four, jnp.zeros((SPAN, LANES), F32))
    for s in (-1, SPAN):
        hf[block_span(s), :] = jnp.zeros((ROWS, LANES), F32)


def inner_resid(xf, hf, gx, gk, kappas, b_ref, x3, resid, x_buf, sems):
    lane = lax.broadcasted_iota(jnp.int32, (ROWS, LANES), 1)
    halves = (0, ROWS)

    def load(ref, w, s):
        return ref[pl.ds(block_row(w, s), ROWS), :]

    def result(n):
        rows = pl.ds(4 * n, 4)
        return pltpu.make_async_copy(x_buf.at[rows], x3.at[rows], sems.at[n])

    def four(q, carry):
        carry = list(carry)
        for n in range(4):
            w = 4 * q + n
            top = jnp.where(w == ROWS - 1, 0.5, 0.0)
            for h, s in enumerate(halves):
                xc, hc = load(xf, w, s), load(hf, w, s)
                x_buf[w, s : s + ROWS, :] = xc
                weight = gk[pl.ds(SPAN * (w + 1) + s, ROWS), :] + top * kappas[SPAN + s : SPAN + s + ROWS, :]
                above = weight * (xc - load(xf, w + 1, s))
                total = above - carry[h]
                carry[h] = above
                for d in (-1, 1):
                    total += (hc + load(hf, w, s + d)) * (xc - load(xf, w, s + d))
                right = gx[pl.ds(SPAN * w + s, ROWS), :] * (xc - pltpu.roll(xc, LANES - 1, 1))
                right = jnp.where(lane == LANES - 1, 0.0, right)
                total += right - pltpu.roll(right, 1, 1)
                resid[w, s : s + ROWS, :] = b_ref[w, s : s + ROWS, :] - (xc + total)
        result(q).start()
        return tuple(carry)

    start = []
    for s in halves:
        weight = gk[s : s + ROWS, :] + 0.5 * kappas[s : s + ROWS, :]
        start.append(weight * (load(xf, -1, s) - load(xf, 0, s)))
    lax.fori_loop(0, ROWS // 4, four, tuple(start))
    for q in range(ROWS // 4):
        result(q).wait()


def last_resid(resid, xf, hf, spans, lefts, rights, dl, dr, out, side_rows, r_buf, sems):
    for k, s in enumerate((0, SPAN - 1)):
        weight = hf[block_span(s), :] + 0.5 * spans[3 - k].astype(F32) + 0.5 * MID
        side_rows[k] = weight * (xf[block_span(s), :] - spans[1 - k].astype(F32))
    at = lax.broadcasted_iota(jnp.int32, (2 * ROWS, LANES), 0)
    to = lax.broadcasted_iota(jnp.int32, (2 * ROWS, LANES), 1)
    place = jnp.where(to == 2 * (at % ROWS) + at // ROWS, 1.0, 0.0).astype(BF16)

    def placed(right, left):
        both = jnp.concatenate([right[...], left[...]], axis=0)
        return lax.dot_general(both, place, (((0,), (0,)), ((), ())), preferred_element_type=F32)

    own, near = placed(dr, dl), placed(rights, lefts)
    sides = (0.5 * (own[SPAN:] + near[SPAN:]) + MID) * (own[:SPAN] - near[:SPAN])
    lane = lax.broadcasted_iota(jnp.int32, (SPAN, LANES), 1)
    ends = (lane == 0) | (lane == LANES - 1)
    row = lax.broadcasted_iota(jnp.int32, (8, LANES), 0)

    def results(q):
        rows = pl.ds(4 * q, 4)
        return pltpu.make_async_copy(r_buf.at[rows], out.at[rows], sems.at[q])

    def four(q, carry):
        for n in range(4):
            w = 4 * q + n
            r = resid[w] - jnp.where(ends, pltpu.roll(sides, LANES - 1 - 2 * w, 1), 0.0)
            r_buf[w, 8 : SPAN - 8, :] = r[8 : SPAN - 8]
            for k, s in enumerate((0, SPAN - 8)):
                flux = side_rows[k, pl.ds(w, 1), :]
                r_buf[w, s : s + 8, :] = r[s : s + 8] - jnp.where(row == 7 * k, flux, 0.0)
        results(q).start()
        return carry

    lax.fori_loop(0, ROWS // 4, four, 0)
    for q in range(ROWS // 4):
        results(q).wait()


def block_edges(es, dl, dr):
    streams = lax.axis_size("stream")
    right = [(i, (i + 1) % streams) for i in range(streams)]
    left = [((i + 1) % streams, i) for i in range(streams)]
    return (
        lax.ppermute(es, "span", [(0, 1), (1, 0)]),
        lax.ppermute(dr, "stream", right),
        lax.ppermute(dl, "stream", left),
    )


def line_shift(value, ds, dx):
    spans, streams = lax.axis_size("span"), lax.axis_size("stream")

    def device(sb, xb):
        sp, y = divmod(sb % (spans * WY), WY)
        st, z = divmod(xb % (streams * WZ), WZ)
        y, z = (WY - 1 - y if sp % 2 else y), (WZ - 1 - z if st % 2 else z)
        return ((y * WZ + z) * spans + sp) * streams + st

    pairs = [
        (device(sb, xb), device(sb + ds, xb + dx))
        for sb in range(spans * WY)
        for xb in range(streams * WZ)
    ]
    return lax.ppermute(value, ("wall", "span", "stream"), pairs)


def line_edges(*edges):
    return (
        line_shift(edges[1], 1, 0),
        line_shift(edges[0], -1, 0),
        line_shift(edges[3], 0, 1),
        line_shift(edges[2], 0, -1),
    )


def body(right_side, viscosity, wall_metric, line_inverse):
    block = pltpu.VMEM((ROWS, SPAN, LANES), F32)
    side = pltpu.VMEM((8, ROWS, LANES), BF16)
    dense = shape((ROWS, LANES), BF16)
    hbm, vmem = pl.BlockSpec(memory_space=pltpu.HBM), pl.BlockSpec(memory_space=pltpu.VMEM)
    sent = (WY * WZ, 4 * ROWS + TAIL, LANES)
    loose = pltpu.VMEM(((SPAN + 1) * ROWS, LANES), F32)
    dma = pltpu.SemaphoreType.DMA
    send, *v_edges = call(
        pack,
        (shape(sent, BF16), shape((2, ROWS, LANES), BF16), dense, dense),
        (
            loose,
            loose,
            pltpu.VMEM((1, ROWS), F32),
            pltpu.VMEM(sent, BF16),
            pltpu.VMEM((2, ROWS, LANES), BF16),
            pltpu.VMEM((ROWS, LANES), BF16),
            pltpu.VMEM((ROWS, LANES), BF16),
            side,
            side,
            dma((2, ROWS)),
            dma((WY,)),
            dma((4,)),
        ),
        62 * MIB + MIB // 2,
        in_specs=(hbm,) * 3,
        out_specs=(hbm,) * 4,
    )(right_side, viscosity, wall_metric.reshape(1, ROWS))
    recv = lax.all_to_all(send, "wall", 0, 0, tiled=True)
    field = shape((CHUNKS * ROW_COUNT, LANES), F32)
    bf, hf, b0, metric, ends, *edges = call(
        to_lines,
        (field, field, shape((BUSY, NW), BF16), shape((1, NW), F32))
        + (shape((WY * WZ, 4, LANES), F32),)
        + (shape((2 * BX, NW), BF16),) * 4,
    )(recv)
    near = line_edges(*edges)
    x1, fw, resid = call(first_lines, (field, field, field))(b0, bf, hf, metric, line_inverse)
    ext = pltpu.VMEM((CHUNKS * ROW_COUNT, LANES), F32)
    rounded = pltpu.VMEM((BUSY, NW), BF16)
    x2, d2, *edges = call(
        second_step,
        (field, field) + (shape((BX, NW), BF16),) * 4,
        (ext, rounded, pltpu.VMEM((4 * BX, NW), BF16)),
    )(resid, x1, hf, *near, line_inverse)
    x_near = line_edges(*edges)
    resid = call(line_resid, field)(bf, x2, hf, fw, metric)
    v, m, _ = lax.optimization_barrier((viscosity, wall_metric, d2))
    smem = pl.BlockSpec(memory_space=pltpu.SMEM)
    cells = shape((BLOCK_ROWS, LANES), F32)
    face_weights = call(
        weights,
        (cells, shape((ROWS * SPAN, LANES), F32), shape(((ROWS + 1) * SPAN, LANES), F32)),
        in_specs=(vmem, smem),
    )(v, m)
    face_weights, resid = lax.optimization_barrier((face_weights, resid))
    send = call(
        third_step, shape((WY * WZ, 2 * ROWS + TAIL, LANES), BF16), (ext, rounded)
    )(resid, x2, d2, hf, *x_near, *near, line_inverse, ends)
    recv = lax.all_to_all(send, "wall", 0, 0, tiled=True)
    xf, kappas, *edges = call(
        unpack,
        (cells, shape((2 * SPAN, LANES), F32), shape((4, ROWS, LANES), BF16), dense, dense),
        (side, side),
    )(recv, *v_edges)
    x_edges = block_edges(*edges)
    whole = shape(right_side.shape, F32)
    x3, resid = call(
        inner_resid, (whole, whole), (block, dma((ROWS // 4,))), out_specs=(hbm, vmem)
    )(xf, *face_weights, kappas, right_side)
    residual = call(
        last_resid,
        whole,
        (pltpu.VMEM((2, ROWS, LANES), F32), block, dma((ROWS // 4,))),
        out_specs=hbm,
    )(resid, xf, face_weights[0], *x_edges, *edges[1:])
    return x3, residual


def solution(mesh):
    in_specs = (P("wall", "span", "stream"), P("wall", "span", "stream"), P("wall"), P())
    out_specs = (P("wall", "span", "stream"), P("wall", "span", "stream"))
    return jax.shard_map(body, mesh=mesh, in_specs=in_specs, out_specs=out_specs, check_vma=False)
```

```python
import functools

import jax
import jax.numpy as jnp
from jax import lax
from jax.experimental import pallas as pl
from jax.experimental.pallas import tpu as pltpu
from jax.sharding import PartitionSpec as P

STEPS = 3
NW, WY, WZ = 1024, 4, 8
ROWS, SPAN, LANES = 32, 64, 128
BS, BX = 16, 16
CELLS = BS * BX
CHUNKS = NW // 128
LP, FIRST, BUSY, ROW_COUNT = BX + 2, 24, 288, 336
RUN = 48
CP = SPAN + 3
BLOCK_ROWS = 2280
TAIL = 8
MID = 0.5
F32, BF16 = jnp.float32, jnp.bfloat16
MIB = 1024 * 1024


def chebyshev_weights(steps):
    lowest = 0.25
    highest = 2.5
    center = 0.5 * (highest + lowest)
    half = 0.5 * (highest - lowest)
    ratio = center / half
    weights = [(0.0, 1.0 / center)]
    rho_old = 1.0 / ratio
    for step in range(1, steps):
        rho_new = 1.0 / (2.0 * ratio - rho_old)
        weights.append((rho_new * rho_old, 2.0 * rho_new / half))
        rho_old = rho_new
    return weights


WEIGHTS = chebyshev_weights(STEPS)


def shape(dims, dtype):
    return jax.ShapeDtypeStruct(dims, dtype)


def call(kernel, outs, scratch=(), limit=40 * MIB, **specs):
    return pl.pallas_call(
        kernel,
        out_shape=outs,
        scratch_shapes=list(scratch),
        compiler_params=pltpu.CompilerParams(vmem_limit_bytes=limit),
        cost_estimate=pl.CostEstimate(flops=10**7, bytes_accessed=4 * 10**6, transcendentals=0),
        **specs,
    )


def skew(arrays):
    block = lax.broadcasted_iota(jnp.int32, arrays[0].shape, 1) // BX
    arrays = list(arrays)
    for bit in range(3):
        step = 1 << bit
        upper = (block // step) % 2 == 1
        arrays = [jnp.where(upper, arrays[(j + step) % 8], arrays[j]) for j in range(8)]
    return [arrays[-z % 8] for z in range(8)]


def to_blocks(rows):
    return skew([pltpu.roll(row, BX * i, 1) if i else row for i, row in enumerate(rows)])


def from_blocks(blocks):
    return [pltpu.roll(row, LANES - BX * i, 1) if i else row for i, row in enumerate(skew(blocks))]


def turned(p):
    z, odd = lax.axis_index("wall") % WZ, lax.axis_index("stream") % 2
    return (p - (z + odd * (WZ - 1 - 2 * z)) + WZ) % WZ


def owner(t, z):
    span, odd = lax.axis_index("span"), lax.axis_index("stream") % 2
    return WZ * (t + span * (WY - 1 - 2 * t)) + z + odd * (WZ - 1 - 2 * z)


def strided(s):
    return pl.ds(s, ROWS, stride=SPAN)


def edge_lanes(blocks, pick, turn, offset):
    at = lax.broadcasted_iota(jnp.int32, (LANES, LANES), 0)
    to = lax.broadcasted_iota(jnp.int32, (LANES, LANES), 1)
    one = jnp.where((at % BX == pick) & (to == (at // BX + turn) % 8), 1.0, 0.0).astype(BF16)
    eights = jnp.dot(blocks.reshape(8 * ROWS, LANES), one, preferred_element_type=F32)
    out = jnp.zeros((ROWS, LANES), F32)
    for q in range(8):
        out += pltpu.roll(eights[ROWS * q : ROWS * (q + 1)], (8 * q + offset) % LANES, 1)
    return out.astype(BF16)


def pack(
    b_hbm, v_hbm, m_hbm, send_hbm, es_hbm, dl_hbm, dr_hbm, b_buf, v_buf, m_buf, send, es, dl, dr, cl, cr,
    sems, done, small,
):
    def copy(k, t):
        src, dst = ((v_hbm, v_buf), (b_hbm, b_buf))[k]
        rows = pl.ds(BS * t, BS)
        return pltpu.make_async_copy(src.at[:, rows, :], dst.at[:, rows, :], sems.at[k, t])

    def result(y):
        peers = pl.ds(WZ * y, WZ)
        return pltpu.make_async_copy(send.at[peers], send_hbm.at[peers], done.at[y])

    for k in range(2):
        for t in range(WY):
            copy(k, t).start()
    metric = pltpu.make_async_copy(m_hbm, m_buf, small.at[3])
    metric.start()
    edges = [
        pltpu.make_async_copy(src, dst, small.at[n])
        for n, (src, dst) in enumerate(((es, es_hbm), (dl, dl_hbm), (dr, dr_hbm)))
    ]

    def move(t, k, buf, mid):
        for g in range(2):
            parts = [buf[strided(16 * t + 8 * g + i), :] - mid for i in range(8)]
            parts = to_blocks([part.astype(BF16) for part in parts])
            rows = slice(ROWS * (2 * k + g), ROWS * (2 * k + g + 1))
            for z in range(WZ):
                send[owner(t, z), rows, :] = parts[z]
            if k:
                cl[2 * t + g] = parts[0]
                cr[2 * t + g] = parts[7]
        return 0

    v_flat, b_flat = (buf.reshape(ROWS * SPAN, LANES) for buf in (v_buf, b_buf))

    def first(t, _):
        copy(0, t).wait()
        move(t, 1, v_flat, MID)
        return 0

    lax.fori_loop(0, WY, first, 0)
    es[0] = (v_flat[strided(0), :] - MID).astype(BF16)
    es[1] = (v_flat[strided(SPAN - 1), :] - MID).astype(BF16)
    dl[...] = edge_lanes(cl[...], 0, 0, SPAN)
    dr[...] = edge_lanes(cr[...], BX - 1, 1, SPAN)
    for edge in edges:
        edge.start()
    metric.wait()
    rest = m_buf[...]
    parts = []
    for _ in range(3):
        part = rest.astype(BF16)
        rest = rest - part.astype(F32)
        parts.append(part.astype(F32))
    tail = jnp.concatenate(parts + [jnp.zeros((TAIL - 3, ROWS), F32)], axis=0)
    tail = jnp.concatenate([tail, jnp.zeros((TAIL, LANES - ROWS), F32)], axis=1).astype(BF16)
    for k in range(WY * WZ):
        send[k, 4 * ROWS :, :] = tail

    def last(t, _):
        copy(1, t).wait()
        move(t, 0, b_flat, 0.0)
        result(owner(t, 0) // WZ).start()
        return 0

    lax.fori_loop(0, WY, last, 0)
    for t in range(WY):
        result(t).wait()
    for edge in edges:
        edge.wait()


def to_lines(recv, bf, hf, b0, metric, ends, *edges):
    count = WY * WZ
    nothing = jnp.zeros((1, LANES), F32)
    for k in range(count):
        rows = []
        for g in range(2):
            for other, at in ((k - 1, ROWS - 1), (k + 1, 0)):
                if not 0 <= other < count:
                    rows.append(nothing)
                    continue
                m = jnp.sum(recv[other, 4 * ROWS :, :].astype(F32), axis=0, keepdims=True)
                v = recv[other, ROWS * (2 + g) : ROWS * (3 + g), :].astype(F32) + MID
                rows.append(v[at : at + 1] * m[:, at : at + 1])
        ends[k] = jnp.concatenate(rows, axis=0)
    for i in range(8):
        row = jnp.zeros((TAIL, LANES), F32)
        for j in range(4):
            row += pltpu.roll(recv[4 * i + j, 4 * ROWS :, :].astype(F32), ROWS * j, 1)
        metric[:, i * LANES : (i + 1) * LANES] = jnp.sum(row, axis=0, keepdims=True)
    for k, ref in enumerate((bf, hf)):
        for i in range(CHUNKS):
            for g in range(2):
                tile = recv[4 * i : 4 * i + 4, ROWS * (2 * k + g) : ROWS * (2 * k + g + 1), :]
                tile = tile.astype(F32).reshape(LANES, LANES).T
                if k:
                    tile = 0.5 * tile + 0.5 * MID
                for p in range(8):
                    ref[line_rows(i, 8 * g + turned(p)), :] = tile[BX * p : BX * (p + 1)]
    for i in range(CHUNKS):
        lanes = slice(i * LANES, (i + 1) * LANES)
        b0[:, lanes] = bf[pl.ds(ROW_COUNT * i + FIRST, BUSY), :].astype(BF16)
        for n, rows in enumerate(edge_rows(i)):
            edges[n][:BX, lanes] = bf[rows, :].astype(BF16)
            edges[n][BX:, lanes] = (2.0 * hf[rows, :] - MID).astype(BF16)
    mirror(hf)


def line_rows(i, s):
    return pl.ds(ROW_COUNT * i + FIRST + LP * s, BX)


def edge_rows(i):
    base = ROW_COUNT * i + FIRST
    return (
        line_rows(i, 0),
        line_rows(i, BS - 1),
        pl.ds(base, BS, stride=LP),
        pl.ds(base + BX - 1, BS, stride=LP),
    )


def near_rows(i):
    base = ROW_COUNT * i + FIRST
    return (
        line_rows(i, -1),
        line_rows(i, BS),
        pl.ds(base - 1, BS, stride=LP),
        pl.ds(base + BX, BS, stride=LP),
    )


def mirror(field):
    for i in range(CHUNKS):
        for near, edge in zip(near_rows(i), edge_rows(i)):
            field[near, :] = field[edge, :]


def busy(i):
    return pl.ds(ROW_COUNT * i + FIRST, BUSY)


def apply_lines(rows, line):
    return lax.dot_general(rows, line, (((1,), (1,)), ((), ())), preferred_element_type=F32)


def first_lines(b0, bf, hf, metric, line, x1, fw, resid):
    y = WEIGHTS[0][1] * apply_lines(b0[...], line[...])
    for i in range(CHUNKS):
        x1[busy(i), :] = y[:, i * LANES : (i + 1) * LANES]
    mirror(x1)
    line_resid(bf, x1, hf, fw, metric, resid, make_weights=True)


def line_resid(bf, xe, he, fw, metric, out, make_weights=False):
    lane = lax.broadcasted_iota(jnp.int32, (RUN, LANES), 1)
    last, first = lane == LANES - 1, lane == 0

    def one(c, _):
        def load(ref, i, shift=0):
            return ref[pl.ds(ROW_COUNT * i + FIRST + shift + RUN * c, RUN), :]

        xc = load(xe, 0)
        moved_x = pltpu.roll(xc, LANES - 1, 1)
        kappa = load(he, 0) * metric[:, :LANES]
        entry = kappa * -xc
        moved_k = pltpu.roll(kappa, LANES - 1, 1)
        for i in range(CHUNKS):
            if i + 1 < CHUNKS:
                after = load(xe, i + 1)
                moved_after = pltpu.roll(after, LANES - 1, 1)
                kappa_after = load(he, i + 1) * metric[:, (i + 1) * LANES : (i + 2) * LANES]
                moved_k_after = pltpu.roll(kappa_after, LANES - 1, 1)
            else:
                after = moved_after = jnp.zeros((RUN, LANES), F32)
                kappa_after = moved_k_after = after
            if make_weights:
                weight = kappa + jnp.where(last, moved_k_after, moved_k)
                fw[pl.ds(ROW_COUNT * i + FIRST + RUN * c, RUN), :] = weight
            else:
                weight = load(fw, i)
            above = weight * (xc - jnp.where(last, moved_after, moved_x))
            below = pltpu.roll(above, 1, 1)
            hc = load(he, i)
            total = above - jnp.where(first, entry, below)
            for shift in (-LP, -1, 1, LP):
                total += (hc + load(he, i, shift)) * (xc - load(xe, i, shift))
            out[pl.ds(ROW_COUNT * i + FIRST + RUN * c, RUN), :] = load(bf, i) - (xc + total)
            xc, moved_x, entry = after, moved_after, below
            kappa, moved_k = kappa_after, moved_k_after
        return 0

    lax.fori_loop(0, BUSY // RUN, one, 0)


def finish_resid(resid, x, hf, near, x_near, out, rounded):
    for i in range(CHUNKS):
        lanes = slice(i * LANES, (i + 1) * LANES)
        out[busy(i), :] = resid[busy(i), :]
        for k, rows in enumerate(edge_rows(i)):
            weight = hf[rows, :] + 0.5 * near[k][BX:, lanes].astype(F32) + 0.5 * MID
            out[rows, :] = out[rows, :] - weight * (x[rows, :] - x_near(k, i))
        rounded[:, lanes] = out[busy(i), :].astype(BF16)


def second_step(resid, x1, hf, su, sd, xl, xr, line, x2, d2, e0, e1, e2, e3, full, rt, ends):
    near = (su, sd, xl, xr)
    for k, ref in enumerate(near):
        ends[k * BX : (k + 1) * BX] = ref[0:BX]
    ends1 = WEIGHTS[0][1] * apply_lines(ends[...], line[...])

    def x_near(k, i):
        return ends1[k * BX : (k + 1) * BX, i * LANES : (i + 1) * LANES]

    finish_resid(resid, x1, hf, near, x_near, full, rt)
    keep, scale = WEIGHTS[1]
    y = scale * apply_lines(rt[...], line[...])
    for i in range(CHUNKS):
        lanes = slice(i * LANES, (i + 1) * LANES)
        x = x1[busy(i), :]
        d = keep * x + y[:, lanes]
        d2[busy(i), :] = d
        x2[busy(i), :] = x + d
        for rows, ref in zip(edge_rows(i), (e0, e1, e2, e3)):
            ref[:, lanes] = x2[rows, :].astype(BF16)
    mirror(x2)


def third_step(
    resid, x2, d2, hf, su, sd, xl, xr, vsu, vsd, vxl, vxr, line, ends, send, xe, rt
):
    x_edges = (su, sd, xl, xr)

    def x_near(k, i):
        return x_edges[k][:, i * LANES : (i + 1) * LANES].astype(F32)

    finish_resid(resid, x2, hf, (vsu, vsd, vxl, vxr), x_near, xe, rt)
    keep, scale = WEIGHTS[2]
    y = scale * apply_lines(rt[...], line[...])
    count = WY * WZ
    nothing = jnp.zeros((1, LANES), F32)
    firsts, lasts = {}, {}
    for i in range(CHUNKS):
        xe[busy(i), :] = x2[busy(i), :] + keep * d2[busy(i), :] + y[:, i * LANES : (i + 1) * LANES]
        for j in range(2):
            tile = jnp.concatenate([xe[line_rows(i, 8 * j + turned(p)), :] for p in range(8)], axis=0).T
            for k in range(4):
                part = tile[ROWS * k : ROWS * (k + 1)]
                send[4 * i + k, ROWS * j : ROWS * (j + 1), :] = part.astype(BF16)
                firsts[4 * i + k, j] = part[:1]
                lasts[4 * i + k, j] = part[ROWS - 1 :]
    for k in range(count):
        rows = []
        for j in range(2):
            rows += [lasts.get((k - 1, j), nothing), firsts.get((k + 1, j), nothing)]
            rows.append(ends[k, 2 * j : 2 * j + 2, :])
        send[k, 2 * ROWS :, :] = jnp.concatenate(rows, axis=0).astype(BF16)


def block_row(w, s=0):
    return CP * (w + 1) + 1 + s


def block_span(s):
    return pl.ds(block_row(0, s), ROWS, stride=CP)


def unpack(recv, ves, vdl, vdr, xf, es, dl, dr, cl, cr):
    def one(t, _):
        for g in range(2):
            rows = slice(ROWS * g, ROWS * (g + 1))
            parts = [recv[owner(t, z), rows, :] for z in range(WZ)]
            cl[2 * t + g] = parts[0]
            cr[2 * t + g] = parts[7]
            parts = from_blocks(parts)
            for i in range(8):
                s = 16 * t + 8 * g + i
                xf[pl.ds(block_row(0) + s, ROWS, stride=CP), :] = parts[i].astype(F32)
        return 0

    lax.fori_loop(0, WY, one, 0)
    for k, (s, beside) in enumerate(((0, -1), (SPAN - 1, SPAN))):
        edge = xf[block_span(s), :]
        xf[block_span(beside), :] = edge
        es[k] = edge.astype(BF16)
    for w, beside in ((0, -1), (ROWS - 1, ROWS)):
        xf[pl.ds(block_row(beside), SPAN), :] = xf[pl.ds(block_row(w), SPAN), :]
    es[2] = ves[0]
    es[3] = ves[1]
    dl[...] = edge_lanes(cl[...], 0, 0, 0) + vdl[...]
    dr[...] = edge_lanes(cr[...], BX - 1, 1, 0) + vdr[...]


def weights(v_ref, m_ref, hf, gx, gk):
    def four(n, below):
        for k in range(4):
            w = 4 * n + k
            half = 0.5 * v_ref[w]
            hf[pl.ds(block_row(w), SPAN), :] = half
            cells = pl.ds(pl.multiple_of(SPAN * w, SPAN), SPAN)
            gx[cells, :] = half + pltpu.roll(half, LANES - 1, 1)
            half = m_ref[w] * half
            gk[cells, :] = below + half
            below = half
        return below

    gk[SPAN * ROWS :, :] = lax.fori_loop(0, ROWS // 4, four, jnp.zeros((SPAN, LANES), F32))
    for s in (-1, SPAN):
        hf[block_span(s), :] = jnp.zeros((ROWS, LANES), F32)


def placed(right, left):
    at = lax.broadcasted_iota(jnp.int32, (2 * ROWS, LANES), 0)
    to = lax.broadcasted_iota(jnp.int32, (2 * ROWS, LANES), 1)
    place = jnp.where(to == 2 * (at % ROWS) + at // ROWS, 1.0, 0.0).astype(BF16)
    both = jnp.concatenate([right[...], left[...]], axis=0)
    return lax.dot_general(both, place, (((0,), (0,)), ((), ())), preferred_element_type=F32)


def inner_resid(xf, hf, gx, gk, recv, b_ref, dl, dr, x3, resid, own, x_buf, beyond, sems):
    lane = lax.broadcasted_iota(jnp.int32, (ROWS, LANES), 1)
    halves = (0, ROWS)

    def load(ref, w, s):
        return ref[pl.ds(block_row(w, s), ROWS), :]

    def result(n):
        rows = pl.ds(4 * n, 4)
        return pltpu.make_async_copy(x_buf.at[rows], x3.at[rows], sems.at[n])

    def four(q, carry):
        carry = list(carry)
        for n in range(4):
            w = 4 * q + n
            for h, s in enumerate(halves):
                xc, hc = load(xf, w, s), load(hf, w, s)
                x_buf[w, s : s + ROWS, :] = xc
                above = gk[pl.ds(SPAN * (w + 1) + s, ROWS), :] * (xc - load(xf, w + 1, s))
                total = above - carry[h]
                carry[h] = above
                for d in (-1, 1):
                    total += (hc + load(hf, w, s + d)) * (xc - load(xf, w, s + d))
                right = gx[pl.ds(SPAN * w + s, ROWS), :] * (xc - pltpu.roll(xc, LANES - 1, 1))
                right = jnp.where(lane == LANES - 1, 0.0, right)
                total += right - pltpu.roll(right, 1, 1)
                resid[w, s : s + ROWS, :] = b_ref[w, s : s + ROWS, :] - (xc + total)
        result(q).start()
        return tuple(carry)

    zero = jnp.zeros((ROWS, LANES), F32)
    lax.fori_loop(0, ROWS // 4, four, (zero, zero))

    def tail(t, _):
        parts = from_blocks([recv[owner(t, z), 2 * ROWS :, :].astype(F32) for z in range(WZ)])
        for g in range(2):
            for i in range(8):
                for k in range(4):
                    row = pl.ds(SPAN * k + 16 * t + 8 * g + i, 1)
                    beyond[row, :] = parts[i][4 * g + k : 4 * g + k + 1]
        return 0

    lax.fori_loop(0, WY, tail, 0)
    for k, w in enumerate((0, ROWS - 1)):
        face = gk[SPAN * ROWS * k : SPAN * (ROWS * k + 1), :]
        weight = face + 0.5 * beyond[SPAN * (2 + k) : SPAN * (3 + k), :]
        x = xf[pl.ds(block_row(w), SPAN), :]
        resid[w] = resid[w] - weight * (x - beyond[SPAN * k : SPAN * (k + 1), :])
    own[...] = placed(dr, dl)
    for q in range(ROWS // 4):
        result(q).wait()


def last_resid(resid, xf, hf, own, spans, lefts, rights, out, side_rows, r_buf, sems):
    for k, s in enumerate((0, SPAN - 1)):
        weight = hf[block_span(s), :] + 0.5 * spans[3 - k].astype(F32) + 0.5 * MID
        side_rows[k] = weight * (xf[block_span(s), :] - spans[1 - k].astype(F32))
    near = placed(rights, lefts)
    sides = (0.5 * (own[SPAN:] + near[SPAN:]) + MID) * (own[:SPAN] - near[:SPAN])
    lane = lax.broadcasted_iota(jnp.int32, (SPAN, LANES), 1)
    ends = (lane == 0) | (lane == LANES - 1)
    row = lax.broadcasted_iota(jnp.int32, (8, LANES), 0)

    def results(q):
        rows = pl.ds(4 * q, 4)
        return pltpu.make_async_copy(r_buf.at[rows], out.at[rows], sems.at[q])

    def four(q, carry):
        for n in range(4):
            w = 4 * q + n
            r = resid[w] - jnp.where(ends, pltpu.roll(sides, LANES - 1 - 2 * w, 1), 0.0)
            r_buf[w, 8 : SPAN - 8, :] = r[8 : SPAN - 8]
            for k, s in enumerate((0, SPAN - 8)):
                flux = side_rows[k, pl.ds(w, 1), :]
                r_buf[w, s : s + 8, :] = r[s : s + 8] - jnp.where(row == 7 * k, flux, 0.0)
        results(q).start()
        return carry

    lax.fori_loop(0, ROWS // 4, four, 0)
    for q in range(ROWS // 4):
        results(q).wait()


def block_edges(es, dl, dr):
    streams = lax.axis_size("stream")
    right = [(i, (i + 1) % streams) for i in range(streams)]
    left = [((i + 1) % streams, i) for i in range(streams)]
    return (
        lax.ppermute(es, "span", [(0, 1), (1, 0)]),
        lax.ppermute(dr, "stream", right),
        lax.ppermute(dl, "stream", left),
    )


def line_shift(value, ds, dx):
    spans, streams = lax.axis_size("span"), lax.axis_size("stream")

    def device(sb, xb):
        sp, y = divmod(sb % (spans * WY), WY)
        st, z = divmod(xb % (streams * WZ), WZ)
        y, z = (WY - 1 - y if sp % 2 else y), (WZ - 1 - z if st % 2 else z)
        return ((y * WZ + z) * spans + sp) * streams + st

    pairs = [
        (device(sb, xb), device(sb + ds, xb + dx))
        for sb in range(spans * WY)
        for xb in range(streams * WZ)
    ]
    return lax.ppermute(value, ("wall", "span", "stream"), pairs)


def line_edges(*edges):
    return (
        line_shift(edges[1], 1, 0),
        line_shift(edges[0], -1, 0),
        line_shift(edges[3], 0, 1),
        line_shift(edges[2], 0, -1),
    )


def body(right_side, viscosity, wall_metric, line_inverse):
    block = pltpu.VMEM((ROWS, SPAN, LANES), F32)
    side = pltpu.VMEM((8, ROWS, LANES), BF16)
    dense = shape((ROWS, LANES), BF16)
    hbm, vmem = pl.BlockSpec(memory_space=pltpu.HBM), pl.BlockSpec(memory_space=pltpu.VMEM)
    sent = (WY * WZ, 4 * ROWS + TAIL, LANES)
    dma = pltpu.SemaphoreType.DMA
    send, *v_edges = call(
        pack,
        (shape(sent, BF16), shape((2, ROWS, LANES), BF16), dense, dense),
        (
            block,
            block,
            pltpu.VMEM((1, ROWS), F32),
            pltpu.VMEM(sent, BF16),
            pltpu.VMEM((2, ROWS, LANES), BF16),
            pltpu.VMEM((ROWS, LANES), BF16),
            pltpu.VMEM((ROWS, LANES), BF16),
            side,
            side,
            dma((2, WY)),
            dma((WY,)),
            dma((4,)),
        ),
        62 * MIB + MIB // 2,
        in_specs=(hbm,) * 3,
        out_specs=(hbm,) * 4,
    )(right_side, viscosity, wall_metric.reshape(1, ROWS))
    recv = lax.all_to_all(send, "wall", 0, 0, tiled=True)
    field = shape((CHUNKS * ROW_COUNT, LANES), F32)
    bf, hf, b0, metric, ends, *edges = call(
        to_lines,
        (field, field, shape((BUSY, NW), BF16), shape((1, NW), F32))
        + (shape((WY * WZ, 4, LANES), F32),)
        + (shape((2 * BX, NW), BF16),) * 4,
    )(recv)
    near = line_edges(*edges)
    x1, fw, resid = call(first_lines, (field, field, field))(b0, bf, hf, metric, line_inverse)
    ext = pltpu.VMEM((CHUNKS * ROW_COUNT, LANES), F32)
    rounded = pltpu.VMEM((BUSY, NW), BF16)
    x2, d2, *edges = call(
        second_step,
        (field, field) + (shape((BX, NW), BF16),) * 4,
        (ext, rounded, pltpu.VMEM((4 * BX, NW), BF16)),
    )(resid, x1, hf, *near, line_inverse)
    x_near = line_edges(*edges)
    resid = call(line_resid, field)(bf, x2, hf, fw, metric)
    v, m, _ = lax.optimization_barrier((viscosity, wall_metric, d2))
    smem = pl.BlockSpec(memory_space=pltpu.SMEM)
    cells = shape((BLOCK_ROWS, LANES), F32)
    face_weights = call(
        weights,
        (cells, shape((ROWS * SPAN, LANES), F32), shape(((ROWS + 1) * SPAN, LANES), F32)),
        in_specs=(vmem, smem),
    )(v, m)
    face_weights, resid = lax.optimization_barrier((face_weights, resid))
    send = call(
        third_step, shape((WY * WZ, 2 * ROWS + TAIL, LANES), BF16), (ext, rounded)
    )(resid, x2, d2, hf, *x_near, *near, line_inverse, ends)
    recv = lax.all_to_all(send, "wall", 0, 0, tiled=True)
    xf, *edges = call(
        unpack,
        (cells, shape((4, ROWS, LANES), BF16), dense, dense),
        (side, side),
    )(recv, *v_edges)
    x_edges = block_edges(*edges)
    whole = shape(right_side.shape, F32)
    x3, resid, own = call(
        inner_resid,
        (whole, whole, shape((LANES, LANES), F32)),
        (block, pltpu.VMEM((4 * SPAN, LANES), F32), dma((ROWS // 4,))),
        out_specs=(hbm, vmem, vmem),
    )(xf, *face_weights, recv, right_side, *edges[1:])
    residual = call(
        last_resid,
        whole,
        (pltpu.VMEM((2, ROWS, LANES), F32), block, dma((ROWS // 4,))),
        out_specs=hbm,
    )(resid, xf, face_weights[0], own, *x_edges)
    return x3, residual


def solution(mesh):
    in_specs = (P("wall", "span", "stream"), P("wall", "span", "stream"), P("wall"), P())
    out_specs = (P("wall", "span", "stream"), P("wall", "span", "stream"))
    return jax.shard_map(body, mesh=mesh, in_specs=in_specs, out_specs=out_specs, check_vma=False)
```

```python
import functools

import jax
import jax.numpy as jnp
from jax import lax
from jax.experimental import pallas as pl
from jax.experimental.pallas import tpu as pltpu
from jax.sharding import PartitionSpec as P

STEPS = 3
NW, WY, WZ = 1024, 4, 8
ROWS, SPAN, LANES = 32, 64, 128
BS, BX = 16, 16
CELLS = BS * BX
CHUNKS = NW // 128
LP, FIRST, BUSY, ROW_COUNT = BX + 2, 24, 288, 336
RUN = 48
CP = SPAN + 3
BLOCK_ROWS = 2280
TAIL = 8
MID = 0.5
F32, BF16 = jnp.float32, jnp.bfloat16
MIB = 1024 * 1024


def chebyshev_weights(steps):
    lowest = 0.25
    highest = 2.5
    center = 0.5 * (highest + lowest)
    half = 0.5 * (highest - lowest)
    ratio = center / half
    weights = [(0.0, 1.0 / center)]
    rho_old = 1.0 / ratio
    for step in range(1, steps):
        rho_new = 1.0 / (2.0 * ratio - rho_old)
        weights.append((rho_new * rho_old, 2.0 * rho_new / half))
        rho_old = rho_new
    return weights


WEIGHTS = chebyshev_weights(STEPS)


def shape(dims, dtype):
    return jax.ShapeDtypeStruct(dims, dtype)


def call(kernel, outs, scratch=(), limit=40 * MIB, **specs):
    return pl.pallas_call(
        kernel,
        out_shape=outs,
        scratch_shapes=list(scratch),
        compiler_params=pltpu.CompilerParams(vmem_limit_bytes=limit),
        cost_estimate=pl.CostEstimate(flops=10**7, bytes_accessed=4 * 10**6, transcendentals=0),
        **specs,
    )


def skew(arrays):
    block = lax.broadcasted_iota(jnp.int32, arrays[0].shape, 1) // BX
    arrays = list(arrays)
    for bit in range(3):
        step = 1 << bit
        upper = (block // step) % 2 == 1
        arrays = [jnp.where(upper, arrays[(j + step) % 8], arrays[j]) for j in range(8)]
    return [arrays[-z % 8] for z in range(8)]


def to_blocks(rows):
    return skew([pltpu.roll(row, BX * i, 1) if i else row for i, row in enumerate(rows)])


def from_blocks(blocks):
    return [pltpu.roll(row, LANES - BX * i, 1) if i else row for i, row in enumerate(skew(blocks))]


def turned(p):
    z, odd = lax.axis_index("wall") % WZ, lax.axis_index("stream") % 2
    return (p - (z + odd * (WZ - 1 - 2 * z)) + WZ) % WZ


def owner(t, z):
    span, odd = lax.axis_index("span"), lax.axis_index("stream") % 2
    return WZ * (t + span * (WY - 1 - 2 * t)) + z + odd * (WZ - 1 - 2 * z)


def strided(s):
    return pl.ds(s, ROWS, stride=SPAN)


def edge_lanes(blocks, pick, turn, offset):
    at = lax.broadcasted_iota(jnp.int32, (LANES, LANES), 0)
    to = lax.broadcasted_iota(jnp.int32, (LANES, LANES), 1)
    one = jnp.where((at % BX == pick) & (to == (at // BX + turn) % 8), 1.0, 0.0).astype(BF16)
    eights = jnp.dot(blocks.reshape(8 * ROWS, LANES), one, preferred_element_type=F32)
    out = jnp.zeros((ROWS, LANES), F32)
    for q in range(8):
        out += pltpu.roll(eights[ROWS * q : ROWS * (q + 1)], (8 * q + offset) % LANES, 1)
    return out.astype(BF16)


def pack(
    b_hbm, v_hbm, m_hbm, send_hbm, es_hbm, dl_hbm, dr_hbm, b_buf, v_buf, m_buf, send, es, dl, dr, cl, cr,
    sems, done, small,
):
    def copy(k, t):
        src, dst = ((v_hbm, v_buf), (b_hbm, b_buf))[k]
        rows = pl.ds(BS * t, BS)
        return pltpu.make_async_copy(src.at[:, rows, :], dst.at[:, rows, :], sems.at[k, t])

    def result(k, y):
        part = (pl.ds(WZ * y, WZ), slice(2 * ROWS, None) if k else slice(0, 2 * ROWS))
        return pltpu.make_async_copy(send.at[part], send_hbm.at[part], done.at[k, y])

    for k in range(2):
        for t in range(WY):
            copy(k, t).start()
    metric = pltpu.make_async_copy(m_hbm, m_buf, small.at[3])
    metric.start()
    edges = [
        pltpu.make_async_copy(src, dst, small.at[n])
        for n, (src, dst) in enumerate(((es, es_hbm), (dl, dl_hbm), (dr, dr_hbm)))
    ]

    def move(t, k, buf, mid):
        for g in range(2):
            parts = [buf[strided(16 * t + 8 * g + i), :] - mid for i in range(8)]
            parts = to_blocks([part.astype(BF16) for part in parts])
            rows = slice(ROWS * (2 * k + g), ROWS * (2 * k + g + 1))
            for z in range(WZ):
                send[owner(t, z), rows, :] = parts[z]
            if k:
                cl[2 * t + g] = parts[0]
                cr[2 * t + g] = parts[7]
        return 0

    v_flat, b_flat = (buf.reshape(ROWS * SPAN, LANES) for buf in (v_buf, b_buf))

    def first(t, _):
        copy(0, t).wait()
        move(t, 1, v_flat, MID)
        return 0

    lax.fori_loop(0, WY, first, 0, unroll=2)
    metric.wait()
    rest = m_buf[...]
    parts = []
    for _ in range(3):
        part = rest.astype(BF16)
        rest = rest - part.astype(F32)
        parts.append(part.astype(F32))
    tail = jnp.concatenate(parts + [jnp.zeros((TAIL - 3, ROWS), F32)], axis=0)
    tail = jnp.concatenate([tail, jnp.zeros((TAIL, LANES - ROWS), F32)], axis=1).astype(BF16)
    for k in range(WY * WZ):
        send[k, 4 * ROWS :, :] = tail
    for t in range(WY):
        result(1, t).start()

    def last(t, _):
        copy(1, t).wait()
        move(t, 0, b_flat, 0.0)
        result(0, owner(t, 0) // WZ).start()
        return 0

    lax.fori_loop(0, WY, last, 0, unroll=2)
    es[0] = (v_flat[strided(0), :] - MID).astype(BF16)
    es[1] = (v_flat[strided(SPAN - 1), :] - MID).astype(BF16)
    dl[...] = edge_lanes(cl[...], 0, 0, SPAN)
    dr[...] = edge_lanes(cr[...], BX - 1, 1, SPAN)
    for edge in edges:
        edge.start()
    for k in range(2):
        for t in range(WY):
            result(k, t).wait()
    for edge in edges:
        edge.wait()


def to_lines(recv, bf, hf, metric, *edges):
    for i in range(8):
        row = jnp.zeros((TAIL, LANES), F32)
        for j in range(4):
            row += pltpu.roll(recv[4 * i + j, 4 * ROWS :, :].astype(F32), ROWS * j, 1)
        metric[:, i * LANES : (i + 1) * LANES] = jnp.sum(row, axis=0, keepdims=True)
    for k, ref in enumerate((bf, hf)):
        for i in range(CHUNKS):
            for g in range(2):
                tile = recv[4 * i : 4 * i + 4, ROWS * (2 * k + g) : ROWS * (2 * k + g + 1), :]
                tile = tile.astype(F32).reshape(LANES, LANES).T
                if k:
                    tile = 0.5 * tile + 0.5 * MID
                for p in range(8):
                    ref[line_rows(i, 8 * g + turned(p)), :] = tile[BX * p : BX * (p + 1)]
    for i in range(CHUNKS):
        lanes = slice(i * LANES, (i + 1) * LANES)
        for n, rows in enumerate(edge_rows(i)):
            edges[n][:BX, lanes] = bf[rows, :].astype(BF16)
            edges[n][BX:, lanes] = (2.0 * hf[rows, :] - MID).astype(BF16)
    mirror(hf)


def line_rows(i, s):
    return pl.ds(ROW_COUNT * i + FIRST + LP * s, BX)


def edge_rows(i):
    base = ROW_COUNT * i + FIRST
    return (
        line_rows(i, 0),
        line_rows(i, BS - 1),
        pl.ds(base, BS, stride=LP),
        pl.ds(base + BX - 1, BS, stride=LP),
    )


def near_rows(i):
    base = ROW_COUNT * i + FIRST
    return (
        line_rows(i, -1),
        line_rows(i, BS),
        pl.ds(base - 1, BS, stride=LP),
        pl.ds(base + BX, BS, stride=LP),
    )


def mirror(field):
    for i in range(CHUNKS):
        for near, edge in zip(near_rows(i), edge_rows(i)):
            field[near, :] = field[edge, :]


def busy(i):
    return pl.ds(ROW_COUNT * i + FIRST, BUSY)


def apply_lines(rows, line):
    return lax.dot_general(rows, line, (((1,), (1,)), ((), ())), preferred_element_type=F32)


def first_lines(bf, hf, metric, line, x1, fw, resid, rounded):
    for i in range(CHUNKS):
        rounded[:, i * LANES : (i + 1) * LANES] = bf[busy(i), :].astype(BF16)
    y = WEIGHTS[0][1] * apply_lines(rounded[...], line[...])
    for i in range(CHUNKS):
        x1[busy(i), :] = y[:, i * LANES : (i + 1) * LANES]
    mirror(x1)
    line_resid(bf, x1, hf, fw, metric, resid, make_weights=True)


def line_resid(bf, xe, he, fw, metric, out, make_weights=False):
    lane = lax.broadcasted_iota(jnp.int32, (RUN, LANES), 1)
    last, first = lane == LANES - 1, lane == 0

    def one(c, _):
        def load(ref, i, shift=0):
            return ref[pl.ds(ROW_COUNT * i + FIRST + shift + RUN * c, RUN), :]

        xc = load(xe, 0)
        moved_x = pltpu.roll(xc, LANES - 1, 1)
        kappa = load(he, 0) * metric[:, :LANES]
        entry = kappa * -xc
        moved_k = pltpu.roll(kappa, LANES - 1, 1)
        for i in range(CHUNKS):
            if i + 1 < CHUNKS:
                after = load(xe, i + 1)
                moved_after = pltpu.roll(after, LANES - 1, 1)
                kappa_after = load(he, i + 1) * metric[:, (i + 1) * LANES : (i + 2) * LANES]
                moved_k_after = pltpu.roll(kappa_after, LANES - 1, 1)
            else:
                after = moved_after = jnp.zeros((RUN, LANES), F32)
                kappa_after = moved_k_after = after
            if make_weights:
                weight = kappa + jnp.where(last, moved_k_after, moved_k)
                fw[pl.ds(ROW_COUNT * i + FIRST + RUN * c, RUN), :] = weight
            else:
                weight = load(fw, i)
            above = weight * (xc - jnp.where(last, moved_after, moved_x))
            below = pltpu.roll(above, 1, 1)
            hc = load(he, i)
            total = above - jnp.where(first, entry, below)
            for shift in (-LP, -1, 1, LP):
                total += (hc + load(he, i, shift)) * (xc - load(xe, i, shift))
            out[pl.ds(ROW_COUNT * i + FIRST + RUN * c, RUN), :] = load(bf, i) - (xc + total)
            xc, moved_x, entry = after, moved_after, below
            kappa, moved_k = kappa_after, moved_k_after
        return 0

    lax.fori_loop(0, BUSY // RUN, one, 0)


def finish_resid(resid, x, hf, near, x_near, out, rounded):
    for i in range(CHUNKS):
        lanes = slice(i * LANES, (i + 1) * LANES)
        out[busy(i), :] = resid[busy(i), :]
        for k, rows in enumerate(edge_rows(i)):
            weight = hf[rows, :] + 0.5 * near[k][BX:, lanes].astype(F32) + 0.5 * MID
            out[rows, :] = out[rows, :] - weight * (x[rows, :] - x_near(k, i))
        rounded[:, lanes] = out[busy(i), :].astype(BF16)


def second_step(resid, x1, hf, su, sd, xl, xr, line, x2, d2, e0, e1, e2, e3, full, rt, ends):
    near = (su, sd, xl, xr)
    for k, ref in enumerate(near):
        ends[k * BX : (k + 1) * BX] = ref[0:BX]
    ends1 = WEIGHTS[0][1] * apply_lines(ends[...], line[...])

    def x_near(k, i):
        return ends1[k * BX : (k + 1) * BX, i * LANES : (i + 1) * LANES]

    finish_resid(resid, x1, hf, near, x_near, full, rt)
    keep, scale = WEIGHTS[1]
    y = scale * apply_lines(rt[...], line[...])
    for i in range(CHUNKS):
        lanes = slice(i * LANES, (i + 1) * LANES)
        x = x1[busy(i), :]
        d = keep * x + y[:, lanes]
        d2[busy(i), :] = d
        x2[busy(i), :] = x + d
        for rows, ref in zip(edge_rows(i), (e0, e1, e2, e3)):
            ref[:, lanes] = x2[rows, :].astype(BF16)
    mirror(x2)


def third_step(
    resid, x2, d2, hf, su, sd, xl, xr, vsu, vsd, vxl, vxr, line, ends, send, xe, rt
):
    x_edges = (su, sd, xl, xr)

    def x_near(k, i):
        return x_edges[k][:, i * LANES : (i + 1) * LANES].astype(F32)

    finish_resid(resid, x2, hf, (vsu, vsd, vxl, vxr), x_near, xe, rt)
    keep, scale = WEIGHTS[2]
    y = scale * apply_lines(rt[...], line[...])
    count = WY * WZ
    nothing = jnp.zeros((1, LANES), F32)
    firsts, lasts = {}, {}
    for i in range(CHUNKS):
        xe[busy(i), :] = x2[busy(i), :] + keep * d2[busy(i), :] + y[:, i * LANES : (i + 1) * LANES]
        for j in range(2):
            tile = jnp.concatenate([xe[line_rows(i, 8 * j + turned(p)), :] for p in range(8)], axis=0).T
            for k in range(4):
                part = tile[ROWS * k : ROWS * (k + 1)]
                send[4 * i + k, ROWS * j : ROWS * (j + 1), :] = part.astype(BF16)
                firsts[4 * i + k, j] = part[:1]
                lasts[4 * i + k, j] = part[ROWS - 1 :]
    for k in range(count):
        rows = []
        for j in range(2):
            rows += [lasts.get((k - 1, j), nothing), firsts.get((k + 1, j), nothing)]
            rows.append(ends[k, 2 * j : 2 * j + 2, :])
        send[k, 2 * ROWS :, :] = jnp.concatenate(rows, axis=0).astype(BF16)


def block_row(w, s=0):
    return CP * (w + 1) + 1 + s


def block_span(s):
    return pl.ds(block_row(0, s), ROWS, stride=CP)


def unpack(recv, ves, vdl, vdr, xf, es, dl, dr, cl, cr):
    def one(t, _):
        for g in range(2):
            rows = slice(ROWS * g, ROWS * (g + 1))
            parts = [recv[owner(t, z), rows, :] for z in range(WZ)]
            cl[2 * t + g] = parts[0]
            cr[2 * t + g] = parts[7]
            parts = from_blocks(parts)
            for i in range(8):
                s = 16 * t + 8 * g + i
                xf[pl.ds(block_row(0) + s, ROWS, stride=CP), :] = parts[i].astype(F32)
        return 0

    lax.fori_loop(0, WY, one, 0, unroll=4)
    for k, (s, beside) in enumerate(((0, -1), (SPAN - 1, SPAN))):
        edge = xf[block_span(s), :]
        xf[block_span(beside), :] = edge
        es[k] = edge.astype(BF16)
    for w, beside in ((0, -1), (ROWS - 1, ROWS)):
        xf[pl.ds(block_row(beside), SPAN), :] = xf[pl.ds(block_row(w), SPAN), :]
    es[2] = ves[0]
    es[3] = ves[1]
    dl[...] = edge_lanes(cl[...], 0, 0, 0) + vdl[...]
    dr[...] = edge_lanes(cr[...], BX - 1, 1, 0) + vdr[...]


def weights(v_ref, m_ref, recv, metric, hf, gx, gk, ends):
    def four(n, below):
        for k in range(4):
            w = 4 * n + k
            half = 0.5 * v_ref[w]
            hf[pl.ds(block_row(w), SPAN), :] = half
            cells = pl.ds(pl.multiple_of(SPAN * w, SPAN), SPAN)
            gx[cells, :] = half + pltpu.roll(half, LANES - 1, 1)
            half = m_ref[w] * half
            gk[cells, :] = below + half
            below = half
        return below

    gk[SPAN * ROWS :, :] = lax.fori_loop(0, ROWS // 4, four, jnp.zeros((SPAN, LANES), F32))
    for s in (-1, SPAN):
        hf[block_span(s), :] = jnp.zeros((ROWS, LANES), F32)
    count = WY * WZ
    nothing = jnp.zeros((1, LANES), F32)
    for k in range(count):
        rows = []
        for g in range(2):
            for other, at in ((k - 1, ROWS - 1), (k + 1, 0)):
                if not 0 <= other < count:
                    rows.append(nothing)
                    continue
                v = recv[other, ROWS * (2 + g) : ROWS * (3 + g), :].astype(F32) + MID
                rows.append(v[at : at + 1] * metric[:, ROWS * other + at : ROWS * other + at + 1])
        ends[k] = jnp.concatenate(rows, axis=0)


def placed(right, left):
    at = lax.broadcasted_iota(jnp.int32, (2 * ROWS, LANES), 0)
    to = lax.broadcasted_iota(jnp.int32, (2 * ROWS, LANES), 1)
    place = jnp.where(to == 2 * (at % ROWS) + at // ROWS, 1.0, 0.0).astype(BF16)
    both = jnp.concatenate([right[...], left[...]], axis=0)
    return lax.dot_general(both, place, (((0,), (0,)), ((), ())), preferred_element_type=F32)


def inner_resid(xf, hf, gx, gk, recv, b_ref, dl, dr, x3, resid, own, x_buf, beyond, sems):
    lane = lax.broadcasted_iota(jnp.int32, (ROWS, LANES), 1)
    halves = (0, ROWS)

    def load(ref, w, s):
        return ref[pl.ds(block_row(w, s), ROWS), :]

    def result(n):
        rows = pl.ds(4 * n, 4)
        return pltpu.make_async_copy(x_buf.at[rows], x3.at[rows], sems.at[n])

    def four(q, carry):
        carry = list(carry)
        for n in range(4):
            w = 4 * q + n
            for h, s in enumerate(halves):
                xc, hc = load(xf, w, s), load(hf, w, s)
                x_buf[w, s : s + ROWS, :] = xc
                above = gk[pl.ds(SPAN * (w + 1) + s, ROWS), :] * (xc - load(xf, w + 1, s))
                total = above - carry[h]
                carry[h] = above
                for d in (-1, 1):
                    total += (hc + load(hf, w, s + d)) * (xc - load(xf, w, s + d))
                right = gx[pl.ds(SPAN * w + s, ROWS), :] * (xc - pltpu.roll(xc, LANES - 1, 1))
                right = jnp.where(lane == LANES - 1, 0.0, right)
                total += right - pltpu.roll(right, 1, 1)
                resid[w, s : s + ROWS, :] = b_ref[w, s : s + ROWS, :] - (xc + total)
        result(q).start()
        return tuple(carry)

    zero = jnp.zeros((ROWS, LANES), F32)
    lax.fori_loop(0, ROWS // 4, four, (zero, zero))

    def tail(t, _):
        parts = from_blocks([recv[owner(t, z), 2 * ROWS :, :].astype(F32) for z in range(WZ)])
        for g in range(2):
            for i in range(8):
                for k in range(4):
                    row = pl.ds(SPAN * k + 16 * t + 8 * g + i, 1)
                    beyond[row, :] = parts[i][4 * g + k : 4 * g + k + 1]
        return 0

    lax.fori_loop(0, WY, tail, 0)
    for k, w in enumerate((0, ROWS - 1)):
        face = gk[SPAN * ROWS * k : SPAN * (ROWS * k + 1), :]
        weight = face + 0.5 * beyond[SPAN * (2 + k) : SPAN * (3 + k), :]
        x = xf[pl.ds(block_row(w), SPAN), :]
        resid[w] = resid[w] - weight * (x - beyond[SPAN * k : SPAN * (k + 1), :])
    own[...] = placed(dr, dl)
    for q in range(ROWS // 4):
        result(q).wait()


def last_resid(resid, xf, hf, own, spans, lefts, rights, out, side_rows, r_buf, sems):
    for k, s in enumerate((0, SPAN - 1)):
        weight = hf[block_span(s), :] + 0.5 * spans[3 - k].astype(F32) + 0.5 * MID
        side_rows[k] = weight * (xf[block_span(s), :] - spans[1 - k].astype(F32))
    near = placed(rights, lefts)
    sides = (0.5 * (own[SPAN:] + near[SPAN:]) + MID) * (own[:SPAN] - near[:SPAN])
    lane = lax.broadcasted_iota(jnp.int32, (SPAN, LANES), 1)
    ends = (lane == 0) | (lane == LANES - 1)
    row = lax.broadcasted_iota(jnp.int32, (8, LANES), 0)

    def results(q):
        rows = pl.ds(4 * q, 4)
        return pltpu.make_async_copy(r_buf.at[rows], out.at[rows], sems.at[q])

    def four(q, carry):
        for n in range(4):
            w = 4 * q + n
            r = resid[w] - jnp.where(ends, pltpu.roll(sides, LANES - 1 - 2 * w, 1), 0.0)
            r_buf[w, 8 : SPAN - 8, :] = r[8 : SPAN - 8]
            for k, s in enumerate((0, SPAN - 8)):
                flux = side_rows[k, pl.ds(w, 1), :]
                r_buf[w, s : s + 8, :] = r[s : s + 8] - jnp.where(row == 7 * k, flux, 0.0)
        results(q).start()
        return carry

    lax.fori_loop(0, ROWS // 4, four, 0)
    for q in range(ROWS // 4):
        results(q).wait()


def block_edges(es, dl, dr):
    streams = lax.axis_size("stream")
    right = [(i, (i + 1) % streams) for i in range(streams)]
    left = [((i + 1) % streams, i) for i in range(streams)]
    return (
        lax.ppermute(es, "span", [(0, 1), (1, 0)]),
        lax.ppermute(dr, "stream", right),
        lax.ppermute(dl, "stream", left),
    )


def line_shift(value, ds, dx):
    spans, streams = lax.axis_size("span"), lax.axis_size("stream")

    def device(sb, xb):
        sp, y = divmod(sb % (spans * WY), WY)
        st, z = divmod(xb % (streams * WZ), WZ)
        y, z = (WY - 1 - y if sp % 2 else y), (WZ - 1 - z if st % 2 else z)
        return ((y * WZ + z) * spans + sp) * streams + st

    pairs = [
        (device(sb, xb), device(sb + ds, xb + dx))
        for sb in range(spans * WY)
        for xb in range(streams * WZ)
    ]
    return lax.ppermute(value, ("wall", "span", "stream"), pairs)


def line_edges(*edges):
    return (
        line_shift(edges[1], 1, 0),
        line_shift(edges[0], -1, 0),
        line_shift(edges[3], 0, 1),
        line_shift(edges[2], 0, -1),
    )


def body(right_side, viscosity, wall_metric, line_inverse):
    block = pltpu.VMEM((ROWS, SPAN, LANES), F32)
    side = pltpu.VMEM((8, ROWS, LANES), BF16)
    dense = shape((ROWS, LANES), BF16)
    hbm, vmem = pl.BlockSpec(memory_space=pltpu.HBM), pl.BlockSpec(memory_space=pltpu.VMEM)
    sent = (WY * WZ, 4 * ROWS + TAIL, LANES)
    dma = pltpu.SemaphoreType.DMA
    send, *v_edges = call(
        pack,
        (shape(sent, BF16), shape((2, ROWS, LANES), BF16), dense, dense),
        (
            block,
            block,
            pltpu.VMEM((1, ROWS), F32),
            pltpu.VMEM(sent, BF16),
            pltpu.VMEM((2, ROWS, LANES), BF16),
            pltpu.VMEM((ROWS, LANES), BF16),
            pltpu.VMEM((ROWS, LANES), BF16),
            side,
            side,
            dma((2, WY)),
            dma((2, WY)),
            dma((4,)),
        ),
        62 * MIB + MIB // 2,
        in_specs=(hbm,) * 3,
        out_specs=(hbm,) * 4,
    )(right_side, viscosity, wall_metric.reshape(1, ROWS))
    recv = lax.all_to_all(send, "wall", 0, 0, tiled=True)
    field = shape((CHUNKS * ROW_COUNT, LANES), F32)
    bf, hf, metric, *edges = call(
        to_lines,
        (field, field, shape((1, NW), F32))
        + (shape((2 * BX, NW), BF16),) * 4,
    )(recv)
    near = line_edges(*edges)
    ext = pltpu.VMEM((CHUNKS * ROW_COUNT, LANES), F32)
    rounded = pltpu.VMEM((BUSY, NW), BF16)
    x1, fw, resid = call(first_lines, (field, field, field), (rounded,))(
        bf, hf, metric, line_inverse
    )
    x2, d2, *edges = call(
        second_step,
        (field, field) + (shape((BX, NW), BF16),) * 4,
        (ext, rounded, pltpu.VMEM((4 * BX, NW), BF16)),
    )(resid, x1, hf, *near, line_inverse)
    x_near = line_edges(*edges)
    resid = call(line_resid, field)(bf, x2, hf, fw, metric)
    v, m, _ = lax.optimization_barrier((viscosity, wall_metric, d2))
    smem = pl.BlockSpec(memory_space=pltpu.SMEM)
    cells = shape((BLOCK_ROWS, LANES), F32)
    *face_weights, ends = call(
        weights,
        (
            cells,
            shape((ROWS * SPAN, LANES), F32),
            shape(((ROWS + 1) * SPAN, LANES), F32),
            shape((WY * WZ, 4, LANES), F32),
        ),
        in_specs=(vmem, smem, vmem, vmem),
    )(v, m, recv, metric)
    face_weights, resid = lax.optimization_barrier((face_weights, resid))
    send = call(
        third_step, shape((WY * WZ, 2 * ROWS + TAIL, LANES), BF16), (ext, rounded)
    )(resid, x2, d2, hf, *x_near, *near, line_inverse, ends)
    recv = lax.all_to_all(send, "wall", 0, 0, tiled=True)
    xf, *edges = call(
        unpack,
        (cells, shape((4, ROWS, LANES), BF16), dense, dense),
        (side, side),
    )(recv, *v_edges)
    x_edges = block_edges(*edges)
    whole = shape(right_side.shape, F32)
    x3, resid, own = call(
        inner_resid,
        (whole, whole, shape((LANES, LANES), F32)),
        (block, pltpu.VMEM((4 * SPAN, LANES), F32), dma((ROWS // 4,))),
        out_specs=(hbm, vmem, vmem),
    )(xf, *face_weights, recv, right_side, *edges[1:])
    residual = call(
        last_resid,
        whole,
        (pltpu.VMEM((2, ROWS, LANES), F32), block, dma((ROWS // 4,))),
        out_specs=hbm,
    )(resid, xf, face_weights[0], own, *x_edges)
    return x3, residual


def solution(mesh):
    in_specs = (P("wall", "span", "stream"), P("wall", "span", "stream"), P("wall"), P())
    out_specs = (P("wall", "span", "stream"), P("wall", "span", "stream"))
    return jax.shard_map(body, mesh=mesh, in_specs=in_specs, out_specs=out_specs, check_vma=False)
```

```python
import functools

import jax
import jax.numpy as jnp
from jax import lax
from jax.experimental import pallas as pl
from jax.experimental.pallas import tpu as pltpu
from jax.sharding import PartitionSpec as P

STEPS = 3
NW, WY, WZ = 1024, 4, 8
ROWS, SPAN, LANES = 32, 64, 128
BS, BX = 16, 16
CELLS = BS * BX
CHUNKS = NW // 128
LP, FIRST, BUSY, ROW_COUNT = BX + 2, 24, 288, 336
RUN = 48
CP = SPAN + 3
BLOCK_ROWS = 2280
TAIL = 8
MID = 0.5
F32, BF16 = jnp.float32, jnp.bfloat16
MIB = 1024 * 1024


def chebyshev_weights(steps):
    lowest = 0.25
    highest = 2.5
    center = 0.5 * (highest + lowest)
    half = 0.5 * (highest - lowest)
    ratio = center / half
    weights = [(0.0, 1.0 / center)]
    rho_old = 1.0 / ratio
    for step in range(1, steps):
        rho_new = 1.0 / (2.0 * ratio - rho_old)
        weights.append((rho_new * rho_old, 2.0 * rho_new / half))
        rho_old = rho_new
    return weights


WEIGHTS = chebyshev_weights(STEPS)


def shape(dims, dtype):
    return jax.ShapeDtypeStruct(dims, dtype)


def call(kernel, outs, scratch=(), limit=40 * MIB, **specs):
    return pl.pallas_call(
        kernel,
        out_shape=outs,
        scratch_shapes=list(scratch),
        compiler_params=pltpu.CompilerParams(vmem_limit_bytes=limit),
        cost_estimate=pl.CostEstimate(flops=10**7, bytes_accessed=4 * 10**6, transcendentals=0),
        **specs,
    )


def skew(arrays):
    block = lax.broadcasted_iota(jnp.int32, arrays[0].shape, 1) // BX
    arrays = list(arrays)
    for bit in range(3):
        step = 1 << bit
        upper = (block // step) % 2 == 1
        arrays = [jnp.where(upper, arrays[(j + step) % 8], arrays[j]) for j in range(8)]
    return [arrays[-z % 8] for z in range(8)]


def to_blocks(rows):
    return skew([pltpu.roll(row, BX * i, 1) if i else row for i, row in enumerate(rows)])


def from_blocks(blocks):
    return [pltpu.roll(row, LANES - BX * i, 1) if i else row for i, row in enumerate(skew(blocks))]


def turned(p):
    z, odd = lax.axis_index("wall") % WZ, lax.axis_index("stream") % 2
    return (p - (z + odd * (WZ - 1 - 2 * z)) + WZ) % WZ


def owner(t, z):
    span, odd = lax.axis_index("span"), lax.axis_index("stream") % 2
    return WZ * (t + span * (WY - 1 - 2 * t)) + z + odd * (WZ - 1 - 2 * z)


def strided(s):
    return pl.ds(s, ROWS, stride=SPAN)


def edge_lanes(blocks, pick, turn, offset):
    at = lax.broadcasted_iota(jnp.int32, (LANES, LANES), 0)
    to = lax.broadcasted_iota(jnp.int32, (LANES, LANES), 1)
    one = jnp.where((at % BX == pick) & (to == (at // BX + turn) % 8), 1.0, 0.0).astype(BF16)
    eights = jnp.dot(blocks.reshape(8 * ROWS, LANES), one, preferred_element_type=F32)
    out = jnp.zeros((ROWS, LANES), F32)
    for q in range(8):
        out += pltpu.roll(eights[ROWS * q : ROWS * (q + 1)], (8 * q + offset) % LANES, 1)
    return out.astype(BF16)


def pack(
    b_hbm, v_hbm, m_hbm, send_hbm, es_hbm, dl_hbm, dr_hbm, b_buf, v_buf, m_buf, send, es, dl, dr, cl, cr,
    sems, done, small,
):
    def copy(k, t):
        src, dst = ((v_hbm, v_buf), (b_hbm, b_buf))[k]
        rows = pl.ds(BS * t, BS)
        return pltpu.make_async_copy(src.at[:, rows, :], dst.at[:, rows, :], sems.at[k, t])

    def result(k, y):
        part = (pl.ds(WZ * y, WZ), slice(2 * ROWS, None) if k else slice(0, 2 * ROWS))
        return pltpu.make_async_copy(send.at[part], send_hbm.at[part], done.at[k, y])

    for k in range(2):
        for t in range(WY):
            copy(k, t).start()
    metric = pltpu.make_async_copy(m_hbm, m_buf, small.at[3])
    metric.start()
    edges = [
        pltpu.make_async_copy(src, dst, small.at[n])
        for n, (src, dst) in enumerate(((es, es_hbm), (dl, dl_hbm), (dr, dr_hbm)))
    ]

    def move(t, k, buf, mid):
        for g in range(2):
            parts = [buf[strided(16 * t + 8 * g + i), :] - mid for i in range(8)]
            parts = to_blocks([part.astype(BF16) for part in parts])
            rows = slice(ROWS * (2 * k + g), ROWS * (2 * k + g + 1))
            for z in range(WZ):
                send[owner(t, z), rows, :] = parts[z]
            if k:
                cl[2 * t + g] = parts[0]
                cr[2 * t + g] = parts[7]
        return 0

    v_flat, b_flat = (buf.reshape(ROWS * SPAN, LANES) for buf in (v_buf, b_buf))

    def first(t, _):
        copy(0, t).wait()
        move(t, 1, v_flat, MID)
        return 0

    lax.fori_loop(0, WY, first, 0, unroll=4)
    metric.wait()
    rest = m_buf[...]
    parts = []
    for _ in range(3):
        part = rest.astype(BF16)
        rest = rest - part.astype(F32)
        parts.append(part.astype(F32))
    tail = jnp.concatenate(parts + [jnp.zeros((TAIL - 3, ROWS), F32)], axis=0)
    tail = jnp.concatenate([tail, jnp.zeros((TAIL, LANES - ROWS), F32)], axis=1).astype(BF16)
    for k in range(WY * WZ):
        send[k, 4 * ROWS :, :] = tail
    for t in range(WY):
        result(1, t).start()

    def last(t, _):
        copy(1, t).wait()
        move(t, 0, b_flat, 0.0)
        result(0, owner(t, 0) // WZ).start()
        return 0

    lax.fori_loop(0, WY, last, 0, unroll=4)
    es[0] = (v_flat[strided(0), :] - MID).astype(BF16)
    es[1] = (v_flat[strided(SPAN - 1), :] - MID).astype(BF16)
    dl[...] = edge_lanes(cl[...], 0, 0, SPAN)
    dr[...] = edge_lanes(cr[...], BX - 1, 1, SPAN)
    for edge in edges:
        edge.start()
    for k in range(2):
        for t in range(WY):
            result(k, t).wait()
    for edge in edges:
        edge.wait()


def to_lines(recv, bf, hf, metric, *edges):
    for i in range(8):
        row = jnp.zeros((TAIL, LANES), F32)
        for j in range(4):
            row += pltpu.roll(recv[4 * i + j, 4 * ROWS :, :].astype(F32), ROWS * j, 1)
        metric[:, i * LANES : (i + 1) * LANES] = jnp.sum(row, axis=0, keepdims=True)
    for k, ref in enumerate((bf, hf)):
        for i in range(CHUNKS):
            for g in range(2):
                tile = recv[4 * i : 4 * i + 4, ROWS * (2 * k + g) : ROWS * (2 * k + g + 1), :]
                tile = tile.astype(F32).reshape(LANES, LANES).T
                if k:
                    tile = 0.5 * tile + 0.5 * MID
                for p in range(8):
                    ref[line_rows(i, 8 * g + turned(p)), :] = tile[BX * p : BX * (p + 1)]
    for i in range(CHUNKS):
        lanes = slice(i * LANES, (i + 1) * LANES)
        for n, rows in enumerate(edge_rows(i)):
            edges[n][:BX, lanes] = bf[rows, :].astype(BF16)
            edges[n][BX:, lanes] = (2.0 * hf[rows, :] - MID).astype(BF16)
    mirror(hf)


def line_rows(i, s):
    return pl.ds(ROW_COUNT * i + FIRST + LP * s, BX)


def edge_rows(i):
    base = ROW_COUNT * i + FIRST
    return (
        line_rows(i, 0),
        line_rows(i, BS - 1),
        pl.ds(base, BS, stride=LP),
        pl.ds(base + BX - 1, BS, stride=LP),
    )


def near_rows(i):
    base = ROW_COUNT * i + FIRST
    return (
        line_rows(i, -1),
        line_rows(i, BS),
        pl.ds(base - 1, BS, stride=LP),
        pl.ds(base + BX, BS, stride=LP),
    )


def mirror(field):
    for i in range(CHUNKS):
        for near, edge in zip(near_rows(i), edge_rows(i)):
            field[near, :] = field[edge, :]


def busy(i):
    return pl.ds(ROW_COUNT * i + FIRST, BUSY)


def apply_lines(rows, line):
    return lax.dot_general(rows, line, (((1,), (1,)), ((), ())), preferred_element_type=F32)


def first_lines(bf, hf, metric, line, x1, fw, resid, rounded):
    for i in range(CHUNKS):
        rounded[:, i * LANES : (i + 1) * LANES] = bf[busy(i), :].astype(BF16)
    y = WEIGHTS[0][1] * apply_lines(rounded[...], line[...])
    for i in range(CHUNKS):
        x1[busy(i), :] = y[:, i * LANES : (i + 1) * LANES]
    mirror(x1)
    line_resid(bf, x1, hf, fw, metric, resid, make_weights=True)


def line_resid(bf, xe, he, fw, metric, out, make_weights=False):
    lane = lax.broadcasted_iota(jnp.int32, (RUN, LANES), 1)
    last, first = lane == LANES - 1, lane == 0

    def one(c, _):
        def load(ref, i, shift=0):
            return ref[pl.ds(ROW_COUNT * i + FIRST + shift + RUN * c, RUN), :]

        xc = load(xe, 0)
        moved_x = pltpu.roll(xc, LANES - 1, 1)
        kappa = load(he, 0) * metric[:, :LANES]
        entry = kappa * -xc
        moved_k = pltpu.roll(kappa, LANES - 1, 1)
        for i in range(CHUNKS):
            if i + 1 < CHUNKS:
                after = load(xe, i + 1)
                moved_after = pltpu.roll(after, LANES - 1, 1)
                kappa_after = load(he, i + 1) * metric[:, (i + 1) * LANES : (i + 2) * LANES]
                moved_k_after = pltpu.roll(kappa_after, LANES - 1, 1)
            else:
                after = moved_after = jnp.zeros((RUN, LANES), F32)
                kappa_after = moved_k_after = after
            if make_weights:
                weight = kappa + jnp.where(last, moved_k_after, moved_k)
                fw[pl.ds(ROW_COUNT * i + FIRST + RUN * c, RUN), :] = weight
            else:
                weight = load(fw, i)
            above = weight * (xc - jnp.where(last, moved_after, moved_x))
            below = pltpu.roll(above, 1, 1)
            hc = load(he, i)
            total = above - jnp.where(first, entry, below)
            for shift in (-LP, -1, 1, LP):
                total += (hc + load(he, i, shift)) * (xc - load(xe, i, shift))
            out[pl.ds(ROW_COUNT * i + FIRST + RUN * c, RUN), :] = load(bf, i) - (xc + total)
            xc, moved_x, entry = after, moved_after, below
            kappa, moved_k = kappa_after, moved_k_after
        return 0

    lax.fori_loop(0, BUSY // RUN, one, 0)


def finish_resid(resid, x, hf, near, x_near, out, rounded):
    for i in range(CHUNKS):
        lanes = slice(i * LANES, (i + 1) * LANES)
        out[busy(i), :] = resid[busy(i), :]
        for k, rows in enumerate(edge_rows(i)):
            weight = hf[rows, :] + 0.5 * near[k][BX:, lanes].astype(F32) + 0.5 * MID
            out[rows, :] = out[rows, :] - weight * (x[rows, :] - x_near(k, i))
        rounded[:, lanes] = out[busy(i), :].astype(BF16)


def second_step(resid, x1, hf, su, sd, xl, xr, line, x2, d2, e0, e1, e2, e3, full, rt, ends):
    near = (su, sd, xl, xr)
    for k, ref in enumerate(near):
        ends[k * BX : (k + 1) * BX] = ref[0:BX]
    ends1 = WEIGHTS[0][1] * apply_lines(ends[...], line[...])

    def x_near(k, i):
        return ends1[k * BX : (k + 1) * BX, i * LANES : (i + 1) * LANES]

    finish_resid(resid, x1, hf, near, x_near, full, rt)
    keep, scale = WEIGHTS[1]
    y = scale * apply_lines(rt[...], line[...])
    for i in range(CHUNKS):
        lanes = slice(i * LANES, (i + 1) * LANES)
        x = x1[busy(i), :]
        d = keep * x + y[:, lanes]
        d2[busy(i), :] = d
        x2[busy(i), :] = x + d
        for rows, ref in zip(edge_rows(i), (e0, e1, e2, e3)):
            ref[:, lanes] = x2[rows, :].astype(BF16)
    mirror(x2)


def third_step(
    resid, x2, d2, hf, su, sd, xl, xr, vsu, vsd, vxl, vxr, line, ends, send, xe, rt
):
    x_edges = (su, sd, xl, xr)

    def x_near(k, i):
        return x_edges[k][:, i * LANES : (i + 1) * LANES].astype(F32)

    finish_resid(resid, x2, hf, (vsu, vsd, vxl, vxr), x_near, xe, rt)
    keep, scale = WEIGHTS[2]
    y = scale * apply_lines(rt[...], line[...])
    count = WY * WZ
    nothing = jnp.zeros((1, LANES), F32)
    firsts, lasts = {}, {}
    for i in range(CHUNKS):
        xe[busy(i), :] = x2[busy(i), :] + keep * d2[busy(i), :] + y[:, i * LANES : (i + 1) * LANES]
        for j in range(2):
            tile = jnp.concatenate([xe[line_rows(i, 8 * j + turned(p)), :] for p in range(8)], axis=0).T
            for k in range(4):
                part = tile[ROWS * k : ROWS * (k + 1)]
                send[4 * i + k, ROWS * j : ROWS * (j + 1), :] = part.astype(BF16)
                firsts[4 * i + k, j] = part[:1]
                lasts[4 * i + k, j] = part[ROWS - 1 :]
    for k in range(count):
        rows = []
        for j in range(2):
            rows += [lasts.get((k - 1, j), nothing), firsts.get((k + 1, j), nothing)]
            rows.append(ends[k, 2 * j : 2 * j + 2, :])
        send[k, 2 * ROWS :, :] = jnp.concatenate(rows, axis=0).astype(BF16)


def block_row(w, s=0):
    return CP * (w + 1) + 1 + s


def block_span(s):
    return pl.ds(block_row(0, s), ROWS, stride=CP)


def unpack(recv, ves, vdl, vdr, xf, es, dl, dr, cl, cr):
    def one(t, _):
        for g in range(2):
            rows = slice(ROWS * g, ROWS * (g + 1))
            parts = [recv[owner(t, z), rows, :] for z in range(WZ)]
            cl[2 * t + g] = parts[0]
            cr[2 * t + g] = parts[7]
            parts = from_blocks(parts)
            for i in range(8):
                s = 16 * t + 8 * g + i
                xf[pl.ds(block_row(0) + s, ROWS, stride=CP), :] = parts[i].astype(F32)
        return 0

    lax.fori_loop(0, WY, one, 0, unroll=4)
    for k, (s, beside) in enumerate(((0, -1), (SPAN - 1, SPAN))):
        edge = xf[block_span(s), :]
        xf[block_span(beside), :] = edge
        es[k] = edge.astype(BF16)
    for w, beside in ((0, -1), (ROWS - 1, ROWS)):
        xf[pl.ds(block_row(beside), SPAN), :] = xf[pl.ds(block_row(w), SPAN), :]
    es[2] = ves[0]
    es[3] = ves[1]
    dl[...] = edge_lanes(cl[...], 0, 0, 0) + vdl[...]
    dr[...] = edge_lanes(cr[...], BX - 1, 1, 0) + vdr[...]


def weights(v_ref, m_ref, recv, metric, hf, gx, gk, ends):
    def four(n, below):
        for k in range(4):
            w = 4 * n + k
            half = 0.5 * v_ref[w]
            hf[pl.ds(block_row(w), SPAN), :] = half
            cells = pl.ds(pl.multiple_of(SPAN * w, SPAN), SPAN)
            gx[cells, :] = half + pltpu.roll(half, LANES - 1, 1)
            half = m_ref[w] * half
            gk[cells, :] = below + half
            below = half
        return below

    gk[SPAN * ROWS :, :] = lax.fori_loop(0, ROWS // 4, four, jnp.zeros((SPAN, LANES), F32))
    for s in (-1, SPAN):
        hf[block_span(s), :] = jnp.zeros((ROWS, LANES), F32)
    count = WY * WZ
    nothing = jnp.zeros((1, LANES), F32)
    for k in range(count):
        rows = []
        for g in range(2):
            for other, at in ((k - 1, ROWS - 1), (k + 1, 0)):
                if not 0 <= other < count:
                    rows.append(nothing)
                    continue
                v = recv[other, ROWS * (2 + g) : ROWS * (3 + g), :].astype(F32) + MID
                rows.append(v[at : at + 1] * metric[:, ROWS * other + at : ROWS * other + at + 1])
        ends[k] = jnp.concatenate(rows, axis=0)


def placed(right, left):
    at = lax.broadcasted_iota(jnp.int32, (2 * ROWS, LANES), 0)
    to = lax.broadcasted_iota(jnp.int32, (2 * ROWS, LANES), 1)
    place = jnp.where(to == 2 * (at % ROWS) + at // ROWS, 1.0, 0.0).astype(BF16)
    both = jnp.concatenate([right[...], left[...]], axis=0)
    return lax.dot_general(both, place, (((0,), (0,)), ((), ())), preferred_element_type=F32)


def inner_resid(xf, hf, gx, gk, recv, b_ref, dl, dr, x3, resid, own, x_buf, beyond, sems):
    lane = lax.broadcasted_iota(jnp.int32, (ROWS, LANES), 1)
    halves = (0, ROWS)

    def load(ref, w, s):
        return ref[pl.ds(block_row(w, s), ROWS), :]

    def result(n):
        rows = pl.ds(4 * n, 4)
        return pltpu.make_async_copy(x_buf.at[rows], x3.at[rows], sems.at[n])

    def four(q, carry):
        carry = list(carry)
        for n in range(4):
            w = 4 * q + n
            for h, s in enumerate(halves):
                xc, hc = load(xf, w, s), load(hf, w, s)
                x_buf[w, s : s + ROWS, :] = xc
                above = gk[pl.ds(SPAN * (w + 1) + s, ROWS), :] * (xc - load(xf, w + 1, s))
                total = above - carry[h]
                carry[h] = above
                for d in (-1, 1):
                    total += (hc + load(hf, w, s + d)) * (xc - load(xf, w, s + d))
                right = gx[pl.ds(SPAN * w + s, ROWS), :] * (xc - pltpu.roll(xc, LANES - 1, 1))
                right = jnp.where(lane == LANES - 1, 0.0, right)
                total += right - pltpu.roll(right, 1, 1)
                resid[w, s : s + ROWS, :] = b_ref[w, s : s + ROWS, :] - (xc + total)
        result(q).start()
        return tuple(carry)

    zero = jnp.zeros((ROWS, LANES), F32)
    lax.fori_loop(0, ROWS // 4, four, (zero, zero))

    def tail(t, _):
        parts = from_blocks([recv[owner(t, z), 2 * ROWS :, :].astype(F32) for z in range(WZ)])
        for g in range(2):
            for i in range(8):
                for k in range(4):
                    row = pl.ds(SPAN * k + 16 * t + 8 * g + i, 1)
                    beyond[row, :] = parts[i][4 * g + k : 4 * g + k + 1]
        return 0

    lax.fori_loop(0, WY, tail, 0)
    for k, w in enumerate((0, ROWS - 1)):
        face = gk[SPAN * ROWS * k : SPAN * (ROWS * k + 1), :]
        weight = face + 0.5 * beyond[SPAN * (2 + k) : SPAN * (3 + k), :]
        x = xf[pl.ds(block_row(w), SPAN), :]
        resid[w] = resid[w] - weight * (x - beyond[SPAN * k : SPAN * (k + 1), :])
    own[...] = placed(dr, dl)
    for q in range(ROWS // 4):
        result(q).wait()


def last_resid(resid, xf, hf, own, spans, lefts, rights, out, side_rows, r_buf, sems):
    for k, s in enumerate((0, SPAN - 1)):
        weight = hf[block_span(s), :] + 0.5 * spans[3 - k].astype(F32) + 0.5 * MID
        side_rows[k] = weight * (xf[block_span(s), :] - spans[1 - k].astype(F32))
    near = placed(rights, lefts)
    sides = (0.5 * (own[SPAN:] + near[SPAN:]) + MID) * (own[:SPAN] - near[:SPAN])
    lane = lax.broadcasted_iota(jnp.int32, (SPAN, LANES), 1)
    ends = (lane == 0) | (lane == LANES - 1)
    row = lax.broadcasted_iota(jnp.int32, (8, LANES), 0)

    def results(q):
        rows = pl.ds(4 * q, 4)
        return pltpu.make_async_copy(r_buf.at[rows], out.at[rows], sems.at[q])

    def four(q, carry):
        for n in range(4):
            w = 4 * q + n
            r = resid[w] - jnp.where(ends, pltpu.roll(sides, LANES - 1 - 2 * w, 1), 0.0)
            r_buf[w, 8 : SPAN - 8, :] = r[8 : SPAN - 8]
            for k, s in enumerate((0, SPAN - 8)):
                flux = side_rows[k, pl.ds(w, 1), :]
                r_buf[w, s : s + 8, :] = r[s : s + 8] - jnp.where(row == 7 * k, flux, 0.0)
        results(q).start()
        return carry

    lax.fori_loop(0, ROWS // 4, four, 0, unroll=4)
    for q in range(ROWS // 4):
        results(q).wait()


def block_edges(es, dl, dr):
    streams = lax.axis_size("stream")
    right = [(i, (i + 1) % streams) for i in range(streams)]
    left = [((i + 1) % streams, i) for i in range(streams)]
    return (
        lax.ppermute(es, "span", [(0, 1), (1, 0)]),
        lax.ppermute(dr, "stream", right),
        lax.ppermute(dl, "stream", left),
    )


def line_shift(value, ds, dx):
    spans, streams = lax.axis_size("span"), lax.axis_size("stream")

    def device(sb, xb):
        sp, y = divmod(sb % (spans * WY), WY)
        st, z = divmod(xb % (streams * WZ), WZ)
        y, z = (WY - 1 - y if sp % 2 else y), (WZ - 1 - z if st % 2 else z)
        return ((y * WZ + z) * spans + sp) * streams + st

    pairs = [
        (device(sb, xb), device(sb + ds, xb + dx))
        for sb in range(spans * WY)
        for xb in range(streams * WZ)
    ]
    return lax.ppermute(value, ("wall", "span", "stream"), pairs)


def line_edges(*edges):
    return (
        line_shift(edges[1], 1, 0),
        line_shift(edges[0], -1, 0),
        line_shift(edges[3], 0, 1),
        line_shift(edges[2], 0, -1),
    )


def body(right_side, viscosity, wall_metric, line_inverse):
    block = pltpu.VMEM((ROWS, SPAN, LANES), F32)
    side = pltpu.VMEM((8, ROWS, LANES), BF16)
    dense = shape((ROWS, LANES), BF16)
    hbm, vmem = pl.BlockSpec(memory_space=pltpu.HBM), pl.BlockSpec(memory_space=pltpu.VMEM)
    sent = (WY * WZ, 4 * ROWS + TAIL, LANES)
    dma = pltpu.SemaphoreType.DMA
    send, *v_edges = call(
        pack,
        (shape(sent, BF16), shape((2, ROWS, LANES), BF16), dense, dense),
        (
            block,
            block,
            pltpu.VMEM((1, ROWS), F32),
            pltpu.VMEM(sent, BF16),
            pltpu.VMEM((2, ROWS, LANES), BF16),
            pltpu.VMEM((ROWS, LANES), BF16),
            pltpu.VMEM((ROWS, LANES), BF16),
            side,
            side,
            dma((2, WY)),
            dma((2, WY)),
            dma((4,)),
        ),
        62 * MIB + MIB // 2,
        in_specs=(hbm,) * 3,
        out_specs=(hbm,) * 4,
    )(right_side, viscosity, wall_metric.reshape(1, ROWS))
    recv = lax.all_to_all(send, "wall", 0, 0, tiled=True)
    field = shape((CHUNKS * ROW_COUNT, LANES), F32)
    bf, hf, metric, *edges = call(
        to_lines,
        (field, field, shape((1, NW), F32))
        + (shape((2 * BX, NW), BF16),) * 4,
    )(recv)
    near = line_edges(*edges)
    ext = pltpu.VMEM((CHUNKS * ROW_COUNT, LANES), F32)
    rounded = pltpu.VMEM((BUSY, NW), BF16)
    x1, fw, resid = call(first_lines, (field, field, field), (rounded,))(
        bf, hf, metric, line_inverse
    )
    x2, d2, *edges = call(
        second_step,
        (field, field) + (shape((BX, NW), BF16),) * 4,
        (ext, rounded, pltpu.VMEM((4 * BX, NW), BF16)),
    )(resid, x1, hf, *near, line_inverse)
    x_near = line_edges(*edges)
    resid = call(line_resid, field)(bf, x2, hf, fw, metric)
    v, m, _ = lax.optimization_barrier((viscosity, wall_metric, d2))
    smem = pl.BlockSpec(memory_space=pltpu.SMEM)
    cells = shape((BLOCK_ROWS, LANES), F32)
    *face_weights, ends = call(
        weights,
        (
            cells,
            shape((ROWS * SPAN, LANES), F32),
            shape(((ROWS + 1) * SPAN, LANES), F32),
            shape((WY * WZ, 4, LANES), F32),
        ),
        in_specs=(vmem, smem, vmem, vmem),
    )(v, m, recv, metric)
    face_weights, resid = lax.optimization_barrier((face_weights, resid))
    send = call(
        third_step, shape((WY * WZ, 2 * ROWS + TAIL, LANES), BF16), (ext, rounded)
    )(resid, x2, d2, hf, *x_near, *near, line_inverse, ends)
    recv = lax.all_to_all(send, "wall", 0, 0, tiled=True)
    xf, *edges = call(
        unpack,
        (cells, shape((4, ROWS, LANES), BF16), dense, dense),
        (side, side),
    )(recv, *v_edges)
    x_edges = block_edges(*edges)
    whole = shape(right_side.shape, F32)
    x3, resid, own = call(
        inner_resid,
        (whole, whole, shape((LANES, LANES), F32)),
        (block, pltpu.VMEM((4 * SPAN, LANES), F32), dma((ROWS // 4,))),
        out_specs=(hbm, vmem, vmem),
    )(xf, *face_weights, recv, right_side, *edges[1:])
    residual = call(
        last_resid,
        whole,
        (pltpu.VMEM((2, ROWS, LANES), F32), block, dma((ROWS // 4,))),
        out_specs=hbm,
    )(resid, xf, face_weights[0], own, *x_edges)
    return x3, residual


def solution(mesh):
    in_specs = (P("wall", "span", "stream"), P("wall", "span", "stream"), P("wall"), P())
    out_specs = (P("wall", "span", "stream"), P("wall", "span", "stream"))
    return jax.shard_map(body, mesh=mesh, in_specs=in_specs, out_specs=out_specs, check_vma=False)
```

```python
import functools

import jax
import jax.numpy as jnp
from jax import lax
from jax.experimental import pallas as pl
from jax.experimental.pallas import tpu as pltpu
from jax.sharding import PartitionSpec as P

STEPS = 3
NW, WY, WZ = 1024, 4, 8
ROWS, SPAN, LANES = 32, 64, 128
BS, BX = 16, 16
CELLS = BS * BX
CHUNKS = NW // 128
LP, FIRST, BUSY, ROW_COUNT = BX + 2, 24, 288, 336
RUN = 48
CP = SPAN + 3
BLOCK_ROWS = 2280
TAIL = 8
MID = 0.5
F32, BF16 = jnp.float32, jnp.bfloat16
MIB = 1024 * 1024


def chebyshev_weights(steps):
    lowest = 0.25
    highest = 2.5
    center = 0.5 * (highest + lowest)
    half = 0.5 * (highest - lowest)
    ratio = center / half
    weights = [(0.0, 1.0 / center)]
    rho_old = 1.0 / ratio
    for step in range(1, steps):
        rho_new = 1.0 / (2.0 * ratio - rho_old)
        weights.append((rho_new * rho_old, 2.0 * rho_new / half))
        rho_old = rho_new
    return weights


WEIGHTS = chebyshev_weights(STEPS)


def shape(dims, dtype):
    return jax.ShapeDtypeStruct(dims, dtype)


def call(kernel, outs, scratch=(), limit=40 * MIB, **specs):
    return pl.pallas_call(
        kernel,
        out_shape=outs,
        scratch_shapes=list(scratch),
        compiler_params=pltpu.CompilerParams(vmem_limit_bytes=limit),
        cost_estimate=pl.CostEstimate(flops=10**7, bytes_accessed=4 * 10**6, transcendentals=0),
        **specs,
    )


def skew(arrays):
    block = lax.broadcasted_iota(jnp.int32, arrays[0].shape, 1) // BX
    arrays = list(arrays)
    for bit in range(3):
        step = 1 << bit
        upper = (block // step) % 2 == 1
        arrays = [jnp.where(upper, arrays[(j + step) % 8], arrays[j]) for j in range(8)]
    return [arrays[-z % 8] for z in range(8)]


def to_blocks(rows):
    return skew([pltpu.roll(row, BX * i, 1) if i else row for i, row in enumerate(rows)])


def from_blocks(blocks):
    return [pltpu.roll(row, LANES - BX * i, 1) if i else row for i, row in enumerate(skew(blocks))]


def turned(p):
    z, odd = lax.axis_index("wall") % WZ, lax.axis_index("stream") % 2
    return (p - (z + odd * (WZ - 1 - 2 * z)) + WZ) % WZ


def owner(t, z):
    span, odd = lax.axis_index("span"), lax.axis_index("stream") % 2
    return WZ * (t + span * (WY - 1 - 2 * t)) + z + odd * (WZ - 1 - 2 * z)


def strided(s):
    return pl.ds(s, ROWS, stride=SPAN)


def edge_lanes(blocks, pick, turn, offset):
    at = lax.broadcasted_iota(jnp.int32, (LANES, LANES), 0)
    to = lax.broadcasted_iota(jnp.int32, (LANES, LANES), 1)
    one = jnp.where((at % BX == pick) & (to == (at // BX + turn) % 8), 1.0, 0.0).astype(BF16)
    eights = jnp.dot(blocks.reshape(8 * ROWS, LANES), one, preferred_element_type=F32)
    out = jnp.zeros((ROWS, LANES), F32)
    for q in range(8):
        out += pltpu.roll(eights[ROWS * q : ROWS * (q + 1)], (8 * q + offset) % LANES, 1)
    return out.astype(BF16)


def pack(
    b_hbm, v_hbm, m_hbm, send_hbm, es_hbm, dl_hbm, dr_hbm, b_buf, v_buf, m_buf, send, es, dl, dr, cl, cr,
    sems, done, small,
):
    def copy(k, t):
        src, dst = ((v_hbm, v_buf), (b_hbm, b_buf))[k]
        rows = pl.ds(BS * t, BS)
        return pltpu.make_async_copy(src.at[:, rows, :], dst.at[:, rows, :], sems.at[k, t])

    def result(k, y):
        part = (pl.ds(WZ * y, WZ), slice(2 * ROWS, None) if k else slice(0, 2 * ROWS))
        return pltpu.make_async_copy(send.at[part], send_hbm.at[part], done.at[k, y])

    for k in range(2):
        for t in range(WY):
            copy(k, t).start()
    metric = pltpu.make_async_copy(m_hbm, m_buf, small.at[3])
    metric.start()
    edges = [
        pltpu.make_async_copy(src, dst, small.at[n])
        for n, (src, dst) in enumerate(((es, es_hbm), (dl, dl_hbm), (dr, dr_hbm)))
    ]

    def move(t, k, buf, mid):
        for g in range(2):
            parts = [buf[strided(16 * t + 8 * g + i), :] - mid for i in range(8)]
            parts = to_blocks([part.astype(BF16) for part in parts])
            rows = slice(ROWS * (2 * k + g), ROWS * (2 * k + g + 1))
            for z in range(WZ):
                send[owner(t, z), rows, :] = parts[z]
            if k:
                cl[2 * t + g] = parts[0]
                cr[2 * t + g] = parts[7]
        return 0

    v_flat, b_flat = (buf.reshape(ROWS * SPAN, LANES) for buf in (v_buf, b_buf))

    def first(t, _):
        copy(0, t).wait()
        move(t, 1, v_flat, MID)
        return 0

    lax.fori_loop(0, WY, first, 0, unroll=4)
    metric.wait()
    rest = m_buf[...]
    parts = []
    for _ in range(3):
        part = rest.astype(BF16)
        rest = rest - part.astype(F32)
        parts.append(part.astype(F32))
    tail = jnp.concatenate(parts + [jnp.zeros((TAIL - 3, ROWS), F32)], axis=0)
    tail = jnp.concatenate([tail, jnp.zeros((TAIL, LANES - ROWS), F32)], axis=1).astype(BF16)
    for k in range(WY * WZ):
        send[k, 4 * ROWS :, :] = tail
    for t in range(WY):
        result(1, t).start()

    def last(t, _):
        copy(1, t).wait()
        move(t, 0, b_flat, 0.0)
        result(0, owner(t, 0) // WZ).start()
        return 0

    lax.fori_loop(0, WY, last, 0, unroll=4)
    es[0] = (v_flat[strided(0), :] - MID).astype(BF16)
    es[1] = (v_flat[strided(SPAN - 1), :] - MID).astype(BF16)
    dl[...] = edge_lanes(cl[...], 0, 0, SPAN)
    dr[...] = edge_lanes(cr[...], BX - 1, 1, SPAN)
    for edge in edges:
        edge.start()
    for k in range(2):
        for t in range(WY):
            result(k, t).wait()
    for edge in edges:
        edge.wait()


def to_lines(recv, bf, hf, metric, *edges):
    for i in range(8):
        row = jnp.zeros((TAIL, LANES), F32)
        for j in range(4):
            row += pltpu.roll(recv[4 * i + j, 4 * ROWS :, :].astype(F32), ROWS * j, 1)
        metric[:, i * LANES : (i + 1) * LANES] = jnp.sum(row, axis=0, keepdims=True)
    for k, ref in enumerate((bf, hf)):
        for i in range(CHUNKS):
            for g in range(2):
                tile = recv[4 * i : 4 * i + 4, ROWS * (2 * k + g) : ROWS * (2 * k + g + 1), :]
                tile = tile.astype(F32).reshape(LANES, LANES).T
                if k:
                    tile = 0.5 * tile + 0.5 * MID
                for p in range(8):
                    ref[line_rows(i, 8 * g + turned(p)), :] = tile[BX * p : BX * (p + 1)]
    for i in range(CHUNKS):
        lanes = slice(i * LANES, (i + 1) * LANES)
        for n, rows in enumerate(edge_rows(i)):
            edges[n][:BX, lanes] = bf[rows, :].astype(BF16)
            edges[n][BX:, lanes] = (2.0 * hf[rows, :] - MID).astype(BF16)
    mirror(hf)


def line_rows(i, s):
    return pl.ds(ROW_COUNT * i + FIRST + LP * s, BX)


def edge_rows(i):
    base = ROW_COUNT * i + FIRST
    return (
        line_rows(i, 0),
        line_rows(i, BS - 1),
        pl.ds(base, BS, stride=LP),
        pl.ds(base + BX - 1, BS, stride=LP),
    )


def near_rows(i):
    base = ROW_COUNT * i + FIRST
    return (
        line_rows(i, -1),
        line_rows(i, BS),
        pl.ds(base - 1, BS, stride=LP),
        pl.ds(base + BX, BS, stride=LP),
    )


def mirror(field):
    for i in range(CHUNKS):
        for near, edge in zip(near_rows(i), edge_rows(i)):
            field[near, :] = field[edge, :]


def busy(i):
    return pl.ds(ROW_COUNT * i + FIRST, BUSY)


def apply_lines(rows, line):
    return lax.dot_general(rows, line, (((1,), (1,)), ((), ())), preferred_element_type=F32)


def first_lines(bf, hf, metric, line, x1, fw, resid, rounded):
    for i in range(CHUNKS):
        rounded[:, i * LANES : (i + 1) * LANES] = bf[busy(i), :].astype(BF16)
    y = WEIGHTS[0][1] * apply_lines(rounded[...], line[...])
    for i in range(CHUNKS):
        x1[busy(i), :] = y[:, i * LANES : (i + 1) * LANES]
    mirror(x1)
    line_resid(bf, x1, hf, fw, metric, resid, make_weights=True)


def line_resid(bf, xe, he, fw, metric, out, make_weights=False):
    lane = lax.broadcasted_iota(jnp.int32, (RUN, LANES), 1)
    last, first = lane == LANES - 1, lane == 0

    def one(c, _):
        def load(ref, i, shift=0):
            return ref[pl.ds(ROW_COUNT * i + FIRST + shift + RUN * c, RUN), :]

        xc = load(xe, 0)
        moved_x = pltpu.roll(xc, LANES - 1, 1)
        kappa = load(he, 0) * metric[:, :LANES]
        entry = kappa * -xc
        moved_k = pltpu.roll(kappa, LANES - 1, 1)
        for i in range(CHUNKS):
            if i + 1 < CHUNKS:
                after = load(xe, i + 1)
                moved_after = pltpu.roll(after, LANES - 1, 1)
                kappa_after = load(he, i + 1) * metric[:, (i + 1) * LANES : (i + 2) * LANES]
                moved_k_after = pltpu.roll(kappa_after, LANES - 1, 1)
            else:
                after = moved_after = jnp.zeros((RUN, LANES), F32)
                kappa_after = moved_k_after = after
            if make_weights:
                weight = kappa + jnp.where(last, moved_k_after, moved_k)
                fw[pl.ds(ROW_COUNT * i + FIRST + RUN * c, RUN), :] = weight
            else:
                weight = load(fw, i)
            above = weight * (xc - jnp.where(last, moved_after, moved_x))
            below = pltpu.roll(above, 1, 1)
            hc = load(he, i)
            total = above - jnp.where(first, entry, below)
            for shift in (-LP, -1, 1, LP):
                total += (hc + load(he, i, shift)) * (xc - load(xe, i, shift))
            out[pl.ds(ROW_COUNT * i + FIRST + RUN * c, RUN), :] = load(bf, i) - (xc + total)
            xc, moved_x, entry = after, moved_after, below
            kappa, moved_k = kappa_after, moved_k_after
        return 0

    lax.fori_loop(0, BUSY // RUN, one, 0)


def finish_resid(resid, x, hf, near, x_near, out, rounded):
    for i in range(CHUNKS):
        lanes = slice(i * LANES, (i + 1) * LANES)
        out[busy(i), :] = resid[busy(i), :]
        for k, rows in enumerate(edge_rows(i)):
            weight = hf[rows, :] + 0.5 * near[k][BX:, lanes].astype(F32) + 0.5 * MID
            out[rows, :] = out[rows, :] - weight * (x[rows, :] - x_near(k, i))
        rounded[:, lanes] = out[busy(i), :].astype(BF16)


def second_step(resid, x1, hf, su, sd, xl, xr, line, x2, d2, e0, e1, e2, e3, full, rt, ends):
    near = (su, sd, xl, xr)
    for k, ref in enumerate(near):
        ends[k * BX : (k + 1) * BX] = ref[0:BX]
    ends1 = WEIGHTS[0][1] * apply_lines(ends[...], line[...])

    def x_near(k, i):
        return ends1[k * BX : (k + 1) * BX, i * LANES : (i + 1) * LANES]

    finish_resid(resid, x1, hf, near, x_near, full, rt)
    keep, scale = WEIGHTS[1]
    y = scale * apply_lines(rt[...], line[...])
    for i in range(CHUNKS):
        lanes = slice(i * LANES, (i + 1) * LANES)
        x = x1[busy(i), :]
        d = keep * x + y[:, lanes]
        d2[busy(i), :] = d
        x2[busy(i), :] = x + d
        for rows, ref in zip(edge_rows(i), (e0, e1, e2, e3)):
            ref[:, lanes] = x2[rows, :].astype(BF16)
    mirror(x2)


def third_step(
    resid, x2, d2, hf, su, sd, xl, xr, vsu, vsd, vxl, vxr, line, ends, send, xe, rt
):
    x_edges = (su, sd, xl, xr)

    def x_near(k, i):
        return x_edges[k][:, i * LANES : (i + 1) * LANES].astype(F32)

    finish_resid(resid, x2, hf, (vsu, vsd, vxl, vxr), x_near, xe, rt)
    keep, scale = WEIGHTS[2]
    y = scale * apply_lines(rt[...], line[...])
    count = WY * WZ
    nothing = jnp.zeros((1, LANES), F32)
    firsts, lasts = {}, {}
    for i in range(CHUNKS):
        xe[busy(i), :] = x2[busy(i), :] + keep * d2[busy(i), :] + y[:, i * LANES : (i + 1) * LANES]
        for j in range(2):
            tile = jnp.concatenate([xe[line_rows(i, 8 * j + turned(p)), :] for p in range(8)], axis=0).T
            for k in range(4):
                part = tile[ROWS * k : ROWS * (k + 1)]
                send[4 * i + k, ROWS * j : ROWS * (j + 1), :] = part.astype(BF16)
                firsts[4 * i + k, j] = part[:1]
                lasts[4 * i + k, j] = part[ROWS - 1 :]
    for k in range(count):
        rows = []
        for j in range(2):
            rows += [lasts.get((k - 1, j), nothing), firsts.get((k + 1, j), nothing)]
            rows.append(ends[k, 2 * j : 2 * j + 2, :])
        send[k, 2 * ROWS :, :] = jnp.concatenate(rows, axis=0).astype(BF16)


def block_row(w, s=0):
    return CP * (w + 1) + 1 + s


def block_span(s):
    return pl.ds(block_row(0, s), ROWS, stride=CP)


def unpack(recv, ves, vdl, vdr, xf, es, dl, dr, cl, cr):
    def one(t, _):
        for g in range(2):
            rows = slice(ROWS * g, ROWS * (g + 1))
            parts = [recv[owner(t, z), rows, :] for z in range(WZ)]
            cl[2 * t + g] = parts[0]
            cr[2 * t + g] = parts[7]
            parts = from_blocks(parts)
            for i in range(8):
                s = 16 * t + 8 * g + i
                xf[pl.ds(block_row(0) + s, ROWS, stride=CP), :] = parts[i].astype(F32)
        return 0

    lax.fori_loop(0, WY, one, 0, unroll=4)
    for k, (s, beside) in enumerate(((0, -1), (SPAN - 1, SPAN))):
        edge = xf[block_span(s), :]
        xf[block_span(beside), :] = edge
        es[k] = edge.astype(BF16)
    for w, beside in ((0, -1), (ROWS - 1, ROWS)):
        xf[pl.ds(block_row(beside), SPAN), :] = xf[pl.ds(block_row(w), SPAN), :]
    es[2] = ves[0]
    es[3] = ves[1]
    dl[...] = edge_lanes(cl[...], 0, 0, 0) + vdl[...]
    dr[...] = edge_lanes(cr[...], BX - 1, 1, 0) + vdr[...]


def weights(v_ref, m_ref, recv, metric, hf, gx, gk, ends):
    def four(n, below):
        for k in range(4):
            w = 4 * n + k
            half = 0.5 * v_ref[w]
            hf[pl.ds(block_row(w), SPAN), :] = half
            cells = pl.ds(pl.multiple_of(SPAN * w, SPAN), SPAN)
            gx[cells, :] = half + pltpu.roll(half, LANES - 1, 1)
            half = m_ref[w] * half
            gk[cells, :] = below + half
            below = half
        return below

    start = jnp.zeros((SPAN, LANES), F32)
    gk[SPAN * ROWS :, :] = lax.fori_loop(0, ROWS // 4, four, start, unroll=2)
    for s in (-1, SPAN):
        hf[block_span(s), :] = jnp.zeros((ROWS, LANES), F32)
    count = WY * WZ
    nothing = jnp.zeros((1, LANES), F32)
    for k in range(count):
        rows = []
        for g in range(2):
            for other, at in ((k - 1, ROWS - 1), (k + 1, 0)):
                if not 0 <= other < count:
                    rows.append(nothing)
                    continue
                v = recv[other, ROWS * (2 + g) : ROWS * (3 + g), :].astype(F32) + MID
                rows.append(v[at : at + 1] * metric[:, ROWS * other + at : ROWS * other + at + 1])
        ends[k] = jnp.concatenate(rows, axis=0)


def placed(right, left):
    at = lax.broadcasted_iota(jnp.int32, (2 * ROWS, LANES), 0)
    to = lax.broadcasted_iota(jnp.int32, (2 * ROWS, LANES), 1)
    place = jnp.where(to == 2 * (at % ROWS) + at // ROWS, 1.0, 0.0).astype(BF16)
    both = jnp.concatenate([right[...], left[...]], axis=0)
    return lax.dot_general(both, place, (((0,), (0,)), ((), ())), preferred_element_type=F32)


def inner_resid(xf, hf, gx, gk, recv, b_ref, dl, dr, x3, resid, own, x_buf, beyond, sems):
    lane = lax.broadcasted_iota(jnp.int32, (ROWS, LANES), 1)
    halves = (0, ROWS)

    def load(ref, w, s):
        return ref[pl.ds(block_row(w, s), ROWS), :]

    def result(n):
        rows = pl.ds(4 * n, 4)
        return pltpu.make_async_copy(x_buf.at[rows], x3.at[rows], sems.at[n])

    def four(q, carry):
        carry = list(carry)
        for n in range(4):
            w = 4 * q + n
            for h, s in enumerate(halves):
                xc, hc = load(xf, w, s), load(hf, w, s)
                x_buf[w, s : s + ROWS, :] = xc
                above = gk[pl.ds(SPAN * (w + 1) + s, ROWS), :] * (xc - load(xf, w + 1, s))
                total = above - carry[h]
                carry[h] = above
                for d in (-1, 1):
                    total += (hc + load(hf, w, s + d)) * (xc - load(xf, w, s + d))
                right = gx[pl.ds(SPAN * w + s, ROWS), :] * (xc - pltpu.roll(xc, LANES - 1, 1))
                right = jnp.where(lane == LANES - 1, 0.0, right)
                total += right - pltpu.roll(right, 1, 1)
                resid[w, s : s + ROWS, :] = b_ref[w, s : s + ROWS, :] - (xc + total)
        result(q).start()
        return tuple(carry)

    zero = jnp.zeros((ROWS, LANES), F32)
    lax.fori_loop(0, ROWS // 4, four, (zero, zero), unroll=2)

    def tail(t, _):
        parts = from_blocks([recv[owner(t, z), 2 * ROWS :, :].astype(F32) for z in range(WZ)])
        for g in range(2):
            for i in range(8):
                for k in range(4):
                    row = pl.ds(SPAN * k + 16 * t + 8 * g + i, 1)
                    beyond[row, :] = parts[i][4 * g + k : 4 * g + k + 1]
        return 0

    lax.fori_loop(0, WY, tail, 0)
    for k, w in enumerate((0, ROWS - 1)):
        face = gk[SPAN * ROWS * k : SPAN * (ROWS * k + 1), :]
        weight = face + 0.5 * beyond[SPAN * (2 + k) : SPAN * (3 + k), :]
        x = xf[pl.ds(block_row(w), SPAN), :]
        resid[w] = resid[w] - weight * (x - beyond[SPAN * k : SPAN * (k + 1), :])
    own[...] = placed(dr, dl)
    for q in range(ROWS // 4):
        result(q).wait()


def last_resid(resid, xf, hf, own, spans, lefts, rights, out, side_rows, r_buf, sems):
    for k, s in enumerate((0, SPAN - 1)):
        weight = hf[block_span(s), :] + 0.5 * spans[3 - k].astype(F32) + 0.5 * MID
        side_rows[k] = weight * (xf[block_span(s), :] - spans[1 - k].astype(F32))
    near = placed(rights, lefts)
    sides = (0.5 * (own[SPAN:] + near[SPAN:]) + MID) * (own[:SPAN] - near[:SPAN])
    lane = lax.broadcasted_iota(jnp.int32, (SPAN, LANES), 1)
    ends = (lane == 0) | (lane == LANES - 1)
    row = lax.broadcasted_iota(jnp.int32, (8, LANES), 0)

    def results(q):
        rows = pl.ds(4 * q, 4)
        return pltpu.make_async_copy(r_buf.at[rows], out.at[rows], sems.at[q])

    def four(q, carry):
        for n in range(4):
            w = 4 * q + n
            r = resid[w] - jnp.where(ends, pltpu.roll(sides, LANES - 1 - 2 * w, 1), 0.0)
            r_buf[w, 8 : SPAN - 8, :] = r[8 : SPAN - 8]
            for k, s in enumerate((0, SPAN - 8)):
                flux = side_rows[k, pl.ds(w, 1), :]
                r_buf[w, s : s + 8, :] = r[s : s + 8] - jnp.where(row == 7 * k, flux, 0.0)
        results(q).start()
        return carry

    lax.fori_loop(0, ROWS // 4, four, 0, unroll=4)
    for q in range(ROWS // 4):
        results(q).wait()


def block_edges(es, dl, dr):
    streams = lax.axis_size("stream")
    right = [(i, (i + 1) % streams) for i in range(streams)]
    left = [((i + 1) % streams, i) for i in range(streams)]
    return (
        lax.ppermute(es, "span", [(0, 1), (1, 0)]),
        lax.ppermute(dr, "stream", right),
        lax.ppermute(dl, "stream", left),
    )


def line_shift(value, ds, dx):
    spans, streams = lax.axis_size("span"), lax.axis_size("stream")

    def device(sb, xb):
        sp, y = divmod(sb % (spans * WY), WY)
        st, z = divmod(xb % (streams * WZ), WZ)
        y, z = (WY - 1 - y if sp % 2 else y), (WZ - 1 - z if st % 2 else z)
        return ((y * WZ + z) * spans + sp) * streams + st

    pairs = [
        (device(sb, xb), device(sb + ds, xb + dx))
        for sb in range(spans * WY)
        for xb in range(streams * WZ)
    ]
    return lax.ppermute(value, ("wall", "span", "stream"), pairs)


def line_edges(*edges):
    return (
        line_shift(edges[1], 1, 0),
        line_shift(edges[0], -1, 0),
        line_shift(edges[3], 0, 1),
        line_shift(edges[2], 0, -1),
    )


def body(right_side, viscosity, wall_metric, line_inverse):
    block = pltpu.VMEM((ROWS, SPAN, LANES), F32)
    side = pltpu.VMEM((8, ROWS, LANES), BF16)
    dense = shape((ROWS, LANES), BF16)
    hbm, vmem = pl.BlockSpec(memory_space=pltpu.HBM), pl.BlockSpec(memory_space=pltpu.VMEM)
    sent = (WY * WZ, 4 * ROWS + TAIL, LANES)
    dma = pltpu.SemaphoreType.DMA
    send, *v_edges = call(
        pack,
        (shape(sent, BF16), shape((2, ROWS, LANES), BF16), dense, dense),
        (
            block,
            block,
            pltpu.VMEM((1, ROWS), F32),
            pltpu.VMEM(sent, BF16),
            pltpu.VMEM((2, ROWS, LANES), BF16),
            pltpu.VMEM((ROWS, LANES), BF16),
            pltpu.VMEM((ROWS, LANES), BF16),
            side,
            side,
            dma((2, WY)),
            dma((2, WY)),
            dma((4,)),
        ),
        62 * MIB + MIB // 2,
        in_specs=(hbm,) * 3,
        out_specs=(hbm,) * 4,
    )(right_side, viscosity, wall_metric.reshape(1, ROWS))
    recv = lax.all_to_all(send, "wall", 0, 0, tiled=True)
    field = shape((CHUNKS * ROW_COUNT, LANES), F32)
    bf, hf, metric, *edges = call(
        to_lines,
        (field, field, shape((1, NW), F32))
        + (shape((2 * BX, NW), BF16),) * 4,
    )(recv)
    near = line_edges(*edges)
    ext = pltpu.VMEM((CHUNKS * ROW_COUNT, LANES), F32)
    rounded = pltpu.VMEM((BUSY, NW), BF16)
    x1, fw, resid = call(first_lines, (field, field, field), (rounded,))(
        bf, hf, metric, line_inverse
    )
    x2, d2, *edges = call(
        second_step,
        (field, field) + (shape((BX, NW), BF16),) * 4,
        (ext, rounded, pltpu.VMEM((4 * BX, NW), BF16)),
    )(resid, x1, hf, *near, line_inverse)
    x_near = line_edges(*edges)
    resid = call(line_resid, field)(bf, x2, hf, fw, metric)
    v, m, _ = lax.optimization_barrier((viscosity, wall_metric, d2))
    smem = pl.BlockSpec(memory_space=pltpu.SMEM)
    cells = shape((BLOCK_ROWS, LANES), F32)
    *face_weights, ends = call(
        weights,
        (
            cells,
            shape((ROWS * SPAN, LANES), F32),
            shape(((ROWS + 1) * SPAN, LANES), F32),
            shape((WY * WZ, 4, LANES), F32),
        ),
        in_specs=(vmem, smem, vmem, vmem),
    )(v, m, recv, metric)
    face_weights, resid = lax.optimization_barrier((face_weights, resid))
    send = call(
        third_step, shape((WY * WZ, 2 * ROWS + TAIL, LANES), BF16), (ext, rounded)
    )(resid, x2, d2, hf, *x_near, *near, line_inverse, ends)
    recv = lax.all_to_all(send, "wall", 0, 0, tiled=True)
    xf, *edges = call(
        unpack,
        (cells, shape((4, ROWS, LANES), BF16), dense, dense),
        (side, side),
    )(recv, *v_edges)
    x_edges = block_edges(*edges)
    whole = shape(right_side.shape, F32)
    x3, resid, own = call(
        inner_resid,
        (whole, whole, shape((LANES, LANES), F32)),
        (block, pltpu.VMEM((4 * SPAN, LANES), F32), dma((ROWS // 4,))),
        out_specs=(hbm, vmem, vmem),
    )(xf, *face_weights, recv, right_side, *edges[1:])
    residual = call(
        last_resid,
        whole,
        (pltpu.VMEM((2, ROWS, LANES), F32), block, dma((ROWS // 4,))),
        out_specs=hbm,
    )(resid, xf, face_weights[0], own, *x_edges)
    return x3, residual


def solution(mesh):
    in_specs = (P("wall", "span", "stream"), P("wall", "span", "stream"), P("wall"), P())
    out_specs = (P("wall", "span", "stream"), P("wall", "span", "stream"))
    return jax.shard_map(body, mesh=mesh, in_specs=in_specs, out_specs=out_specs, check_vma=False)
```
